32 devices in a mesh: dp: 16 (over z, y, core), mp: 2 (over x).
Axes of the slice: x: 2, y: 2, z: 4, core: 2. Of those that a mesh axis runs over, the one named last changes fastest.
Arguments:
- patches: bfloat16 [16, 1568, 768], P('dp', 'mp'), may hold values from -6 to 6
- cube_mask: int32 [16, 1568], P('dp', 'mp'), may hold values from 0 to 1, as said below
- mask_token: float32 [768], replicated, may hold values from -5 to 5
- cotangent: bfloat16 [16, 1568, 768], P('dp', 'mp'), may hold values from -6 to 6
- vectors: float32 [12, 768], replicated
- vector_first: float32 [12, 768], replicated
- vector_second: float32 [12, 768], replicated, as said below
- attend_master: float32 [768, 3, 768], P('dp', None, 'mp')
- attend_first: float32 [768, 3, 768], P('dp', None, 'mp')
- attend_second: float32 [768, 3, 768], P('dp', None, 'mp'), as said below
- mixing_master: float32 [768, 768], P('dp', 'mp')
- mixing_first: float32 [768, 768], P('dp', 'mp')
- mixing_second: float32 [768, 768], P('dp', 'mp'), as said below
- expand_master: float32 [768, 3072], P('dp', 'mp')
- expand_first: float32 [768, 3072], P('dp', 'mp')
- expand_second: float32 [768, 3072], P('dp', 'mp'), as said below
- shrink_master: float32 [768, 3072], P('dp', 'mp')
- shrink_first: float32 [768, 3072], P('dp', 'mp')
- shrink_second: float32 [768, 3072], P('dp', 'mp'), as said below
Outputs:
- block_out: bfloat16 [16, 1568, 768], P('dp', 'mp')
- patch_grad: bfloat16 [16, 1568, 768], P('dp', 'mp')
- token_grad: float32 [768], replicated
- bias_grad: float32 [768], replicated
- attend_moment: float32 [768, 3, 768], P('dp', None, 'mp')
- attend_square: float32 [768, 3, 768], P('dp', None, 'mp')
- attend_weight: float32 [768, 3, 768], P('dp', None, 'mp')
- attend_copy: bfloat16 [768, 3, 768], P('dp', None, 'mp')
- mixing_moment: float32 [768, 768], P('dp', 'mp')
- mixing_square: float32 [768, 768], P('dp', 'mp')
- mixing_weight: float32 [768, 768], P('dp', 'mp')
- mixing_copy: bfloat16 [768, 768], P('dp', 'mp')
- expand_moment: float32 [768, 3072], P('dp', 'mp')
- expand_square: float32 [768, 3072], P('dp', 'mp')
- expand_weight: float32 [768, 3072], P('dp', 'mp')
- expand_copy: bfloat16 [768, 3072], P('dp', 'mp')
- shrink_moment: float32 [768, 3072], P('dp', 'mp')
- shrink_square: float32 [768, 3072], P('dp', 'mp')
- shrink_weight: float32 [768, 3072], P('dp', 'mp')
- shrink_copy: bfloat16 [768, 3072], P('dp', 'mp')
- vector_moment: float32 [12, 768], replicated
- vector_square: float32 [12, 768], replicated
- vector_weight: float32 [12, 768], replicated
- trust_norms: float32 [4, 2], replicated
The draws below stay inside these ranges and needn't reach their ends.
Inputs may be any that keep to these rules, and one draw needn't show every extreme that they name: `cube_mask`: 1 marks a masked tube; masked tubes come in whole cubes of 2 x 2 x 2 tubes of a clip's 8 x 14 x 14 grid, tubes ordered by time, height, width. `attend_second`: positive. `mixing_second`: positive. `expand_second`: positive. `shrink_second`: positive. `vector_second`: positive.
All inputs are finite; a program needn't handle non-finite values.
Results may differ from the reference program's by a relative error of at most 0.018.
The reference program's roundings to bfloat16 on the way count: a program that leaves them out, or rounds other values in their place, can miss the bound.
Values may be sent and summed in bfloat16 or wider, within the bound.
A program may use at most 128 MiB of HBM per device.

```python
import math
import jax
import jax.numpy as jnp
from jax import lax

D = 768
H = 12
HD = 64
FF = 3072
LT = 8
GRID = 14
LEN = 1568
CLIPS = 16
TOKENS = 25088
STEP = 5


def rising(number, factor):
    fraction = jnp.arange(number, dtype=jnp.float32) / max(number - 1, 1)
    return jnp.exp((fraction - 0.5) * math.log(factor))


def flatten(factor):
    return math.sqrt((factor ** 2 - factor ** (-2)) / (4.0 * math.log(factor)))


def col_rise(number, repeats, factor):
    return jnp.tile(rising(number, factor), repeats)


def moment_values(random, grad_size, number, columns, repeats, factor):
    return random * grad_size * rising(number, factor)[:, None] * col_rise(columns, repeats, factor)[None, :]


def square_values(spread, grad_size, number, columns, repeats, factor):
    scale = grad_size * rising(number, math.sqrt(factor))[:, None] * col_rise(columns, repeats, math.sqrt(factor))[None, :]
    return spread * scale * scale


def vector_levels():
    levels = jnp.array([2.6, 2.6, 1.5, 1.5, 1.2, 0.6, 0.6, 0.3, 0.3, 0.3, 0.3, 1.0], jnp.float32)
    return levels * math.sqrt(TOKENS)


def draw_cube_mask(key, part):
    key = jax.random.fold_in(key, 7)
    block_draw = jax.random.randint(key, (CLIPS, LT // 2, GRID // 2, GRID // 2), 0, 1000)
    clip_index = jnp.arange(CLIPS, dtype=jnp.int32)[:, None, None, None]
    level_base = 200 + 400 * clip_index // max(CLIPS - 1, 1)
    later_half = (jnp.arange(LT // 2, dtype=jnp.int32) >= LT // 4)[None, :, None, None]
    threshold = jnp.where(later_half, level_base * 3 // 2, level_base // 2)
    chosen = (block_draw < threshold).astype(jnp.int32)
    expanded = jnp.repeat(jnp.repeat(jnp.repeat(chosen, 2, axis=1), 2, axis=2), 2, axis=3)
    return expanded.reshape(CLIPS, LEN)


def draw_vectors(key, part):
    key = jax.random.fold_in(key, 17)
    random = jnp.clip(jax.random.normal(key, (12, D), jnp.float32), -5.0, 5.0)
    factor = 3.0
    gains = rising(D, factor)[None, :] * (1.0 + 0.1 * random)
    row_index = jnp.arange(12)[:, None]
    is_gain = (row_index == 0) | (row_index == 5)
    return jnp.where(is_gain, gains, 0.3 * random)


def draw_vector_first(key, part):
    key = jax.random.fold_in(key, 19)
    random = jnp.clip(jax.random.normal(key, (12, D), jnp.float32), -5.0, 5.0)
    return random * vector_levels()[:, None]


def draw_vector_second(key, part):
    key = jax.random.fold_in(key, 23)
    spread = jnp.exp(jax.random.uniform(key, (12, D), jnp.float32, 0.0, math.log(4.0)))
    levels = vector_levels()[:, None]
    return spread * levels * levels


def draw_attend_master(key, part):
    key = jax.random.fold_in(key, 29)
    random = jnp.clip(jax.random.normal(key, (D, 3 * D), jnp.float32), -5.0, 5.0)
    factor = 3.0
    row_scale = rising(D, factor) / flatten(factor)
    part_scale = jnp.repeat(jnp.array([1.5, 1.0, 1.0], jnp.float32), D)
    col_scale = col_rise(D, 3, math.sqrt(factor)) * part_scale
    return (random * D ** (-0.5) * row_scale[:, None] * col_scale[None, :]).reshape(D, 3, D)


def draw_attend_first(key, part):
    key = jax.random.fold_in(key, 31)
    random = jnp.clip(jax.random.normal(key, (D, 3 * D), jnp.float32), -5.0, 5.0)
    factor = 3.0
    return moment_values(random, 1.5 * math.sqrt(TOKENS), D, D, 3, factor).reshape(D, 3, D)


def draw_attend_second(key, part):
    key = jax.random.fold_in(key, 37)
    spread = jnp.exp(jax.random.uniform(key, (D, 3 * D), jnp.float32, 0.0, math.log(4.0)))
    factor = 3.0
    return square_values(spread, 1.5 * math.sqrt(TOKENS), D, D, 3, factor).reshape(D, 3, D)


def draw_mixing_master(key, part):
    key = jax.random.fold_in(key, 41)
    random = jnp.clip(jax.random.normal(key, (D, D), jnp.float32), -5.0, 5.0)
    factor = 3.0
    fan_size = max(1, 8 * D // LEN)
    return random * fan_size ** (-0.5) * rising(D, factor)[:, None] * rising(D, math.sqrt(factor))[None, :]


def draw_mixing_first(key, part):
    key = jax.random.fold_in(key, 43)
    random = jnp.clip(jax.random.normal(key, (D, D), jnp.float32), -5.0, 5.0)
    factor = 3.0
    return moment_values(random, 3.8 * math.sqrt(TOKENS / LEN), D, D, 1, factor)


def draw_mixing_second(key, part):
    key = jax.random.fold_in(key, 47)
    spread = jnp.exp(jax.random.uniform(key, (D, D), jnp.float32, 0.0, math.log(4.0)))
    factor = 3.0
    return square_values(spread, 3.8 * math.sqrt(TOKENS / LEN), D, D, 1, factor)


def draw_expand_master(key, part):
    key = jax.random.fold_in(key, 53)
    random = jnp.clip(jax.random.normal(key, (D, FF), jnp.float32), -5.0, 5.0)
    factor = 3.0
    row_scale = rising(D, factor) / flatten(factor)
    return random * D ** (-0.5) * row_scale[:, None] * rising(FF, math.sqrt(factor))[None, :]


def draw_expand_first(key, part):
    key = jax.random.fold_in(key, 59)
    random = jnp.clip(jax.random.normal(key, (D, FF), jnp.float32), -5.0, 5.0)
    factor = 3.0
    return moment_values(random, 0.3 * math.sqrt(TOKENS), D, FF, 1, factor)


def draw_expand_second(key, part):
    key = jax.random.fold_in(key, 61)
    spread = jnp.exp(jax.random.uniform(key, (D, FF), jnp.float32, 0.0, math.log(4.0)))
    factor = 3.0
    return square_values(spread, 0.3 * math.sqrt(TOKENS), D, FF, 1, factor)


def draw_shrink_master(key, part):
    key = jax.random.fold_in(key, 67)
    random = jnp.clip(jax.random.normal(key, (D, FF), jnp.float32), -5.0, 5.0)
    factor = 3.0
    return random * FF ** (-0.5) * rising(D, factor)[:, None] * rising(FF, math.sqrt(factor))[None, :]


def draw_shrink_first(key, part):
    key = jax.random.fold_in(key, 71)
    random = jnp.clip(jax.random.normal(key, (D, FF), jnp.float32), -5.0, 5.0)
    factor = 3.0
    return moment_values(random, 0.6 * math.sqrt(TOKENS), D, FF, 1, factor)


def draw_shrink_second(key, part):
    key = jax.random.fold_in(key, 73)
    spread = jnp.exp(jax.random.uniform(key, (D, FF), jnp.float32, 0.0, math.log(4.0)))
    factor = 3.0
    return square_values(spread, 0.6 * math.sqrt(TOKENS), D, FF, 1, factor)


def shard_levels(stream_key, shape, pieces, smallest, top_value):
    level, own = 1.0, jax.random.fold_in(stream_key, 6)
    for dim, parts in pieces:
        draws = jnp.exp(jax.random.uniform(jax.random.fold_in(own, dim), (parts,), jnp.float32, smallest / len(pieces), top_value / len(pieces)))
        level = level * jnp.repeat(draws, shape[dim] // parts).reshape([-1 if axis == dim else 1 for axis in range(len(shape))])
    return level


def centred(rng, extent, width, limit, split=(), held_as=jnp.bfloat16):
    loudness = shard_levels(rng, extent, split, -0.22, 0.18) if split else 1.0
    entries = jax.random.normal(rng, extent, jnp.float32) * width * loudness
    return jnp.minimum(jnp.maximum(entries, -limit), limit).astype(held_as)


def setup_inputs(seed: int = 0) -> dict:
    keys = jax.random.split(jax.random.key(seed), 20)
    patches = centred(keys[0], (CLIPS, LEN, D), 1.0, 6.0, ((0, 16), (1, 2)))
    cube_mask = draw_cube_mask(jax.random.fold_in(keys[19], 71), 0)
    mask_token = centred(keys[2], (D,), 1.0, 5.0, (), jnp.float32)
    cotangent = centred(keys[3], (CLIPS, LEN, D), 1.0, 6.0, ((0, 16), (1, 2)))
    vectors = draw_vectors(jax.random.fold_in(keys[19], 71), 0)
    vector_first = draw_vector_first(jax.random.fold_in(keys[19], 71), 0)
    vector_second = draw_vector_second(jax.random.fold_in(keys[19], 71), 0)
    attend_master = draw_attend_master(jax.random.fold_in(keys[19], 71), 0)
    attend_first = draw_attend_first(jax.random.fold_in(keys[19], 71), 0)
    attend_second = draw_attend_second(jax.random.fold_in(keys[19], 71), 0)
    mixing_master = draw_mixing_master(jax.random.fold_in(keys[19], 71), 0)
    mixing_first = draw_mixing_first(jax.random.fold_in(keys[19], 71), 0)
    mixing_second = draw_mixing_second(jax.random.fold_in(keys[19], 71), 0)
    expand_master = draw_expand_master(jax.random.fold_in(keys[19], 71), 0)
    expand_first = draw_expand_first(jax.random.fold_in(keys[19], 71), 0)
    expand_second = draw_expand_second(jax.random.fold_in(keys[19], 71), 0)
    shrink_master = draw_shrink_master(jax.random.fold_in(keys[19], 71), 0)
    shrink_first = draw_shrink_first(jax.random.fold_in(keys[19], 71), 0)
    shrink_second = draw_shrink_second(jax.random.fold_in(keys[19], 71), 0)
    return dict(patches=patches, cube_mask=cube_mask, mask_token=mask_token, cotangent=cotangent, vectors=vectors, vector_first=vector_first, vector_second=vector_second, attend_master=attend_master, attend_first=attend_first, attend_second=attend_second, mixing_master=mixing_master, mixing_first=mixing_first, mixing_second=mixing_second, expand_master=expand_master, expand_first=expand_first, expand_second=expand_second, shrink_master=shrink_master, shrink_first=shrink_first, shrink_second=shrink_second)


@jax.custom_vjp
def low(v):
    return lax.optimization_barrier(v.astype(jnp.bfloat16)).astype(jnp.float32)

@jax.custom_vjp
def low_back(v):
    return v

def low_keep(v):
    return (low(v), None)

def low_pass(kept, grad):
    return (grad,)

def back_keep(v):
    return (v, None)

def back_low(kept, grad):
    return (low(grad),)
low.defvjp(low_keep, low_pass)
low_back.defvjp(back_keep, back_low)
highest = lax.Precision.HIGHEST

def layer_norm(values, scales, shifts):
    centered = values - lax.optimization_barrier(jnp.mean(values, axis=-1, keepdims=True))
    spread = lax.optimization_barrier(jnp.mean(centered * centered, axis=-1, keepdims=True))
    return centered * lax.rsqrt(spread + 1e-06) * scales + shifts

def attend_clip(triple):
    queries, key_rows, values = triple
    scores = jnp.einsum('qhd,khd->hqk', queries, key_rows, precision=highest) * HD ** (-0.5)
    scores = low_back(scores)
    attention = jax.nn.softmax(scores, axis=-1)
    return jnp.einsum('hqk,khd->qhd', low(attention), values, precision=highest)

def forward(flat_rows, token_row, vectors, attend, mixing, expand, shrink, masked):
    row_count = flat_rows.shape[0]
    residual = jnp.where(masked[:, None] > 0, token_row[None, :], flat_rows)
    normed = low(layer_norm(residual, vectors[0], vectors[1]))
    joined = jnp.dot(normed, low(attend).reshape(D, 3 * D), precision=highest)
    queries = low(low_back(joined[:, :D] + vectors[2]))
    key_rows = low(low_back(joined[:, D:2 * D]))
    values = low(low_back(joined[:, 2 * D:] + vectors[3]))
    layout = (row_count // LEN, LEN, H, HD)
    attended = lax.map(jax.checkpoint(attend_clip), (queries.reshape(layout), key_rows.reshape(layout), values.reshape(layout)))
    mixed = low(low_back(attended.reshape(row_count, D)))
    branch = low_back(jnp.dot(mixed, low(mixing).T, precision=highest) + vectors[4])
    middle = residual + branch
    normed_two = low(layer_norm(middle, vectors[5], vectors[6]))
    hidden = low_back(jnp.dot(normed_two, low(expand), precision=highest) + vectors[7:11].reshape(FF))
    active = low(jax.nn.gelu(hidden, approximate=False))
    return middle + low_back(jnp.dot(active, low(shrink).T, precision=highest) + vectors[11])

def lamb_update(weight, moment, square, gradient):
    moment_new = 0.5 * moment + 0.5 * gradient
    square_new = 0.5 * square + 0.5 * gradient * gradient
    correct = 1.0 - 0.5 ** STEP
    update = moment_new / correct / (jnp.sqrt(square_new / correct) + 1e-06) + 0.01 * weight
    weight_norm = jnp.sqrt(jnp.sum(weight * weight))
    update_norm = jnp.sqrt(jnp.sum(update * update))
    renewed = weight - 0.5 * weight_norm / (update_norm + 1e-06) * update
    return (moment_new, square_new, renewed, renewed.astype(jnp.bfloat16), jnp.stack([weight_norm, update_norm]))

def reference(patches, cube_mask, mask_token, cotangent, vectors, vector_first, vector_second, attend_master, attend_first, attend_second, mixing_master, mixing_first, mixing_second, expand_master, expand_first, expand_second, shrink_master, shrink_first, shrink_second):
    row_count = CLIPS * LEN
    flat_rows = patches.reshape(row_count, D).astype(jnp.float32)
    masked = cube_mask.reshape(row_count)

    def run(flat_in, token_in, vector_in, attend_in, mixing_in, expand_in, shrink_in):
        return forward(flat_in, token_in, vector_in, attend_in, mixing_in, expand_in, shrink_in, masked)
    result, backward = jax.vjp(run, flat_rows, mask_token, vectors, attend_master, mixing_master, expand_master, shrink_master)
    grad_flat, grad_token, grad_vectors, grad_attend, grad_mixing, grad_expand, grad_shrink = backward(cotangent.reshape(row_count, D).astype(jnp.float32))
    block_out = result.astype(jnp.bfloat16).reshape(CLIPS, LEN, D)
    patch_grad = grad_flat.astype(jnp.bfloat16).reshape(CLIPS, LEN, D)
    attend_out = lamb_update(attend_master, attend_first, attend_second, grad_attend)
    mixing_out = lamb_update(mixing_master, mixing_first, mixing_second, grad_mixing)
    expand_out = lamb_update(expand_master, expand_first, expand_second, grad_expand)
    shrink_out = lamb_update(shrink_master, shrink_first, shrink_second, grad_shrink)
    vector_moment = 0.5 * vector_first + 0.5 * grad_vectors
    vector_square = 0.5 * vector_second + 0.5 * grad_vectors * grad_vectors
    correct = 1.0 - 0.5 ** STEP
    update = vector_moment / correct / (jnp.sqrt(vector_square / correct) + 1e-06) + 0.01 * vectors
    row_weight = jnp.sqrt(lax.optimization_barrier(jnp.sum(vectors * vectors, axis=-1, keepdims=True)))
    row_update = jnp.sqrt(lax.optimization_barrier(jnp.sum(update * update, axis=-1, keepdims=True)))
    vector_weight = vectors - 0.5 * row_weight / (row_update + 1e-06) * update
    trust_norms = jnp.stack([attend_out[4], mixing_out[4], expand_out[4], shrink_out[4]])
    bias_grad = grad_vectors[11]
    return (block_out, patch_grad, grad_token, bias_grad, attend_out[0], attend_out[1], attend_out[2], attend_out[3], mixing_out[0], mixing_out[1], mixing_out[2], mixing_out[3], expand_out[0], expand_out[1], expand_out[2], expand_out[3], shrink_out[0], shrink_out[1], shrink_out[2], shrink_out[3], vector_moment, vector_square, vector_weight, trust_norms)
```

```python
import functools

import jax
import jax.numpy as jnp
from jax import lax
from jax.experimental import pallas as pl
from jax.experimental.pallas import tpu as pltpu
from jax.sharding import PartitionSpec as P

HD = 64
PAIR = 2 * HD
STEP = 5
BF = jnp.bfloat16
F32 = jnp.float32
NN = (((1,), (0,)), ((), ()))
NT = (((1,), (1,)), ((), ()))
TN = (((0,), (0,)), ((), ()))
LOG2E = 1.4426950408889634
MESH = pl.DeviceIdType.MESH
VMEM_LIMIT = 60 * 2**20


def dot(a, b, dims=NN):
    return lax.dot_general(a, b, dims, preferred_element_type=F32)


def params(**kw):
    return pltpu.CompilerParams(vmem_limit_bytes=VMEM_LIMIT, **kw)


def anywhere():
    return pl.BlockSpec(memory_space=pl.ANY)


def in_vmem():
    return pl.BlockSpec(memory_space=pltpu.VMEM)


def place():
    dp, x = lax.axis_index("dp"), lax.axis_index("mp")
    return x, dp // 4, lax.rem(dp // 2, 2), lax.rem(dp, 2)


def device(x, z, y, c):
    return ((z * 2 + y) * 2 + c, x)


def neighbours():
    x, z, y, c = place()
    lines = [device(x, lax.rem(z + k, 4), y, c) for k in (1, 2, 3)]
    return lines, device(1 - x, z, y, c), device(x, z, 1 - y, c), device(x, z, y, 1 - c)


def greet():
    lines, over_x, over_y, sibling = neighbours()
    barrier = pltpu.get_barrier_semaphore()
    for other in (*lines, over_x, over_y, sibling):
        pl.semaphore_signal(barrier, inc=1, device_id=other, device_id_type=MESH)
    pl.semaphore_wait(barrier, 6)


def gather_kernel(count, *refs):
    shards, wholes = refs[:count], refs[count : 2 * count]
    own_sem, send_sem, recv_sem = refs[2 * count :]
    x, z, y, c = place()
    lines, over_x, over_y, sibling = neighbours()
    greet()

    def remote(i, slot, src, dst, other):
        return pltpu.make_async_remote_copy(
            src_ref=src,
            dst_ref=dst,
            send_sem=send_sem.at[i, slot],
            recv_sem=recv_sem.at[i, slot],
            device_id=other,
            device_id_type=MESH,
        )

    def own(i):
        return pltpu.make_async_copy(shards[i], wholes[i].at[x, z, y, c], own_sem.at[i])

    def line(i, k):
        return remote(i, k - 1, shards[i], wholes[i].at[x, z, y, c], lines[k - 1])

    def plane(i, slot, other, part):
        view = wholes[i].at[part]
        return remote(i, slot, view, view, other)

    def lane(i, k):
        return (x, slice(None), y, c)

    def step_two(i):
        part = (x, slice(None), y, c)
        return [plane(i, 3, over_x, part), plane(i, 4, over_y, part), plane(i, 7, sibling, part)]

    def step_three(i):
        return [
            plane(i, 5, over_x, (x, pl.ds(0, 2), 1 - y, c)),
            plane(i, 6, over_y, (1 - x, pl.ds(2, 2), y, c)),
            plane(i, 8, sibling, (1 - x, slice(None), y, c)),
            plane(i, 9, sibling, (x, slice(None), 1 - y, c)),
        ]

    def step_four(i):
        return [plane(i, 10, sibling, (1 - x, slice(None), 1 - y, c))]

    started = []

    def start(copies):
        for copy in copies:
            copy.start()
            started.append(copy)

    for i in range(count):
        own(i).start()
        start([line(i, k) for k in (1, 2, 3)])
    for turn in range(count + 2):
        if turn < count:
            i = turn
            own(i).wait()
            for k in (1, 2, 3):
                line(i, k).wait_recv()
            start(step_two(i))
        if 0 <= turn - 1 < count:
            i = turn - 1
            two = step_two(i)
            two[0].wait_recv()
            two[1].wait_recv()
            start(step_three(i))
        if 0 <= turn - 2 < count:
            i = turn - 2
            three = step_three(i)
            three[0].wait_recv()
            three[1].wait_recv()
            start(step_four(i))
    for i in range(count):
        step_two(i)[2].wait_recv()
        step_three(i)[2].wait_recv()
        step_three(i)[3].wait_recv()
        step_four(i)[0].wait_recv()
    for copy in started:
        copy.wait_send()


def gather_all(shards):
    count = len(shards)
    outs = [jax.ShapeDtypeStruct((2, 4, 2, 2, *s.shape), s.dtype) for s in shards]
    wholes = pl.pallas_call(
        functools.partial(gather_kernel, count),
        out_shape=outs,
        in_specs=[anywhere()] * count,
        out_specs=[anywhere()] * count,
        scratch_shapes=[
            pltpu.SemaphoreType.DMA((count,)),
            pltpu.SemaphoreType.DMA((count, 11)),
            pltpu.SemaphoreType.DMA((count, 11)),
        ],
        compiler_params=params(collective_id=0, has_side_effects=True),
        name="gather_weights",
    )(*shards)
    return [w.reshape(2, -1, s.shape[-1]) for w, s in zip(wholes, shards)]


def scatter_kernel(count, *refs):
    grads, totals = refs[:count], refs[count : 2 * count]
    refs = refs[2 * count :]
    mine, sib, diag, side, far = (refs[k * count : (k + 1) * count] for k in range(5))
    own_sem, send_sem, recv_sem = refs[5 * count :]
    x, z, y, c = place()
    lines, over_x, over_y, sibling = neighbours()
    greet()

    def remote(i, slot, src, dst, other):
        return pltpu.make_async_remote_copy(
            src_ref=src,
            dst_ref=dst,
            send_sem=send_sem.at[i, slot],
            recv_sem=recv_sem.at[i, slot],
            device_id=other,
            device_id_type=MESH,
        )

    def add(dst, one, other):
        dst[...] = (one[...].astype(F32) + other[...].astype(F32)).astype(BF)

    def own(i):
        return pltpu.make_async_copy(grads[i].at[:, :, :, c], mine[i], own_sem.at[i])

    def step_one(i):
        return remote(i, 0, grads[i].at[:, :, :, 1 - c], sib[i], sibling)

    def step_two(i):
        return [
            remote(i, 1, mine[i].at[1 - x, pl.ds(0, 2), 1 - y], diag[i].at[0], over_x),
            remote(i, 2, mine[i].at[1 - x, pl.ds(2, 2), 1 - y], diag[i].at[1], over_y),
        ]

    def step_three(i):
        return [
            remote(i, 3, mine[i].at[1 - x, :, y], side[i].at[0], over_x),
            remote(i, 4, mine[i].at[x, :, 1 - y], side[i].at[1], over_y),
        ]

    def step_four(i):
        return [
            remote(i, 4 + k, mine[i].at[x, lax.rem(z + k, 4), y], far[i].at[k - 1], lines[k - 1])
            for k in (1, 2, 3)
        ]

    started = []

    def start(copies):
        for copy in copies:
            copy.start()
            started.append(copy)

    for i in range(count):
        own(i).start()
        start([step_one(i)])
    for turn in range(count + 3):
        if turn < count:
            i = turn
            own(i).wait()
            step_one(i).wait_recv()

            def sweep(n, _, i=i):
                part = (n // 8, lax.rem(n // 2, 4), lax.rem(n, 2))
                add(mine[i].at[part], mine[i].at[part], sib[i].at[part])
                return 0

            lax.fori_loop(0, 16, sweep, 0)
            start(step_two(i))
        if 0 <= turn - 1 < count:
            i = turn - 1
            two = step_two(i)
            for copy in two:
                copy.wait()

            def sweep(n, _, i=i):
                low, high = (x, n, 1 - y), (1 - x, 2 + n, y)
                add(mine[i].at[low], mine[i].at[low], diag[i].at[0, n])
                add(mine[i].at[high], mine[i].at[high], diag[i].at[1, n])
                return 0

            lax.fori_loop(0, 2, sweep, 0)
            start(step_three(i))
        if 0 <= turn - 2 < count:
            i = turn - 2
            three = step_three(i)
            for copy in three:
                copy.wait()

            def sweep(n, _, i=i):
                part = mine[i].at[x, n, y]
                both = side[i][0, n].astype(F32) + side[i][1, n].astype(F32)
                part[...] = (part[...].astype(F32) + both).astype(BF)
                return 0

            lax.fori_loop(0, 4, sweep, 0)
            start(step_four(i))
        if 0 <= turn - 3 < count:
            i = turn - 3
            for copy in step_four(i):
                copy.wait()
            total = mine[i][x, z, y].astype(F32)
            for k in range(3):
                total = total + far[i][k].astype(F32)
            totals[i][...] = total
    for i in range(count):
        step_one(i).wait_send()


def scatter_all(grads, rows):
    count = len(grads)
    widths = [g.shape[-1] for g in grads]
    grads = [g.reshape(2, 4, 2, 2, rows, w) for g, w in zip(grads, widths)]
    return pl.pallas_call(
        functools.partial(scatter_kernel, count),
        out_shape=[jax.ShapeDtypeStruct((rows, w), F32) for w in widths],
        in_specs=[anywhere()] * count,
        out_specs=[in_vmem()] * count,
        scratch_shapes=[pltpu.VMEM((2, 4, 2, rows, w), BF) for w in widths]
        + [pltpu.VMEM((2, 4, 2, rows, w), BF) for w in widths]
        + [pltpu.VMEM((2, 2, rows, w), BF) for w in widths]
        + [pltpu.VMEM((2, 4, rows, w), BF) for w in widths]
        + [pltpu.VMEM((3, rows, w), BF) for w in widths]
        + [
            pltpu.SemaphoreType.DMA((count,)),
            pltpu.SemaphoreType.DMA((count, 8)),
            pltpu.SemaphoreType.DMA((count, 8)),
        ],
        compiler_params=params(collective_id=1, has_side_effects=True),
        name="scatter_grads",
    )(*grads)


def project_kernel(mine_ref, other_ref, w_ref, bias_ref, q_ref, k_ref, v_ref):
    rows = mine_ref.shape[0]
    half = w_ref.shape[2] // 3
    for h in range(2):
        cols = slice(h * half, (h + 1) * half)
        queries = dot(mine_ref[...], w_ref[h, :, :half]) + bias_ref[0:1, cols]
        q_ref[:, cols] = (queries.astype(BF).astype(F32) * HD**-0.5).astype(BF)
        for part, ref in ((0, mine_ref), (1, other_ref)):
            span = slice(part * rows, (part + 1) * rows)
            k_ref[span, cols] = dot(ref[...], w_ref[h, :, half : 2 * half]).astype(BF)
            v_ref[span, cols] = (dot(ref[...], w_ref[h, :, 2 * half :]) + bias_ref[1:2, cols]).astype(BF)


def project(mine, other, weight, bias):
    rows, width = mine.shape
    keys = jax.ShapeDtypeStruct((2 * rows, width), BF)
    return pl.pallas_call(
        project_kernel,
        out_shape=[jax.ShapeDtypeStruct((rows, width), BF), keys, keys],
        in_specs=[in_vmem()] * 4,
        out_specs=[in_vmem()] * 3,
        compiler_params=params(),
        name="project",
    )(mine, other, weight, bias)


def half_lanes():
    lane = lax.broadcasted_iota(jnp.int32, (1, PAIR), 1)
    return lane < HD, lane >= HD


def attend_kernel(q_ref, k_ref, v_ref, o_ref, low_ref, p_ref):
    sides = half_lanes()
    q, k, v = q_ref[...], k_ref[...], v_ref[...]
    outs = []
    for h in range(2):
        s = dot(jnp.where(sides[h], q, jnp.zeros_like(q)), k, NT)
        top = jnp.max(s, axis=-1, keepdims=True)
        e = jnp.exp2(s * LOG2E - top * LOG2E)
        total = jnp.sum(e, axis=-1, keepdims=True)
        p = (e * (1.0 / total)).astype(BF)
        p_ref[h] = p
        outs.append(dot(p, v))
    o = jnp.where(sides[0], outs[0], outs[1])
    o_ref[...] = o
    low_ref[...] = o.astype(BF)


def attend(q, k, v):
    rows, width = q.shape
    keys = k.shape[0]
    pairs = width // PAIR
    of_q = pl.BlockSpec((rows, PAIR), lambda i: (0, i))
    of_k = pl.BlockSpec((keys, PAIR), lambda i: (0, i))
    return pl.pallas_call(
        attend_kernel,
        grid=(pairs,),
        in_specs=[of_q, of_k, of_k],
        out_specs=[of_q, of_q, pl.BlockSpec((2, rows, keys), lambda i: (i, 0, 0))],
        out_shape=[
            jax.ShapeDtypeStruct((rows, width), F32),
            jax.ShapeDtypeStruct((rows, width), BF),
            jax.ShapeDtypeStruct((2 * pairs, rows, keys), BF),
        ],
        compiler_params=params(),
        name="attend",
    )(q, k, v)


def attend_back_kernel(q_ref, k_ref, v_ref, do_ref, o_ref, p_ref, dq_ref, dk_ref, dv_ref):
    sides = half_lanes()
    q, k, v, do = q_ref[...], k_ref[...], v_ref[...], do_ref[...]
    prod = do.astype(F32) * o_ref[...]
    outs, grad_k, grad_v = [], None, None
    for h in range(2):
        do_h = jnp.where(sides[h], do, jnp.zeros_like(do))
        q_h = jnp.where(sides[h], q, jnp.zeros_like(q))
        grad_p = dot(do_h, v, NT)
        row_dot = jnp.sum(jnp.where(sides[h], prod, 0.0), axis=-1, keepdims=True)
        p = p_ref[h]
        ds = (p.astype(F32) * (grad_p - row_dot)).astype(BF)
        outs.append(dot(ds, k))
        more_k, more_v = dot(ds, q_h, TN), dot(p, do_h, TN)
        grad_k = more_k if grad_k is None else grad_k + more_k
        grad_v = more_v if grad_v is None else grad_v + more_v
    dq_ref[...] = (jnp.where(sides[0], outs[0], outs[1]) * HD**-0.5).astype(BF)
    dk_ref[...] = grad_k.astype(BF)
    dv_ref[...] = grad_v.astype(BF)


def attend_back(q, k, v, do, o, p):
    rows, width = q.shape
    keys = k.shape[0]
    pairs = width // PAIR
    of_q = pl.BlockSpec((rows, PAIR), lambda i: (0, i))
    of_k = pl.BlockSpec((keys, PAIR), lambda i: (0, i))
    return pl.pallas_call(
        attend_back_kernel,
        grid=(pairs,),
        in_specs=[of_q, of_k, of_k, of_q, of_q, pl.BlockSpec((2, rows, keys), lambda i: (i, 0, 0))],
        out_specs=[of_q, of_k, of_k],
        out_shape=[
            jax.ShapeDtypeStruct((rows, width), BF),
            jax.ShapeDtypeStruct((keys, width), BF),
            jax.ShapeDtypeStruct((keys, width), BF),
        ],
        compiler_params=params(),
        name="attend_back",
    )(q, k, v, do, o, p)


def normal_parts(h):
    z = jnp.abs(h) * 0.7071067811865476
    t = 1.0 / (1.0 + 0.3275911 * z)
    bell = jnp.exp(-z * z)
    poly = t * (
        0.254829592
        + t * (-0.284496736 + t * (1.421413741 + t * (-1.453152027 + t * 1.061405429)))
    )
    tail = 0.5 * poly * bell
    return jnp.where(h < 0, tail, 1.0 - tail), bell * 0.3989422804014327


def mean_rows(values):
    return jnp.mean(values, axis=-1, keepdims=True)


def middle_kernel(
    x_ref,
    o_ref,
    dy_ref,
    vec_ref,
    bu_ref,
    wm_ref,
    we_ref,
    ws_ref,
    out_ref,
    dx1_ref,
    do_ref,
    gm_ref,
    ge_ref,
    gs_ref,
    gu_ref,
    gv_ref,
    x1_ref,
    a2_ref,
    acc_ref,
    da2_ref,
):
    i = pl.program_id(0)
    half = wm_ref.shape[2]

    @pl.when(i == 0)
    def _():
        x1 = x_ref[...] + vec_ref[4:5]
        for h in range(2):
            x1 = x1 + dot(o_ref[:, h * half : (h + 1) * half], wm_ref[h], NT)
        x1_ref[...] = x1
        centred = x1 - mean_rows(x1)
        scale = lax.rsqrt(mean_rows(centred * centred) + 1e-6)
        a2_ref[...] = (centred * scale * vec_ref[5:6] + vec_ref[6:7]).astype(BF)
        acc_ref[...] = x1 + vec_ref[11:12]
        da2_ref[...] = jnp.zeros_like(da2_ref)

    a2, dy = a2_ref[...], dy_ref[...]
    we, ws = we_ref[0], ws_ref[0]
    hidden = dot(a2, we) + bu_ref[...]
    cdf, density = normal_parts(hidden)
    u = (hidden * cdf).astype(BF)
    du = dot(dy, ws)
    dh = (du * (cdf + hidden * density)).astype(BF)
    acc_ref[...] += dot(u, ws, NT)
    da2_ref[...] += dot(dh, we, NT)
    gs_ref[0] = dot(dy, u, TN).astype(BF)
    ge_ref[0] = dot(a2, dh, TN).astype(BF)
    gu_ref[...] = jnp.sum(dh.astype(F32), axis=0, keepdims=True)

    @pl.when(i == pl.num_programs(0) - 1)
    def _():
        out_ref[...] = acc_ref[...].astype(BF)
        x1 = x1_ref[...]
        top = dy_ref[...].astype(F32)
        centred = x1 - mean_rows(x1)
        scale = lax.rsqrt(mean_rows(centred * centred) + 1e-6)
        xh = centred * scale
        da2 = da2_ref[...]
        e = da2 * vec_ref[5:6]
        dx1 = top + scale * (e - mean_rows(e) - xh * mean_rows(e * xh))
        dx1_ref[...] = dx1
        dxb = dx1.astype(BF)
        for h in range(2):
            cols = slice(h * half, (h + 1) * half)
            do_ref[:, cols] = dot(dxb, wm_ref[h]).astype(BF)
            gm_ref[h] = dot(dxb, o_ref[:, cols], TN).astype(BF)
        gv_ref[0:1] = jnp.sum(dxb.astype(F32), axis=0, keepdims=True)
        gv_ref[1:2] = jnp.sum(da2 * xh, axis=0, keepdims=True)
        gv_ref[2:3] = jnp.sum(da2, axis=0, keepdims=True)
        gv_ref[3:4] = jnp.sum(top, axis=0, keepdims=True)
        gv_ref[4:] = jnp.zeros((4, gv_ref.shape[1]), F32)


def middle(x, o, dy, vectors, wm, we, ws):
    rows, width = x.shape
    hidden = we.shape[2]
    block = 512
    per = hidden // block
    steps = 2 * per
    of_w = pl.BlockSpec((1, width, block), lambda i: (i // per, 0, lax.rem(i, per)))
    of_u = pl.BlockSpec((1, block), lambda i: (0, i))

    def whole(shape):
        return pl.BlockSpec(shape, lambda i: (0,) * len(shape))

    return pl.pallas_call(
        middle_kernel,
        grid=(steps,),
        in_specs=[
            whole((rows, width)),
            whole((rows, width)),
            whole((rows, width)),
            whole(vectors.shape),
            of_u,
            whole(wm.shape),
            of_w,
            of_w,
        ],
        out_specs=[
            whole((rows, width)),
            whole((rows, width)),
            whole((rows, width)),
            whole(wm.shape),
            of_w,
            of_w,
            of_u,
            whole((8, width)),
        ],
        out_shape=[
            jax.ShapeDtypeStruct((rows, width), BF),
            jax.ShapeDtypeStruct((rows, width), F32),
            jax.ShapeDtypeStruct((rows, width), BF),
            jax.ShapeDtypeStruct(wm.shape, BF),
            jax.ShapeDtypeStruct(we.shape, BF),
            jax.ShapeDtypeStruct(ws.shape, BF),
            jax.ShapeDtypeStruct((1, 2 * hidden), F32),
            jax.ShapeDtypeStruct((8, width), F32),
        ],
        scratch_shapes=[
            pltpu.VMEM((rows, width), F32),
            pltpu.VMEM((rows, width), BF),
            pltpu.VMEM((rows, width), F32),
            pltpu.VMEM((rows, width), F32),
        ],
        compiler_params=params(),
        name="middle",
    )(x, o, dy, vectors, vectors[7:11].reshape(1, -1), wm, we, ws)


def unproject_kernel(
    mine_ref, other_ref, dq_ref, dk_ref, dv_ref, w_ref, da_ref, send_ref, gw_ref, gv_ref
):
    rows = mine_ref.shape[0]
    half = w_ref.shape[2] // 3
    da, send = None, None
    gv_ref[...] = jnp.zeros_like(gv_ref)
    for h in range(2):
        cols = slice(h * half, (h + 1) * half)
        dq = dq_ref[:, cols]
        dk, dv = dk_ref[:, cols], dv_ref[:, cols]
        wq, wk, wv = (w_ref[h, :, n * half : (n + 1) * half] for n in range(3))
        mine = dot(dq, wq, NT) + dot(dk[:rows], wk, NT) + dot(dv[:rows], wv, NT)
        other = dot(dk[rows:], wk, NT) + dot(dv[rows:], wv, NT)
        da = mine if da is None else da + mine
        send = other if send is None else send + other
        a, b = mine_ref[...], other_ref[...]
        gw_ref[h, :, :half] = dot(a, dq, TN).astype(BF)
        gw_ref[h, :, half : 2 * half] = (dot(a, dk[:rows], TN) + dot(b, dk[rows:], TN)).astype(BF)
        gw_ref[h, :, 2 * half :] = (dot(a, dv[:rows], TN) + dot(b, dv[rows:], TN)).astype(BF)
        gv_ref[0:1, cols] = jnp.sum(dq.astype(F32), axis=0, keepdims=True)
        gv_ref[1:2, cols] = jnp.sum(dv.astype(F32), axis=0, keepdims=True)
    da_ref[...] = da
    send_ref[...] = send.astype(BF)


def unproject(mine, other, dq, dk, dv, weight):
    rows, width = mine.shape
    return pl.pallas_call(
        unproject_kernel,
        out_shape=[
            jax.ShapeDtypeStruct((rows, width), F32),
            jax.ShapeDtypeStruct((rows, width), BF),
            jax.ShapeDtypeStruct(weight.shape, BF),
            jax.ShapeDtypeStruct((8, width), F32),
        ],
        in_specs=[in_vmem()] * 6,
        out_specs=[in_vmem()] * 4,
        compiler_params=params(),
        name="unproject",
    )(mine, other, dq, dk, dv, weight)


def lamb_terms(weight, moment, square, gradient):
    moment_new = 0.5 * moment + 0.5 * gradient
    square_new = 0.5 * square + 0.5 * gradient * gradient
    correct = 1.0 - 0.5**STEP
    update = moment_new / correct / (jnp.sqrt(square_new / correct) + 1e-06) + 0.01 * weight
    return (
        moment_new,
        square_new,
        update,
        jnp.stack([jnp.sum(weight * weight), jnp.sum(update * update)]),
    )


def lamb_apply(weight, update, norms):
    renewed = weight - 0.5 * norms[0] / (norms[1] + 1e-06) * update
    return (renewed, renewed.astype(BF))


def per_device(
    patches,
    cube_mask,
    mask_token,
    cotangent,
    vectors,
    vector_first,
    vector_second,
    attend_master,
    attend_first,
    attend_second,
    mixing_master,
    mixing_first,
    mixing_second,
    expand_master,
    expand_first,
    expand_second,
    shrink_master,
    shrink_first,
    shrink_second,
):
    clips, rows, width = patches.shape
    axis = lax.axis_size("dp")
    own_rows = attend_master.shape[0]
    direct = axis == 16 and lax.axis_size("mp") == 2
    masters = [
        attend_master.reshape(own_rows, -1),
        mixing_master,
        expand_master,
        shrink_master,
    ]
    shards = [m.astype(BF) for m in masters]
    if direct:
        wa, wm, we, ws = gather_all(shards)
    else:
        wa, wm, we, ws = (
            lax.all_gather(lax.all_gather(s, "dp", axis=0, tiled=True), "mp", axis=0) for s in shards
        )
    swap = [(0, 1), (1, 0)]
    chosen = cube_mask[0, :, None] > 0
    x = jnp.where(chosen, mask_token, patches[0].astype(F32))
    centred = x - mean_rows(x)
    scale = lax.rsqrt(mean_rows(centred * centred) + 1e-6)
    a1 = (centred * scale * vectors[0] + vectors[1]).astype(BF)
    a1_other = lax.ppermute(a1, "mp", swap)
    q, k, v = project(a1, a1_other, wa, vectors[2:4])
    o, o_low, p = attend(q, k, v)
    dy = cotangent[0]
    block_out, dx1, do, gm, ge, gs, gu, gv = middle(x, o_low, dy, vectors, wm, we, ws)
    dq, dk, dv = attend_back(q, k, v, do, o, p)
    da1, da1_send, ga, gqv = unproject(a1, a1_other, dq, dk, dv, wa)
    da1 = da1 + lax.ppermute(da1_send, "mp", swap).astype(F32)
    grads = [ga, gm, ge, gs]
    if direct:
        totals = scatter_all(grads, own_rows)
    else:
        totals = []
        for g in grads:
            g = lax.psum_scatter(g, "mp", scatter_dimension=0, tiled=True)
            totals.append(
                lax.psum_scatter(g[0].astype(F32), "dp", scatter_dimension=0, tiled=True)
            )
    xh = centred * scale
    e = da1 * vectors[0]
    dx = dx1 + scale * (e - mean_rows(e) - xh * mean_rows(e * xh))
    patch_grad = jnp.where(chosen, 0.0, dx).astype(BF)
    token_part = jnp.sum(jnp.where(chosen, dx, 0.0), axis=0)
    vector_part = jnp.concatenate(
        [
            jnp.sum(da1 * xh, axis=0)[None],
            jnp.sum(da1, axis=0)[None],
            gqv[0:2],
            gv[0:3],
            gu.reshape(4, width),
            gv[3:4],
        ],
        axis=0,
    )
    terms = [
        lamb_terms(w, m, s, g)
        for w, m, s, g in zip(
            masters,
            [attend_first.reshape(own_rows, -1), mixing_first, expand_first, shrink_first],
            [attend_second.reshape(own_rows, -1), mixing_second, expand_second, shrink_second],
            totals,
        )
    ]
    squares = jnp.stack([t[3] for t in terms])
    vector_total, token_grad, square_total = lax.psum(
        (vector_part, token_part, squares), ("dp", "mp")
    )
    trust_norms = jnp.sqrt(square_total)
    results = []
    for n, (w, t) in enumerate(zip(masters, terms)):
        group = [t[0], t[1], *lamb_apply(w, t[2], trust_norms[n])]
        if n == 0:
            group = [g.reshape(attend_master.shape) for g in group]
        results.extend(group)
    vector_moment = 0.5 * vector_first + 0.5 * vector_total
    vector_square = 0.5 * vector_second + 0.5 * vector_total * vector_total
    correct = 1.0 - 0.5**STEP
    vector_update = (
        vector_moment / correct / (jnp.sqrt(vector_square / correct) + 1e-06) + 0.01 * vectors
    )
    row_weight = jnp.sqrt(jnp.sum(vectors * vectors, axis=-1, keepdims=True))
    row_update = jnp.sqrt(jnp.sum(vector_update * vector_update, axis=-1, keepdims=True))
    vector_weight = vectors - 0.5 * row_weight / (row_update + 1e-06) * vector_update
    return (
        block_out[None],
        patch_grad[None],
        token_grad,
        vector_total[11],
        *results,
        vector_moment,
        vector_square,
        vector_weight,
        trust_norms,
    )


def solution(mesh):
    rows = P("dp", "mp", None)
    flat = P("dp", "mp")
    deep = P("dp", None, "mp")
    copied = P()
    return jax.shard_map(
        per_device,
        mesh=mesh,
        in_specs=(rows, flat, copied, rows, copied, copied, copied, *[deep] * 3, *[flat] * 9),
        out_specs=(rows, rows, copied, copied, *[deep] * 4, *[flat] * 12, *[copied] * 4),
        check_vma=False,
    )
```

```python
import functools

import jax
import jax.numpy as jnp
from jax import lax
from jax.experimental import pallas as pl
from jax.experimental.pallas import tpu as pltpu
from jax.sharding import PartitionSpec as P

HD = 64
PAIR = 2 * HD
STEP = 5
BF = jnp.bfloat16
F32 = jnp.float32
NN = (((1,), (0,)), ((), ()))
NT = (((1,), (1,)), ((), ()))
TN = (((0,), (0,)), ((), ()))
LOG2E = 1.4426950408889634
MESH = pl.DeviceIdType.MESH
VMEM_LIMIT = 60 * 2**20


def dot(a, b, dims=NN):
    return lax.dot_general(a, b, dims, preferred_element_type=F32)


def params(**kw):
    return pltpu.CompilerParams(vmem_limit_bytes=VMEM_LIMIT, **kw)


def anywhere():
    return pl.BlockSpec(memory_space=pl.ANY)


def in_vmem():
    return pl.BlockSpec(memory_space=pltpu.VMEM)


def place():
    dp, x = lax.axis_index("dp"), lax.axis_index("mp")
    return x, dp // 4, lax.rem(dp // 2, 2), lax.rem(dp, 2)


def device(x, z, y, c):
    return ((z * 2 + y) * 2 + c, x)


def neighbours():
    x, z, y, c = place()
    lines = [device(x, lax.rem(z + k, 4), y, c) for k in (1, 2, 3)]
    return lines, device(1 - x, z, y, c), device(x, z, 1 - y, c), device(x, z, y, 1 - c)


def greet():
    lines, over_x, over_y, sibling = neighbours()
    barrier = pltpu.get_barrier_semaphore()
    for other in (*lines, over_x, over_y, sibling):
        pl.semaphore_signal(barrier, inc=1, device_id=other, device_id_type=MESH)
    pl.semaphore_wait(barrier, 6)


class Wires:
    def __init__(self, send_sem, recv_sem):
        self.send_sem, self.recv_sem = send_sem, recv_sem
        self.started = []

    def copy(self, slot, src, dst, other):
        return pltpu.make_async_remote_copy(
            src_ref=src,
            dst_ref=dst,
            send_sem=self.send_sem.at[slot],
            recv_sem=self.recv_sem.at[slot],
            device_id=other,
            device_id_type=MESH,
        )

    def start(self, slot, src, dst, other):
        self.copy(slot, src, dst, other).start()
        self.started.append((slot, src))

    def send(self, slot, whole, part, other):
        self.copy(slot, whole.at[part], whole.at[part], other).start()
        self.started.append((slot, whole, part))

    def arrive(self, slot, dst):
        x, z, y, c = place()
        self.copy(slot, dst, dst, device(x, z, y, 1 - c)).wait_recv()

    def sent(self, slot, src):
        x, z, y, c = place()
        self.copy(slot, src, src, device(x, z, y, 1 - c)).wait_send()

    def drain(self):
        for slot, src, *part in self.started:
            self.sent(slot, src.at[part[0]] if part else src)


ALL = slice(None)


def first_kernel(*refs):
    (sa, sm, se, ss, patch_ref, mask_ref, token_ref, vec_ref) = refs[:8]
    (wa_out, wm, we, ws, q_ref, k_ref, v_ref, a1_ref, other_ref) = refs[8:17]
    wa, landing, own_sem, send_sem, recv_sem = refs[17:]
    x, z, y, c = place()
    lines, over_x, over_y, sibling = neighbours()
    wires = Wires(send_sem, recv_sem)
    rows = a1_ref.shape[0]
    cut = rows // 32 * 16
    halves = (pl.ds(0, cut), pl.ds(cut, rows - cut))
    greet()

    def back(k):
        return lax.rem(z + 4 - k, 4)

    own = [pltpu.make_async_copy(sa, wa.at[x, z, y, c], own_sem.at[0])]
    for n, (shard, whole) in enumerate(((sm, wm), (se, we), (ss, ws))):
        own.append(pltpu.make_async_copy(shard, whole.at[x, z, y, c], own_sem.at[n + 1]))
    for copy in own:
        copy.start()
    for k in (1, 2, 3):
        wires.start(k - 1, sa, wa.at[x, z, y, c], lines[k - 1])
    wires.start(3, sa, wa.at[x, z, y, c], over_x)
    wires.start(7, sa, wa.at[x, z, y, c], over_y)

    tubes = jnp.where(mask_ref[...] > 0, token_ref[...], patch_ref[...].astype(F32))
    centred = tubes - mean_rows(tubes)
    scale = lax.rsqrt(mean_rows(centred * centred) + 1e-6)
    a1_ref[...] = (centred * scale * vec_ref[0:1] + vec_ref[1:2]).astype(BF)
    wires.start(19, a1_ref.at[halves[0]], landing.at[halves[0]], over_x)

    for k in (1, 2, 3):
        part = wa.at[x, back(k), y, c]
        wires.arrive(k - 1, part)
        wires.start(3 + k, part, part, over_x)
        wires.start(7 + k, part, part, over_y)
    wires.start(20, a1_ref.at[halves[1]], landing.at[halves[1]], over_x)
    for copy in own:
        copy.wait()
    line = wa.at[x, ALL, y, c]
    wires.start(15, line, line, sibling)
    others = ((sm, wm), (se, we), (ss, ws))
    for n, (shard, whole) in enumerate(others):
        for k in (1, 2, 3):
            wires.start(21 + 3 * n + k - 1, shard, whole.at[x, z, y, c], lines[k - 1])
    for k in range(4):
        part = wa.at[1 - x, back(k), y, c]
        wires.arrive(3 + k, part)
        wires.start(11 + k, part, part, over_y)
    for n in range(2):
        shard, whole = others[n]
        wires.start(30 + 4 * n, shard, whole.at[x, z, y, c], over_y)
    line = wa.at[1 - x, ALL, y, c]
    wires.start(16, line, line, sibling)
    for k in range(4):
        wires.arrive(7 + k, wa.at[x, back(k), 1 - y, c])
    line = wa.at[x, ALL, 1 - y, c]
    wires.start(17, line, line, sibling)

    def pass_on(n):
        whole = others[n][1]
        for k in (1, 2, 3):
            part = whole.at[x, back(k), y, c]
            wires.arrive(21 + 3 * n + k - 1, part)
            wires.start(30 + 4 * n + k, part, part, over_y)

    pass_on(0)
    for k in range(4):
        wires.arrive(11 + k, wa.at[1 - x, back(k), 1 - y, c])
    line = wa.at[1 - x, ALL, 1 - y, c]
    wires.start(18, line, line, sibling)
    for n, (i, j) in enumerate(((x, y), (1 - x, y), (x, 1 - y), (1 - x, 1 - y))):
        wires.arrive(15 + n, wa.at[i, ALL, j, 1 - c])
    out_copy = pltpu.make_async_copy(wa, wa_out, own_sem.at[0])
    out_copy.start()

    width = wa.shape[-1] // 3
    depth = a1_ref.shape[1]

    def weight(h, n):
        return wa[h, :, :, :, :, n * width : (n + 1) * width].reshape(depth, width)

    def keys_values(h, source, span):
        k_ref[h, span] = dot(source, weight(h, 1)).astype(BF)
        values = dot(source, weight(h, 2)) + vec_ref[3:4, h * width : (h + 1) * width]
        v_ref[h, span] = values.astype(BF)

    for h in range(2):
        queries = dot(a1_ref[...], weight(h, 0)) + vec_ref[2:3, h * width : (h + 1) * width]
        q_ref[h] = (queries.astype(BF).astype(F32) * HD**-0.5).astype(BF)
        keys_values(h, a1_ref[...], pl.ds(0, rows))
    pass_on(1)
    for n in range(2):
        wires.arrive(19 + n, landing.at[halves[n]])
        part = landing[halves[n]]
        other_ref[halves[n]] = part
        span = pl.ds(rows + (cut if n else 0), part.shape[0])
        for h in range(2):
            keys_values(h, part, span)
    for n in range(2):
        for k in range(4):
            wires.arrive(30 + 4 * n + k, others[n][1].at[x, back(k), 1 - y, c])
    for k in (1, 2, 3):
        wires.arrive(27 + k - 1, ws.at[x, back(k), y, c])
    out_copy.wait()
    wires.drain()


def first(shards, patches, mask, token, vectors):
    rows, width = patches.shape
    half = width // 2
    gathered = [(2, 4, 2, 2, *s.shape) for s in shards]
    wholes = [jax.ShapeDtypeStruct(g, BF) for g in gathered]
    keys = jax.ShapeDtypeStruct((2, 2 * rows, half), BF)
    flat = jax.ShapeDtypeStruct((rows, width), BF)
    return pl.pallas_call(
        first_kernel,
        out_shape=[*wholes, jax.ShapeDtypeStruct((2, rows, half), BF), keys, keys, flat, flat],
        in_specs=[anywhere()] * 4 + [in_vmem()] * 4,
        out_specs=[anywhere()] * 4 + [in_vmem()] * 5,
        scratch_shapes=[
            pltpu.VMEM(gathered[0], BF),
            pltpu.VMEM((rows, width), BF),
            pltpu.SemaphoreType.DMA((4,)),
            pltpu.SemaphoreType.DMA((38,)),
            pltpu.SemaphoreType.DMA((38,)),
        ],
        compiler_params=params(collective_id=0, has_side_effects=True),
        name="first",
    )(*shards, patches, mask, token, vectors)


def scatter_kernel(count, *refs):
    grads, totals = refs[:count], refs[count : 2 * count]
    refs = refs[2 * count :]
    mine, sib, diag, side, far = (refs[k * count : (k + 1) * count] for k in range(5))
    own_sem, send_sem, recv_sem = refs[5 * count :]
    x, z, y, c = place()
    lines, over_x, over_y, sibling = neighbours()
    greet()

    def remote(i, slot, src, dst, other):
        return pltpu.make_async_remote_copy(
            src_ref=src,
            dst_ref=dst,
            send_sem=send_sem.at[i, slot],
            recv_sem=recv_sem.at[i, slot],
            device_id=other,
            device_id_type=MESH,
        )

    def add(dst, one, other):
        dst[...] = (one[...].astype(F32) + other[...].astype(F32)).astype(BF)

    def own(i):
        return pltpu.make_async_copy(grads[i].at[:, :, :, c], mine[i], own_sem.at[i])

    def step_one(i):
        return remote(i, 0, grads[i].at[:, :, :, 1 - c], sib[i], sibling)

    def step_two(i):
        return [
            remote(i, 1, mine[i].at[1 - x, pl.ds(0, 2), 1 - y], diag[i].at[0], over_x),
            remote(i, 2, mine[i].at[1 - x, pl.ds(2, 2), 1 - y], diag[i].at[1], over_y),
        ]

    def step_three(i):
        return [
            remote(i, 3, mine[i].at[1 - x, :, y], side[i].at[0], over_x),
            remote(i, 4, mine[i].at[x, :, 1 - y], side[i].at[1], over_y),
        ]

    def step_four(i):
        return [
            remote(i, 4 + k, mine[i].at[x, lax.rem(z + k, 4), y], far[i].at[k - 1], lines[k - 1])
            for k in (1, 2, 3)
        ]

    started = []

    def start(copies):
        for copy in copies:
            copy.start()
            started.append(copy)

    for i in range(count):
        own(i).start()
        start([step_one(i)])
    for turn in range(count + 3):
        if turn < count:
            i = turn
            own(i).wait()
            step_one(i).wait_recv()

            def sweep(n, _, i=i):
                part = (n // 8, lax.rem(n // 2, 4), lax.rem(n, 2))
                add(mine[i].at[part], mine[i].at[part], sib[i].at[part])
                return 0

            lax.fori_loop(0, 16, sweep, 0)
            start(step_two(i))
        if 0 <= turn - 1 < count:
            i = turn - 1
            two = step_two(i)
            for copy in two:
                copy.wait()

            def sweep(n, _, i=i):
                low, high = (x, n, 1 - y), (1 - x, 2 + n, y)
                add(mine[i].at[low], mine[i].at[low], diag[i].at[0, n])
                add(mine[i].at[high], mine[i].at[high], diag[i].at[1, n])
                return 0

            lax.fori_loop(0, 2, sweep, 0)
            start(step_three(i))
        if 0 <= turn - 2 < count:
            i = turn - 2
            three = step_three(i)
            for copy in three:
                copy.wait()

            def sweep(n, _, i=i):
                part = mine[i].at[x, n, y]
                both = side[i][0, n].astype(F32) + side[i][1, n].astype(F32)
                part[...] = (part[...].astype(F32) + both).astype(BF)
                return 0

            lax.fori_loop(0, 4, sweep, 0)
            start(step_four(i))
        if 0 <= turn - 3 < count:
            i = turn - 3
            for copy in step_four(i):
                copy.wait()
            total = mine[i][x, z, y].astype(F32)
            for k in range(3):
                total = total + far[i][k].astype(F32)
            totals[i][...] = total
    for i in range(count):
        step_one(i).wait_send()


def scatter_all(grads, rows):
    count = len(grads)
    widths = [g.shape[-1] for g in grads]
    grads = [g.reshape(2, 4, 2, 2, rows, w) for g, w in zip(grads, widths)]
    return pl.pallas_call(
        functools.partial(scatter_kernel, count),
        out_shape=[jax.ShapeDtypeStruct((rows, w), F32) for w in widths],
        in_specs=[anywhere()] * count,
        out_specs=[in_vmem()] * count,
        scratch_shapes=[pltpu.VMEM((2, 4, 2, rows, w), BF) for w in widths]
        + [pltpu.VMEM((2, 4, 2, rows, w), BF) for w in widths]
        + [pltpu.VMEM((2, 2, rows, w), BF) for w in widths]
        + [pltpu.VMEM((2, 4, rows, w), BF) for w in widths]
        + [pltpu.VMEM((3, rows, w), BF) for w in widths]
        + [
            pltpu.SemaphoreType.DMA((count,)),
            pltpu.SemaphoreType.DMA((count, 8)),
            pltpu.SemaphoreType.DMA((count, 8)),
        ],
        compiler_params=params(collective_id=1, has_side_effects=True),
        name="scatter_grads",
    )(*grads)


def project_kernel(mine_ref, other_ref, w_ref, bias_ref, q_ref, k_ref, v_ref):
    rows = mine_ref.shape[0]
    half = w_ref.shape[2] // 3
    for h in range(2):
        cols = slice(h * half, (h + 1) * half)
        queries = dot(mine_ref[...], w_ref[h, :, :half]) + bias_ref[0:1, cols]
        q_ref[h] = (queries.astype(BF).astype(F32) * HD**-0.5).astype(BF)
        for part, ref in ((0, mine_ref), (1, other_ref)):
            span = slice(part * rows, (part + 1) * rows)
            k_ref[h, span] = dot(ref[...], w_ref[h, :, half : 2 * half]).astype(BF)
            v_ref[h, span] = (dot(ref[...], w_ref[h, :, 2 * half :]) + bias_ref[1:2, cols]).astype(BF)


def project(mine, other, weight, bias):
    rows, width = mine.shape
    keys = jax.ShapeDtypeStruct((2, 2 * rows, width // 2), BF)
    return pl.pallas_call(
        project_kernel,
        out_shape=[jax.ShapeDtypeStruct((2, rows, width // 2), BF), keys, keys],
        in_specs=[in_vmem()] * 4,
        out_specs=[in_vmem()] * 3,
        compiler_params=params(),
        name="project",
    )(mine, other, weight, bias)


def half_lanes():
    lane = lax.broadcasted_iota(jnp.int32, (1, PAIR), 1)
    return lane < HD, lane >= HD


def attend_head(h, q, k, v, p_ref):
    s = dot(jnp.where(half_lanes()[h], q, jnp.zeros_like(q)), k, NT)
    top = jnp.max(s, axis=-1, keepdims=True)
    e = jnp.exp2(s * LOG2E - top * LOG2E)
    total = jnp.sum(e, axis=-1, keepdims=True)
    p = (e * (1.0 / total)).astype(BF)
    p_ref[h] = p
    return dot(p, v)


def attend_plain_kernel(q_ref, k_ref, v_ref, o_ref, low_ref, p_ref):
    q, k, v = q_ref[0], k_ref[0], v_ref[0]
    o = jnp.where(half_lanes()[0], *(attend_head(h, q, k, v, p_ref) for h in range(2)))
    o_ref[0] = o
    low_ref[0] = o.astype(BF)


def attend_kernel(*refs):
    q_ref, k_ref, v_ref = refs[:3]
    o_ref, low_ref, p_ref, wm, we, ws, send_sem, recv_sem = refs[6:]
    i = pl.program_id(0)
    x, z, y, c = place()
    lines, over_x, over_y, sibling = neighbours()
    wires = Wires(send_sem, recv_sem)
    here, side, flank, across = (x, ALL, y, c), (1 - x, ALL, y, c), (x, ALL, 1 - y, c), (1 - x, ALL, 1 - y, c)

    send = wires.send

    @pl.when(i == 0)
    def _():
        greet()
        send(0, wm, here, over_x)
        send(1, we, here, over_x)
        send(2, ws, here, over_y)
        send(3, ws, here, over_x)
        send(4, wm, flank, over_x)
        send(5, wm, here, sibling)
        send(6, wm, flank, sibling)
        send(7, we, here, sibling)
        send(8, we, flank, sibling)
        send(9, ws, here, sibling)

    @pl.when(i == 2)
    def _():
        wires.arrive(0, wm.at[side])
        send(10, wm, side, sibling)
        wires.arrive(1, we.at[side])
        send(11, we, side, over_y)
        send(12, we, side, sibling)

    @pl.when(i == 4)
    def _():
        wires.arrive(3, ws.at[side])
        send(13, ws, side, over_y)
        send(14, ws, side, sibling)
        wires.arrive(2, ws.at[flank])
        send(15, ws, flank, sibling)
        wires.arrive(4, wm.at[across])
        send(16, wm, across, sibling)

    q, k, v = q_ref[0], k_ref[0], v_ref[0]
    o = jnp.where(half_lanes()[0], *(attend_head(h, q, k, v, p_ref) for h in range(2)))
    o_ref[0] = o
    low_ref[0] = o.astype(BF)

    @pl.when(i == pl.num_programs(0) - 1)
    def _():
        wires.arrive(11, we.at[across])
        send(17, we, across, sibling)
        wires.arrive(13, ws.at[across])
        send(18, ws, across, sibling)
        for slot, whole, (a, b) in (
            (5, wm, (x, y)),
            (6, wm, (x, 1 - y)),
            (7, we, (x, y)),
            (8, we, (x, 1 - y)),
            (9, ws, (x, y)),
            (10, wm, (1 - x, y)),
            (12, we, (1 - x, y)),
            (14, ws, (1 - x, y)),
            (15, ws, (x, 1 - y)),
            (16, wm, (1 - x, 1 - y)),
            (17, we, (1 - x, 1 - y)),
            (18, ws, (1 - x, 1 - y)),
        ):
            wires.arrive(slot, whole.at[a, ALL, b, 1 - c])
        wires.drain()


def attend(q, k, v, wholes):
    _, rows, half = q.shape
    keys = k.shape[1]
    per = half // PAIR
    of_q = pl.BlockSpec((1, rows, PAIR), lambda i: (i // per, 0, lax.rem(i, per)))
    of_k = pl.BlockSpec((1, keys, PAIR), lambda i: (i // per, 0, lax.rem(i, per)))
    shapes = [
        jax.ShapeDtypeStruct(q.shape, F32),
        jax.ShapeDtypeStruct(q.shape, BF),
        jax.ShapeDtypeStruct((4 * per, rows, keys), BF),
    ]
    of_p = pl.BlockSpec((2, rows, keys), lambda i: (i, 0, 0))
    common = dict(grid=(2 * per,), name="attend")
    if not wholes:
        return pl.pallas_call(
            attend_plain_kernel,
            in_specs=[of_q, of_k, of_k],
            out_specs=[of_q, of_q, of_p],
            out_shape=shapes,
            compiler_params=params(),
            **common,
        )(q, k, v)
    return pl.pallas_call(
        attend_kernel,
        in_specs=[of_q, of_k, of_k, *[anywhere()] * 3],
        out_specs=[of_q, of_q, of_p, *[anywhere()] * 3],
        out_shape=[*shapes, *[jax.ShapeDtypeStruct(w.shape, BF) for w in wholes]],
        input_output_aliases={3: 3, 4: 4, 5: 5},
        scratch_shapes=[pltpu.SemaphoreType.DMA((19,)), pltpu.SemaphoreType.DMA((19,))],
        compiler_params=params(collective_id=2, has_side_effects=True),
        **common,
    )(q, k, v, *wholes)


def attend_back_kernel(q_ref, k_ref, v_ref, do_ref, o_ref, p_ref, dq_ref, dk_ref, dv_ref):
    sides = half_lanes()
    q, k, v, do = q_ref[0], k_ref[0], v_ref[0], do_ref[0]
    prod = do.astype(F32) * o_ref[0]
    outs, grad_k, grad_v = [], None, None
    for h in range(2):
        do_h = jnp.where(sides[h], do, jnp.zeros_like(do))
        q_h = jnp.where(sides[h], q, jnp.zeros_like(q))
        grad_p = dot(do_h, v, NT)
        row_dot = jnp.sum(jnp.where(sides[h], prod, 0.0), axis=-1, keepdims=True)
        p = p_ref[h]
        ds = (p.astype(F32) * (grad_p - row_dot)).astype(BF)
        outs.append(dot(ds, k))
        more_k, more_v = dot(ds, q_h, TN), dot(p, do_h, TN)
        grad_k = more_k if grad_k is None else grad_k + more_k
        grad_v = more_v if grad_v is None else grad_v + more_v
    dq_ref[0] = (jnp.where(sides[0], outs[0], outs[1]) * HD**-0.5).astype(BF)
    dk_ref[0] = grad_k.astype(BF)
    dv_ref[0] = grad_v.astype(BF)


def attend_back(q, k, v, do, o, p):
    _, rows, half = q.shape
    keys = k.shape[1]
    per = half // PAIR
    of_q = pl.BlockSpec((1, rows, PAIR), lambda i: (i // per, 0, lax.rem(i, per)))
    of_k = pl.BlockSpec((1, keys, PAIR), lambda i: (i // per, 0, lax.rem(i, per)))
    return pl.pallas_call(
        attend_back_kernel,
        grid=(2 * per,),
        in_specs=[of_q, of_k, of_k, of_q, of_q, pl.BlockSpec((2, rows, keys), lambda i: (i, 0, 0))],
        out_specs=[of_q, of_k, of_k],
        out_shape=[
            jax.ShapeDtypeStruct(q.shape, BF),
            jax.ShapeDtypeStruct(k.shape, BF),
            jax.ShapeDtypeStruct(k.shape, BF),
        ],
        compiler_params=params(),
        name="attend_back",
    )(q, k, v, do, o, p)


def normal_parts(h):
    z = jnp.abs(h) * 0.7071067811865476
    t = 1.0 / (1.0 + 0.3275911 * z)
    bell = jnp.exp(-z * z)
    poly = t * (
        0.254829592
        + t * (-0.284496736 + t * (1.421413741 + t * (-1.453152027 + t * 1.061405429)))
    )
    tail = 0.5 * poly * bell
    return jnp.where(h < 0, tail, 1.0 - tail), bell * 0.3989422804014327


def mean_rows(values):
    return jnp.mean(values, axis=-1, keepdims=True)


def middle_kernel(
    patch_ref,
    mask_ref,
    token_ref,
    o_ref,
    dy_ref,
    vec_ref,
    bu_ref,
    wm_ref,
    we_ref,
    ws_ref,
    out_ref,
    dx1_ref,
    do_ref,
    gm_ref,
    ge_ref,
    gs_ref,
    gu_ref,
    gv_ref,
    x1_ref,
    a2_ref,
    acc_ref,
    da2_ref,
):
    i = pl.program_id(0)

    @pl.when(i == 0)
    def _():
        x1 = jnp.where(mask_ref[...] > 0, token_ref[...], patch_ref[...].astype(F32)) + vec_ref[4:5]
        for h in range(2):
            x1 = x1 + dot(o_ref[h], wm_ref[h], NT)
        x1_ref[...] = x1
        centred = x1 - mean_rows(x1)
        scale = lax.rsqrt(mean_rows(centred * centred) + 1e-6)
        a2_ref[...] = (centred * scale * vec_ref[5:6] + vec_ref[6:7]).astype(BF)
        acc_ref[...] = x1 + vec_ref[11:12]
        da2_ref[...] = jnp.zeros_like(da2_ref)

    a2, dy = a2_ref[...], dy_ref[...]
    we, ws = we_ref[0], ws_ref[0]
    hidden = dot(a2, we) + bu_ref[...]
    cdf, density = normal_parts(hidden)
    u = (hidden * cdf).astype(BF)
    du = dot(dy, ws)
    dh = (du * (cdf + hidden * density)).astype(BF)
    acc_ref[...] += dot(u, ws, NT)
    da2_ref[...] += dot(dh, we, NT)
    gs_ref[0] = dot(dy, u, TN).astype(BF)
    ge_ref[0] = dot(a2, dh, TN).astype(BF)
    gu_ref[...] = jnp.sum(dh.astype(F32), axis=0, keepdims=True)

    @pl.when(i == pl.num_programs(0) - 1)
    def _():
        out_ref[...] = acc_ref[...].astype(BF)
        x1 = x1_ref[...]
        top = dy_ref[...].astype(F32)
        centred = x1 - mean_rows(x1)
        scale = lax.rsqrt(mean_rows(centred * centred) + 1e-6)
        xh = centred * scale
        da2 = da2_ref[...]
        e = da2 * vec_ref[5:6]
        dx1 = top + scale * (e - mean_rows(e) - xh * mean_rows(e * xh))
        dx1_ref[...] = dx1
        dxb = dx1.astype(BF)
        for h in range(2):
            do_ref[h] = dot(dxb, wm_ref[h]).astype(BF)
            gm_ref[h] = dot(dxb, o_ref[h], TN).astype(BF)
        gv_ref[0:1] = jnp.sum(dxb.astype(F32), axis=0, keepdims=True)
        gv_ref[1:2] = jnp.sum(da2 * xh, axis=0, keepdims=True)
        gv_ref[2:3] = jnp.sum(da2, axis=0, keepdims=True)
        gv_ref[3:4] = jnp.sum(top, axis=0, keepdims=True)
        gv_ref[4:] = jnp.zeros((4, gv_ref.shape[1]), F32)


def middle(patches, mask, token, o, dy, vectors, wm, we, ws):
    rows, width = patches.shape
    hidden = we.shape[2]
    block = 512
    per = hidden // block
    steps = 2 * per
    of_w = pl.BlockSpec((1, width, block), lambda i: (i // per, 0, lax.rem(i, per)))
    of_u = pl.BlockSpec((1, block), lambda i: (0, i))

    def whole(shape):
        return pl.BlockSpec(shape, lambda i: (0,) * len(shape))

    return pl.pallas_call(
        middle_kernel,
        grid=(steps,),
        in_specs=[
            whole((rows, width)),
            whole((rows, 1)),
            whole((1, width)),
            whole(o.shape),
            whole((rows, width)),
            whole(vectors.shape),
            of_u,
            whole(wm.shape),
            of_w,
            of_w,
        ],
        out_specs=[
            whole((rows, width)),
            whole((rows, width)),
            whole(o.shape),
            whole(wm.shape),
            of_w,
            of_w,
            of_u,
            whole((8, width)),
        ],
        out_shape=[
            jax.ShapeDtypeStruct((rows, width), BF),
            jax.ShapeDtypeStruct((rows, width), F32),
            jax.ShapeDtypeStruct(o.shape, BF),
            jax.ShapeDtypeStruct(wm.shape, BF),
            jax.ShapeDtypeStruct(we.shape, BF),
            jax.ShapeDtypeStruct(ws.shape, BF),
            jax.ShapeDtypeStruct((1, 2 * hidden), F32),
            jax.ShapeDtypeStruct((8, width), F32),
        ],
        scratch_shapes=[
            pltpu.VMEM((rows, width), F32),
            pltpu.VMEM((rows, width), BF),
            pltpu.VMEM((rows, width), F32),
            pltpu.VMEM((rows, width), F32),
        ],
        compiler_params=params(),
        name="middle",
    )(patches, mask, token, o, dy, vectors, vectors[7:11].reshape(1, -1), wm, we, ws)


def unproject_kernel(
    mine_ref, other_ref, dq_ref, dk_ref, dv_ref, w_ref, da_ref, send_ref, gw_ref, gv_ref
):
    rows = mine_ref.shape[0]
    half = w_ref.shape[2] // 3
    da, send = None, None
    gv_ref[...] = jnp.zeros_like(gv_ref)
    for h in range(2):
        cols = slice(h * half, (h + 1) * half)
        dq, dk, dv = dq_ref[h], dk_ref[h], dv_ref[h]
        wq, wk, wv = (w_ref[h, :, n * half : (n + 1) * half] for n in range(3))
        mine = dot(dq, wq, NT) + dot(dk[:rows], wk, NT) + dot(dv[:rows], wv, NT)
        other = dot(dk[rows:], wk, NT) + dot(dv[rows:], wv, NT)
        da = mine if da is None else da + mine
        send = other if send is None else send + other
        a, b = mine_ref[...], other_ref[...]
        gw_ref[h, :, :half] = dot(a, dq, TN).astype(BF)
        gw_ref[h, :, half : 2 * half] = (dot(a, dk[:rows], TN) + dot(b, dk[rows:], TN)).astype(BF)
        gw_ref[h, :, 2 * half :] = (dot(a, dv[:rows], TN) + dot(b, dv[rows:], TN)).astype(BF)
        gv_ref[0:1, cols] = jnp.sum(dq.astype(F32), axis=0, keepdims=True)
        gv_ref[1:2, cols] = jnp.sum(dv.astype(F32), axis=0, keepdims=True)
    da_ref[...] = da
    send_ref[...] = send.astype(BF)


def unproject(mine, other, dq, dk, dv, weight):
    rows, width = mine.shape
    return pl.pallas_call(
        unproject_kernel,
        out_shape=[
            jax.ShapeDtypeStruct((rows, width), F32),
            jax.ShapeDtypeStruct((rows, width), BF),
            jax.ShapeDtypeStruct(weight.shape, BF),
            jax.ShapeDtypeStruct((8, width), F32),
        ],
        in_specs=[in_vmem()] * 6,
        out_specs=[in_vmem()] * 4,
        compiler_params=params(),
        name="unproject",
    )(mine, other, dq, dk, dv, weight)


def lamb_terms(weight, moment, square, gradient):
    moment_new = 0.5 * moment + 0.5 * gradient
    square_new = 0.5 * square + 0.5 * gradient * gradient
    correct = 1.0 - 0.5**STEP
    update = moment_new / correct / (jnp.sqrt(square_new / correct) + 1e-06) + 0.01 * weight
    return (
        moment_new,
        square_new,
        update,
        jnp.stack([jnp.sum(weight * weight), jnp.sum(update * update)]),
    )


def lamb_apply(weight, update, norms):
    renewed = weight - 0.5 * norms[0] / (norms[1] + 1e-06) * update
    return (renewed, renewed.astype(BF))


def per_device(
    patches,
    cube_mask,
    mask_token,
    cotangent,
    vectors,
    vector_first,
    vector_second,
    attend_master,
    attend_first,
    attend_second,
    mixing_master,
    mixing_first,
    mixing_second,
    expand_master,
    expand_first,
    expand_second,
    shrink_master,
    shrink_first,
    shrink_second,
):
    clips, rows, width = patches.shape
    axis = lax.axis_size("dp")
    own_rows = attend_master.shape[0]
    direct = axis == 16 and lax.axis_size("mp") == 2
    masters = [
        attend_master.reshape(own_rows, -1),
        mixing_master,
        expand_master,
        shrink_master,
    ]
    shards = [m.astype(BF) for m in masters]
    swap = [(0, 1), (1, 0)]
    mask, token, dy = cube_mask.reshape(rows, 1), mask_token[None], cotangent[0]
    chosen = mask > 0
    x = jnp.where(chosen, token, patches[0].astype(F32))
    centred = x - mean_rows(x)
    scale = lax.rsqrt(mean_rows(centred * centred) + 1e-6)
    if direct:
        *wholes, q, k, v, a1, a1_other = first(shards, patches[0], mask, token, vectors)
        wa = wholes[0].reshape(2, width, -1)
        o, o_low, p, *rest = attend(q, k, v, wholes[1:])
        wm, we, ws = (w.reshape(2, width, -1) for w in rest)
    else:
        wa, wm, we, ws = (
            lax.all_gather(lax.all_gather(s, "dp", axis=0, tiled=True), "mp", axis=0) for s in shards
        )
        a1 = (centred * scale * vectors[0] + vectors[1]).astype(BF)
        a1_other = lax.ppermute(a1, "mp", swap)
        q, k, v = project(a1, a1_other, wa, vectors[2:4])
        o, o_low, p = attend(q, k, v, [])
    block_out, dx1, do, gm, ge, gs, gu, gv = middle(
        patches[0], mask, token, o_low, dy, vectors, wm, we, ws
    )
    dq, dk, dv = attend_back(q, k, v, do, o, p)
    da1, da1_send, ga, gqv = unproject(a1, a1_other, dq, dk, dv, wa)
    da1 = da1 + lax.ppermute(da1_send, "mp", swap).astype(F32)
    grads = [ga, gm, ge, gs]
    if direct:
        totals = scatter_all(grads, own_rows)
    else:
        totals = []
        for g in grads:
            g = lax.psum_scatter(g, "mp", scatter_dimension=0, tiled=True)
            totals.append(
                lax.psum_scatter(g[0].astype(F32), "dp", scatter_dimension=0, tiled=True)
            )
    xh = centred * scale
    e = da1 * vectors[0]
    dx = dx1 + scale * (e - mean_rows(e) - xh * mean_rows(e * xh))
    patch_grad = jnp.where(chosen, 0.0, dx).astype(BF)
    token_part = jnp.sum(jnp.where(chosen, dx, 0.0), axis=0)
    vector_part = jnp.concatenate(
        [
            jnp.sum(da1 * xh, axis=0)[None],
            jnp.sum(da1, axis=0)[None],
            gqv[0:2],
            gv[0:3],
            gu.reshape(4, width),
            gv[3:4],
        ],
        axis=0,
    )
    terms = [
        lamb_terms(w, m, s, g)
        for w, m, s, g in zip(
            masters,
            [attend_first.reshape(own_rows, -1), mixing_first, expand_first, shrink_first],
            [attend_second.reshape(own_rows, -1), mixing_second, expand_second, shrink_second],
            totals,
        )
    ]
    squares = jnp.stack([t[3] for t in terms])
    vector_total, token_grad, square_total = lax.psum(
        (vector_part, token_part, squares), ("dp", "mp")
    )
    trust_norms = jnp.sqrt(square_total)
    results = []
    for n, (w, t) in enumerate(zip(masters, terms)):
        group = [t[0], t[1], *lamb_apply(w, t[2], trust_norms[n])]
        if n == 0:
            group = [g.reshape(attend_master.shape) for g in group]
        results.extend(group)
    vector_moment = 0.5 * vector_first + 0.5 * vector_total
    vector_square = 0.5 * vector_second + 0.5 * vector_total * vector_total
    correct = 1.0 - 0.5**STEP
    vector_update = (
        vector_moment / correct / (jnp.sqrt(vector_square / correct) + 1e-06) + 0.01 * vectors
    )
    row_weight = jnp.sqrt(jnp.sum(vectors * vectors, axis=-1, keepdims=True))
    row_update = jnp.sqrt(jnp.sum(vector_update * vector_update, axis=-1, keepdims=True))
    vector_weight = vectors - 0.5 * row_weight / (row_update + 1e-06) * vector_update
    return (
        block_out[None],
        patch_grad[None],
        token_grad,
        vector_total[11],
        *results,
        vector_moment,
        vector_square,
        vector_weight,
        trust_norms,
    )


def solution(mesh):
    rows = P("dp", "mp", None)
    flat = P("dp", "mp")
    deep = P("dp", None, "mp")
    copied = P()
    return jax.shard_map(
        per_device,
        mesh=mesh,
        in_specs=(rows, flat, copied, rows, copied, copied, copied, *[deep] * 3, *[flat] * 9),
        out_specs=(rows, rows, copied, copied, *[deep] * 4, *[flat] * 12, *[copied] * 4),
        check_vma=False,
    )
```

```python
import functools

import jax
import jax.numpy as jnp
from jax import lax
from jax.experimental import pallas as pl
from jax.experimental.pallas import tpu as pltpu
from jax.sharding import PartitionSpec as P

HD = 64
PAIR = 2 * HD
STEP = 5
BF = jnp.bfloat16
F32 = jnp.float32
NN = (((1,), (0,)), ((), ()))
NT = (((1,), (1,)), ((), ()))
TN = (((0,), (0,)), ((), ()))
LOG2E = 1.4426950408889634
MESH = pl.DeviceIdType.MESH
VMEM_LIMIT = 60 * 2**20


def dot(a, b, dims=NN):
    return lax.dot_general(a, b, dims, preferred_element_type=F32)


def params(**kw):
    return pltpu.CompilerParams(vmem_limit_bytes=VMEM_LIMIT, **kw)


def anywhere():
    return pl.BlockSpec(memory_space=pl.ANY)


def in_vmem():
    return pl.BlockSpec(memory_space=pltpu.VMEM)


def place():
    dp, x = lax.axis_index("dp"), lax.axis_index("mp")
    return x, dp // 4, lax.rem(dp // 2, 2), lax.rem(dp, 2)


def device(x, z, y, c):
    return ((z * 2 + y) * 2 + c, x)


def neighbours():
    x, z, y, c = place()
    lines = [device(x, lax.rem(z + k, 4), y, c) for k in (1, 2, 3)]
    return lines, device(1 - x, z, y, c), device(x, z, 1 - y, c), device(x, z, y, 1 - c)


def greet():
    lines, over_x, over_y, sibling = neighbours()
    barrier = pltpu.get_barrier_semaphore()
    for other in (*lines, over_x, over_y, sibling):
        pl.semaphore_signal(barrier, inc=1, device_id=other, device_id_type=MESH)
    pl.semaphore_wait(barrier, 6)


class Wires:
    def __init__(self, send_sem, recv_sem):
        self.send_sem, self.recv_sem = send_sem, recv_sem
        self.started = []

    def copy(self, slot, src, dst, other):
        return pltpu.make_async_remote_copy(
            src_ref=src,
            dst_ref=dst,
            send_sem=self.send_sem.at[slot],
            recv_sem=self.recv_sem.at[slot],
            device_id=other,
            device_id_type=MESH,
        )

    def start(self, slot, src, dst, other):
        self.copy(slot, src, dst, other).start()
        self.started.append((slot, src))

    def send(self, slot, whole, part, other):
        self.copy(slot, whole.at[part], whole.at[part], other).start()
        self.started.append((slot, whole, part))

    def arrive(self, slot, dst):
        x, z, y, c = place()
        self.copy(slot, dst, dst, device(x, z, y, 1 - c)).wait_recv()

    def sent(self, slot, src):
        x, z, y, c = place()
        self.copy(slot, src, src, device(x, z, y, 1 - c)).wait_send()

    def drain(self):
        for slot, src, *part in self.started:
            self.sent(slot, src.at[part[0]] if part else src)


ALL = slice(None)


def first_kernel(*refs):
    (sa, sm, se, ss, patch_ref, mask_ref, token_ref, vec_ref) = refs[:8]
    (wa_out, wm, we, ws, q_ref, k_ref, v_ref, a1_ref, other_ref) = refs[8:17]
    wa, landing, own_sem, send_sem, recv_sem = refs[17:]
    x, z, y, c = place()
    lines, over_x, over_y, sibling = neighbours()
    wires = Wires(send_sem, recv_sem)
    rows = a1_ref.shape[0]
    cut = rows // 32 * 16
    halves = (pl.ds(0, cut), pl.ds(cut, rows - cut))
    greet()

    def back(k):
        return lax.rem(z + 4 - k, 4)

    own = [pltpu.make_async_copy(sa, wa.at[x, z, y, c], own_sem.at[0])]
    for n, (shard, whole) in enumerate(((sm, wm), (se, we), (ss, ws))):
        own.append(pltpu.make_async_copy(shard, whole.at[x, z, y, c], own_sem.at[n + 1]))
    for copy in own:
        copy.start()
    for k in (1, 2, 3):
        wires.start(k - 1, sa, wa.at[x, z, y, c], lines[k - 1])
    wires.start(3, sa, wa.at[x, z, y, c], over_x)
    wires.start(7, sa, wa.at[x, z, y, c], over_y)

    tubes = jnp.where(mask_ref[...] > 0, token_ref[...], patch_ref[...].astype(F32))
    centred = tubes - mean_rows(tubes)
    scale = lax.rsqrt(mean_rows(centred * centred) + 1e-6)
    a1_ref[...] = (centred * scale * vec_ref[0:1] + vec_ref[1:2]).astype(BF)
    wires.start(19, a1_ref.at[halves[0]], landing.at[halves[0]], over_x)

    for k in (1, 2, 3):
        part = wa.at[x, back(k), y, c]
        wires.arrive(k - 1, part)
        wires.start(3 + k, part, part, over_x)
        wires.start(7 + k, part, part, over_y)
    wires.start(20, a1_ref.at[halves[1]], landing.at[halves[1]], over_x)
    for copy in own:
        copy.wait()
    line = wa.at[x, ALL, y, c]
    wires.start(15, line, line, sibling)
    others = ((sm, wm), (se, we), (ss, ws))
    for n, (shard, whole) in enumerate(others):
        for k in (1, 2, 3):
            wires.start(21 + 3 * n + k - 1, shard, whole.at[x, z, y, c], lines[k - 1])
    for k in range(4):
        part = wa.at[1 - x, back(k), y, c]
        wires.arrive(3 + k, part)
        wires.start(11 + k, part, part, over_y)
    for n in range(2):
        shard, whole = others[n]
        wires.start(30 + 4 * n, shard, whole.at[x, z, y, c], over_y)
    line = wa.at[1 - x, ALL, y, c]
    wires.start(16, line, line, sibling)
    for k in range(4):
        wires.arrive(7 + k, wa.at[x, back(k), 1 - y, c])
    line = wa.at[x, ALL, 1 - y, c]
    wires.start(17, line, line, sibling)

    def pass_on(n):
        whole = others[n][1]
        for k in (1, 2, 3):
            part = whole.at[x, back(k), y, c]
            wires.arrive(21 + 3 * n + k - 1, part)
            wires.start(30 + 4 * n + k, part, part, over_y)

    pass_on(0)
    for k in range(4):
        wires.arrive(11 + k, wa.at[1 - x, back(k), 1 - y, c])
    line = wa.at[1 - x, ALL, 1 - y, c]
    wires.start(18, line, line, sibling)
    for n, (i, j) in enumerate(((x, y), (1 - x, y), (x, 1 - y), (1 - x, 1 - y))):
        wires.arrive(15 + n, wa.at[i, ALL, j, 1 - c])
    out_copy = pltpu.make_async_copy(wa, wa_out, own_sem.at[0])
    out_copy.start()

    width = wa.shape[-1] // 3
    depth = a1_ref.shape[1]

    def weight(h, n):
        return wa[h, :, :, :, :, n * width : (n + 1) * width].reshape(depth, width)

    def keys_values(h, source, span):
        k_ref[h, span] = dot(source, weight(h, 1)).astype(BF)
        values = dot(source, weight(h, 2)) + vec_ref[3:4, h * width : (h + 1) * width]
        v_ref[h, span] = values.astype(BF)

    for h in range(2):
        queries = dot(a1_ref[...], weight(h, 0)) + vec_ref[2:3, h * width : (h + 1) * width]
        q_ref[h] = (queries.astype(BF).astype(F32) * HD**-0.5).astype(BF)
        keys_values(h, a1_ref[...], pl.ds(0, rows))
    pass_on(1)
    for n in range(2):
        wires.arrive(19 + n, landing.at[halves[n]])
        part = landing[halves[n]]
        other_ref[halves[n]] = part
        span = pl.ds(rows + (cut if n else 0), part.shape[0])
        for h in range(2):
            keys_values(h, part, span)
    for n in range(2):
        for k in range(4):
            wires.arrive(30 + 4 * n + k, others[n][1].at[x, back(k), 1 - y, c])
    for k in (1, 2, 3):
        wires.arrive(27 + k - 1, ws.at[x, back(k), y, c])
    out_copy.wait()
    wires.drain()


def first(shards, patches, mask, token, vectors):
    rows, width = patches.shape
    half = width // 2
    gathered = [(2, 4, 2, 2, *s.shape) for s in shards]
    wholes = [jax.ShapeDtypeStruct(g, BF) for g in gathered]
    keys = jax.ShapeDtypeStruct((2, 2 * rows, half), BF)
    flat = jax.ShapeDtypeStruct((rows, width), BF)
    return pl.pallas_call(
        first_kernel,
        out_shape=[*wholes, jax.ShapeDtypeStruct((2, rows, half), BF), keys, keys, flat, flat],
        in_specs=[anywhere()] * 4 + [in_vmem()] * 4,
        out_specs=[anywhere()] * 4 + [in_vmem()] * 5,
        scratch_shapes=[
            pltpu.VMEM(gathered[0], BF),
            pltpu.VMEM((rows, width), BF),
            pltpu.SemaphoreType.DMA((4,)),
            pltpu.SemaphoreType.DMA((38,)),
            pltpu.SemaphoreType.DMA((38,)),
        ],
        compiler_params=params(collective_id=0, has_side_effects=True),
        name="first",
    )(*shards, patches, mask, token, vectors)


def add_into(dst, other):
    dst[...] = (dst[...].astype(F32) + other[...].astype(F32)).astype(BF)


def project_kernel(mine_ref, other_ref, w_ref, bias_ref, q_ref, k_ref, v_ref):
    rows = mine_ref.shape[0]
    half = w_ref.shape[2] // 3
    for h in range(2):
        cols = slice(h * half, (h + 1) * half)
        queries = dot(mine_ref[...], w_ref[h, :, :half]) + bias_ref[0:1, cols]
        q_ref[h] = (queries.astype(BF).astype(F32) * HD**-0.5).astype(BF)
        for part, ref in ((0, mine_ref), (1, other_ref)):
            span = slice(part * rows, (part + 1) * rows)
            k_ref[h, span] = dot(ref[...], w_ref[h, :, half : 2 * half]).astype(BF)
            v_ref[h, span] = (dot(ref[...], w_ref[h, :, 2 * half :]) + bias_ref[1:2, cols]).astype(BF)


def project(mine, other, weight, bias):
    rows, width = mine.shape
    keys = jax.ShapeDtypeStruct((2, 2 * rows, width // 2), BF)
    return pl.pallas_call(
        project_kernel,
        out_shape=[jax.ShapeDtypeStruct((2, rows, width // 2), BF), keys, keys],
        in_specs=[in_vmem()] * 4,
        out_specs=[in_vmem()] * 3,
        compiler_params=params(),
        name="project",
    )(mine, other, weight, bias)


def half_lanes():
    lane = lax.broadcasted_iota(jnp.int32, (1, PAIR), 1)
    return lane < HD, lane >= HD


def attend_head(h, q, k, v, p_ref):
    s = dot(jnp.where(half_lanes()[h], q, jnp.zeros_like(q)), k, NT)
    top = jnp.max(s, axis=-1, keepdims=True)
    e = jnp.exp2(s * LOG2E - top * LOG2E)
    total = jnp.sum(e, axis=-1, keepdims=True)
    p = (e * (1.0 / total)).astype(BF)
    p_ref[h] = p
    return dot(p, v)


def attend_plain_kernel(q_ref, k_ref, v_ref, o_ref, low_ref, p_ref):
    q, k, v = q_ref[0], k_ref[0], v_ref[0]
    o = jnp.where(half_lanes()[0], *(attend_head(h, q, k, v, p_ref) for h in range(2)))
    o_ref[0] = o
    low_ref[0] = o.astype(BF)


def attend_kernel(*refs):
    q_ref, k_ref, v_ref = refs[:3]
    o_ref, low_ref, p_ref, wm, we, ws, send_sem, recv_sem = refs[6:]
    i = pl.program_id(0)
    x, z, y, c = place()
    lines, over_x, over_y, sibling = neighbours()
    wires = Wires(send_sem, recv_sem)
    here, side, flank, across = (x, ALL, y, c), (1 - x, ALL, y, c), (x, ALL, 1 - y, c), (1 - x, ALL, 1 - y, c)

    send = wires.send

    @pl.when(i == 0)
    def _():
        greet()
        send(0, wm, here, over_x)
        send(1, we, here, over_x)
        send(2, ws, here, over_y)
        send(3, ws, here, over_x)
        send(4, wm, flank, over_x)
        send(5, wm, here, sibling)
        send(6, wm, flank, sibling)
        send(7, we, here, sibling)
        send(8, we, flank, sibling)
        send(9, ws, here, sibling)

    @pl.when(i == 2)
    def _():
        wires.arrive(0, wm.at[side])
        send(10, wm, side, sibling)
        wires.arrive(1, we.at[side])
        send(11, we, side, over_y)
        send(12, we, side, sibling)

    @pl.when(i == 4)
    def _():
        wires.arrive(3, ws.at[side])
        send(13, ws, side, over_y)
        send(14, ws, side, sibling)
        wires.arrive(2, ws.at[flank])
        send(15, ws, flank, sibling)
        wires.arrive(4, wm.at[across])
        send(16, wm, across, sibling)

    q, k, v = q_ref[0], k_ref[0], v_ref[0]
    o = jnp.where(half_lanes()[0], *(attend_head(h, q, k, v, p_ref) for h in range(2)))
    o_ref[0] = o
    low_ref[0] = o.astype(BF)

    @pl.when(i == pl.num_programs(0) - 1)
    def _():
        wires.arrive(11, we.at[across])
        send(17, we, across, sibling)
        wires.arrive(13, ws.at[across])
        send(18, ws, across, sibling)
        for slot, whole, (a, b) in (
            (5, wm, (x, y)),
            (6, wm, (x, 1 - y)),
            (7, we, (x, y)),
            (8, we, (x, 1 - y)),
            (9, ws, (x, y)),
            (10, wm, (1 - x, y)),
            (12, we, (1 - x, y)),
            (14, ws, (1 - x, y)),
            (15, ws, (x, 1 - y)),
            (16, wm, (1 - x, 1 - y)),
            (17, we, (1 - x, 1 - y)),
            (18, ws, (1 - x, 1 - y)),
        ):
            wires.arrive(slot, whole.at[a, ALL, b, 1 - c])
        wires.drain()


def attend(q, k, v, wholes):
    _, rows, half = q.shape
    keys = k.shape[1]
    per = half // PAIR
    of_q = pl.BlockSpec((1, rows, PAIR), lambda i: (i // per, 0, lax.rem(i, per)))
    of_k = pl.BlockSpec((1, keys, PAIR), lambda i: (i // per, 0, lax.rem(i, per)))
    shapes = [
        jax.ShapeDtypeStruct(q.shape, F32),
        jax.ShapeDtypeStruct(q.shape, BF),
        jax.ShapeDtypeStruct((4 * per, rows, keys), BF),
    ]
    of_p = pl.BlockSpec((2, rows, keys), lambda i: (i, 0, 0))
    common = dict(grid=(2 * per,), name="attend")
    if not wholes:
        return pl.pallas_call(
            attend_plain_kernel,
            in_specs=[of_q, of_k, of_k],
            out_specs=[of_q, of_q, of_p],
            out_shape=shapes,
            compiler_params=params(),
            **common,
        )(q, k, v)
    return pl.pallas_call(
        attend_kernel,
        in_specs=[of_q, of_k, of_k, *[anywhere()] * 3],
        out_specs=[of_q, of_q, of_p, *[anywhere()] * 3],
        out_shape=[*shapes, *[jax.ShapeDtypeStruct(w.shape, BF) for w in wholes]],
        input_output_aliases={3: 3, 4: 4, 5: 5},
        scratch_shapes=[pltpu.SemaphoreType.DMA((19,)), pltpu.SemaphoreType.DMA((19,))],
        compiler_params=params(collective_id=2, has_side_effects=True),
        **common,
    )(q, k, v, *wholes)


def attend_back_pair(q_ref, k_ref, v_ref, do_ref, o_ref, p_ref, dq_ref, dk_ref, dv_ref):
    sides = half_lanes()
    q, k, v, do = q_ref[0], k_ref[0], v_ref[0], do_ref[0]
    prod = do.astype(F32) * o_ref[0]
    outs, grad_k, grad_v = [], None, None
    for h in range(2):
        do_h = jnp.where(sides[h], do, jnp.zeros_like(do))
        q_h = jnp.where(sides[h], q, jnp.zeros_like(q))
        grad_p = dot(do_h, v, NT)
        row_dot = jnp.sum(jnp.where(sides[h], prod, 0.0), axis=-1, keepdims=True)
        p = p_ref[h]
        ds = (p.astype(F32) * (grad_p - row_dot)).astype(BF)
        outs.append(dot(ds, k))
        more_k, more_v = dot(ds, q_h, TN), dot(p, do_h, TN)
        grad_k = more_k if grad_k is None else grad_k + more_k
        grad_v = more_v if grad_v is None else grad_v + more_v
    dq_ref[0] = (jnp.where(sides[0], outs[0], outs[1]) * HD**-0.5).astype(BF)
    dk_ref[0] = grad_k.astype(BF)
    dv_ref[0] = grad_v.astype(BF)


def attend_back_kernel(*refs):
    ins, grads = refs[:6], refs[6:9]
    outs, totals = refs[9:12], refs[12:15]
    refs = refs[15:]
    mine, sib, diag, side = refs[:3], refs[3:6], refs[6:9], refs[9:12]
    own_sem, send_sem, recv_sem = refs[12:]
    i = pl.program_id(0)
    x, z, y, c = place()
    lines, over_x, over_y, sibling = neighbours()
    wires = Wires(send_sem, recv_sem)

    def keep(n):
        return pltpu.make_async_copy(grads[n].at[:, :, :, c], mine[n], own_sem.at[n])

    def after_sibling(n):
        keep(n).wait()
        wires.arrive(5 * n, sib[n])

        def sweep(m, _):
            part = (m // 8, lax.rem(m // 2, 4), lax.rem(m, 2))
            add_into(mine[n].at[part], sib[n].at[part])
            return 0

        lax.fori_loop(0, 16, sweep, 0)
        wires.start(5 * n + 1, mine[n].at[1 - x, pl.ds(0, 2), 1 - y], diag[n].at[0], over_x)
        wires.start(5 * n + 2, mine[n].at[1 - x, pl.ds(2, 2), 1 - y], diag[n].at[1], over_y)

    def after_diagonal(n):
        wires.arrive(5 * n + 1, diag[n].at[0])
        wires.arrive(5 * n + 2, diag[n].at[1])

        def sweep(m, _):
            add_into(mine[n].at[x, m, 1 - y], diag[n].at[0, m])
            add_into(mine[n].at[1 - x, 2 + m, y], diag[n].at[1, m])
            return 0

        lax.fori_loop(0, 2, sweep, 0)
        wires.start(5 * n + 3, mine[n].at[1 - x, :, y], side[n].at[0], over_x)
        wires.start(5 * n + 4, mine[n].at[x, :, 1 - y], side[n].at[1], over_y)

    def after_sides(n):
        wires.arrive(5 * n + 3, side[n].at[0])
        wires.arrive(5 * n + 4, side[n].at[1])

        def sweep(m, _):
            both = side[n][0, m].astype(F32) + side[n][1, m].astype(F32)
            totals[n][m] = (mine[n][x, m, y].astype(F32) + both).astype(BF)
            return 0

        lax.fori_loop(0, 4, sweep, 0)

    @pl.when(i == 0)
    def _():
        greet()
        for n in range(3):
            keep(n).start()
            wires.start(5 * n, grads[n].at[:, :, :, 1 - c], sib[n], sibling)

    @pl.when(i == 1)
    def _():
        after_sibling(0)

    @pl.when(i == 2)
    def _():
        after_sibling(1)
        after_diagonal(0)
        after_sibling(2)

    @pl.when(i == 4)
    def _():
        after_diagonal(1)
        after_diagonal(2)

    attend_back_pair(*ins, *outs)

    @pl.when(i == pl.num_programs(0) - 1)
    def _():
        for n in range(3):
            after_sides(n)
        for n in range(3):
            wires.sent(5 * n, grads[n].at[:, :, :, 1 - c])
            wires.sent(5 * n + 1, mine[n].at[1 - x, pl.ds(0, 2), 1 - y])
            wires.sent(5 * n + 2, mine[n].at[1 - x, pl.ds(2, 2), 1 - y])
            wires.sent(5 * n + 3, mine[n].at[1 - x, :, y])
            wires.sent(5 * n + 4, mine[n].at[x, :, 1 - y])


def attend_back(q, k, v, do, o, p, grads, own_rows):
    _, rows, half = q.shape
    keys = k.shape[1]
    per = half // PAIR
    of_q = pl.BlockSpec((1, rows, PAIR), lambda i: (i // per, 0, lax.rem(i, per)))
    of_k = pl.BlockSpec((1, keys, PAIR), lambda i: (i // per, 0, lax.rem(i, per)))
    of_p = pl.BlockSpec((2, rows, keys), lambda i: (i, 0, 0))
    shapes = [
        jax.ShapeDtypeStruct(q.shape, BF),
        jax.ShapeDtypeStruct(k.shape, BF),
        jax.ShapeDtypeStruct(k.shape, BF),
    ]
    common = dict(grid=(2 * per,), name="attend_back")
    if not grads:
        return pl.pallas_call(
            attend_back_pair,
            in_specs=[of_q, of_k, of_k, of_q, of_q, of_p],
            out_specs=[of_q, of_k, of_k],
            out_shape=shapes,
            compiler_params=params(),
            **common,
        )(q, k, v, do, o, p)
    widths = [g.shape[-1] for g in grads]
    lined = [(4, own_rows, w) for w in widths]
    return pl.pallas_call(
        attend_back_kernel,
        in_specs=[of_q, of_k, of_k, of_q, of_q, of_p, *[anywhere()] * 3],
        out_specs=[of_q, of_k, of_k, *[pl.BlockSpec(t, lambda i: (0, 0, 0)) for t in lined]],
        out_shape=[*shapes, *[jax.ShapeDtypeStruct(t, BF) for t in lined]],
        scratch_shapes=[
            *[pltpu.VMEM((2, 4, 2, own_rows, w), BF) for w in widths],
            *[pltpu.VMEM((2, 4, 2, own_rows, w), BF) for w in widths],
            *[pltpu.VMEM((2, 2, own_rows, w), BF) for w in widths],
            *[pltpu.VMEM((2, 4, own_rows, w), BF) for w in widths],
            pltpu.SemaphoreType.DMA((3,)),
            pltpu.SemaphoreType.DMA((15,)),
            pltpu.SemaphoreType.DMA((15,)),
        ],
        compiler_params=params(collective_id=3, has_side_effects=True),
        **common,
    )(q, k, v, do, o, p, *[g.reshape(2, 4, 2, 2, own_rows, w) for g, w in zip(grads, widths)])


def normal_parts(h):
    z = jnp.abs(h) * 0.7071067811865476
    t = 1.0 / (1.0 + 0.3275911 * z)
    bell = jnp.exp(-z * z)
    poly = t * (
        0.254829592
        + t * (-0.284496736 + t * (1.421413741 + t * (-1.453152027 + t * 1.061405429)))
    )
    tail = 0.5 * poly * bell
    return jnp.where(h < 0, tail, 1.0 - tail), bell * 0.3989422804014327


def mean_rows(values):
    return jnp.mean(values, axis=-1, keepdims=True)


def middle_kernel(
    patch_ref,
    mask_ref,
    token_ref,
    o_ref,
    dy_ref,
    vec_ref,
    bu_ref,
    wm_ref,
    we_ref,
    ws_ref,
    out_ref,
    dx1_ref,
    do_ref,
    gm_ref,
    ge_ref,
    gs_ref,
    gu_ref,
    gv_ref,
    x1_ref,
    a2_ref,
    acc_ref,
    da2_ref,
):
    i = pl.program_id(0)

    @pl.when(i == 0)
    def _():
        x1 = jnp.where(mask_ref[...] > 0, token_ref[...], patch_ref[...].astype(F32)) + vec_ref[4:5]
        for h in range(2):
            x1 = x1 + dot(o_ref[h], wm_ref[h], NT)
        x1_ref[...] = x1
        centred = x1 - mean_rows(x1)
        scale = lax.rsqrt(mean_rows(centred * centred) + 1e-6)
        a2_ref[...] = (centred * scale * vec_ref[5:6] + vec_ref[6:7]).astype(BF)
        acc_ref[...] = x1 + vec_ref[11:12]
        da2_ref[...] = jnp.zeros_like(da2_ref)

    a2, dy = a2_ref[...], dy_ref[...]
    we, ws = we_ref[0], ws_ref[0]
    hidden = dot(a2, we) + bu_ref[...]
    cdf, density = normal_parts(hidden)
    u = (hidden * cdf).astype(BF)
    du = dot(dy, ws)
    dh = (du * (cdf + hidden * density)).astype(BF)
    acc_ref[...] += dot(u, ws, NT)
    da2_ref[...] += dot(dh, we, NT)
    gs_ref[0] = dot(dy, u, TN).astype(BF)
    ge_ref[0] = dot(a2, dh, TN).astype(BF)
    gu_ref[...] = jnp.sum(dh.astype(F32), axis=0, keepdims=True)

    @pl.when(i == pl.num_programs(0) - 1)
    def _():
        out_ref[...] = acc_ref[...].astype(BF)
        x1 = x1_ref[...]
        top = dy_ref[...].astype(F32)
        centred = x1 - mean_rows(x1)
        scale = lax.rsqrt(mean_rows(centred * centred) + 1e-6)
        xh = centred * scale
        da2 = da2_ref[...]
        e = da2 * vec_ref[5:6]
        dx1 = top + scale * (e - mean_rows(e) - xh * mean_rows(e * xh))
        dx1_ref[...] = dx1
        dxb = dx1.astype(BF)
        for h in range(2):
            do_ref[h] = dot(dxb, wm_ref[h]).astype(BF)
            gm_ref[h] = dot(dxb, o_ref[h], TN).astype(BF)
        gv_ref[0:1] = jnp.sum(dxb.astype(F32), axis=0, keepdims=True)
        gv_ref[1:2] = jnp.sum(da2 * xh, axis=0, keepdims=True)
        gv_ref[2:3] = jnp.sum(da2, axis=0, keepdims=True)
        gv_ref[3:4] = jnp.sum(top, axis=0, keepdims=True)
        gv_ref[4:] = jnp.zeros((4, gv_ref.shape[1]), F32)


def middle(patches, mask, token, o, dy, vectors, wm, we, ws):
    rows, width = patches.shape
    hidden = we.shape[2]
    block = 512
    per = hidden // block
    steps = 2 * per
    of_w = pl.BlockSpec((1, width, block), lambda i: (i // per, 0, lax.rem(i, per)))
    of_u = pl.BlockSpec((1, block), lambda i: (0, i))

    def whole(shape):
        return pl.BlockSpec(shape, lambda i: (0,) * len(shape))

    return pl.pallas_call(
        middle_kernel,
        grid=(steps,),
        in_specs=[
            whole((rows, width)),
            whole((rows, 1)),
            whole((1, width)),
            whole(o.shape),
            whole((rows, width)),
            whole(vectors.shape),
            of_u,
            whole(wm.shape),
            of_w,
            of_w,
        ],
        out_specs=[
            whole((rows, width)),
            whole((rows, width)),
            whole(o.shape),
            whole(wm.shape),
            of_w,
            of_w,
            of_u,
            whole((8, width)),
        ],
        out_shape=[
            jax.ShapeDtypeStruct((rows, width), BF),
            jax.ShapeDtypeStruct((rows, width), F32),
            jax.ShapeDtypeStruct(o.shape, BF),
            jax.ShapeDtypeStruct(wm.shape, BF),
            jax.ShapeDtypeStruct(we.shape, BF),
            jax.ShapeDtypeStruct(ws.shape, BF),
            jax.ShapeDtypeStruct((1, 2 * hidden), F32),
            jax.ShapeDtypeStruct((8, width), F32),
        ],
        scratch_shapes=[
            pltpu.VMEM((rows, width), F32),
            pltpu.VMEM((rows, width), BF),
            pltpu.VMEM((rows, width), F32),
            pltpu.VMEM((rows, width), F32),
        ],
        compiler_params=params(),
        name="middle",
    )(patches, mask, token, o, dy, vectors, vectors[7:11].reshape(1, -1), wm, we, ws)


def unproject_kernel(
    mine_ref, other_ref, dq_ref, dk_ref, dv_ref, w_ref, da_ref, send_ref, gw_ref, gv_ref
):
    rows = mine_ref.shape[0]
    half = w_ref.shape[2] // 3
    da, send = None, None
    gv_ref[...] = jnp.zeros_like(gv_ref)
    for h in range(2):
        cols = slice(h * half, (h + 1) * half)
        dq, dk, dv = dq_ref[h], dk_ref[h], dv_ref[h]
        wq, wk, wv = (w_ref[h, :, n * half : (n + 1) * half] for n in range(3))
        mine = dot(dq, wq, NT) + dot(dk[:rows], wk, NT) + dot(dv[:rows], wv, NT)
        other = dot(dk[rows:], wk, NT) + dot(dv[rows:], wv, NT)
        da = mine if da is None else da + mine
        send = other if send is None else send + other
        a, b = mine_ref[...], other_ref[...]
        gw_ref[h, :, :half] = dot(a, dq, TN).astype(BF)
        gw_ref[h, :, half : 2 * half] = (dot(a, dk[:rows], TN) + dot(b, dk[rows:], TN)).astype(BF)
        gw_ref[h, :, 2 * half :] = (dot(a, dv[:rows], TN) + dot(b, dv[rows:], TN)).astype(BF)
        gv_ref[0:1, cols] = jnp.sum(dq.astype(F32), axis=0, keepdims=True)
        gv_ref[1:2, cols] = jnp.sum(dv.astype(F32), axis=0, keepdims=True)
    da_ref[...] = da
    send_ref[...] = send.astype(BF)


def unproject(mine, other, dq, dk, dv, weight):
    rows, width = mine.shape
    return pl.pallas_call(
        unproject_kernel,
        out_shape=[
            jax.ShapeDtypeStruct((rows, width), F32),
            jax.ShapeDtypeStruct((rows, width), BF),
            jax.ShapeDtypeStruct(weight.shape, BF),
            jax.ShapeDtypeStruct((8, width), F32),
        ],
        in_specs=[in_vmem()] * 6,
        out_specs=[in_vmem()] * 4,
        compiler_params=params(),
        name="unproject",
    )(mine, other, dq, dk, dv, weight)


def last_kernel(*refs):
    a_ref, b_ref, dq_ref, dk_ref, dv_ref, w_ref, patch_ref, mask_ref, token_ref, vec_ref, dx1_ref = refs[:11]
    lined = refs[11:14]
    pg_ref, gv_ref, *totals = refs[14:20]
    refs = refs[20:]
    gw, sib, diag, side, da_ref, send_ref, landing = refs[:7]
    far = refs[7:11]
    send_sem, recv_sem = refs[11:]
    x, z, y, c = place()
    lines, over_x, over_y, sibling = neighbours()
    wires = Wires(send_sem, recv_sem)
    rows, depth = a_ref.shape
    half = w_ref.shape[2] // 3
    cut = rows // 32 * 16
    spans = (pl.ds(0, cut), pl.ds(cut, rows - cut))
    greet()

    def along(n, source):
        for k in (1, 2, 3):
            wires.start(3 * n + k - 1, source(lax.rem(z + k, 4)), far[n].at[k - 1], lines[k - 1])

    def settle(n, own):
        total = own.astype(F32)
        for k in range(3):
            wires.arrive(3 * n + k, far[n].at[k])
            total = total + far[n][k].astype(F32)
        totals[n][...] = total

    for n in range(3):
        along(n + 1, lambda t, n=n: lined[n].at[t])
    w = [[w_ref[h, :, n * half : (n + 1) * half] for n in range(3)] for h in range(2)]
    for n, (start, size) in enumerate(((rows, cut), (rows + cut, rows - cut))):
        span = pl.ds(start, size)
        send = None
        for h in range(2):
            part = dot(dk_ref[h, span], w[h][1], NT) + dot(dv_ref[h, span], w[h][2], NT)
            send = part if send is None else send + part
        send_ref[spans[n]] = send.astype(BF)
        wires.start(12 + n, send_ref.at[spans[n]], landing.at[spans[n]], over_x)
    a, b = a_ref[...], b_ref[...]
    own, other = pl.ds(0, rows), pl.ds(rows, rows)
    for h in range(2):
        for n in range(3):
            if n == 0:
                grad = dot(a, dq_ref[h], TN)
            else:
                ref = dk_ref if n == 1 else dv_ref
                grad = dot(a, ref[h, own], TN) + dot(b, ref[h, other], TN)
            gw[h, :, :, :, :, n * half : (n + 1) * half] = grad.astype(BF).reshape(4, 2, 2, -1, half)
        wires.start(14 + h, gw.at[h, :, :, 1 - c], sib.at[h], sibling)
    da = None
    for h in range(2):
        part = dot(dq_ref[h], w[h][0], NT) + dot(dk_ref[h, own], w[h][1], NT) + dot(dv_ref[h, own], w[h][2], NT)
        da = part if da is None else da + part
    da_ref[...] = da
    for h in range(2):
        wires.arrive(14 + h, sib.at[h])

    def sweep(m, _):
        i, j, k = m // 8, lax.rem(m // 2, 4), lax.rem(m, 2)
        add_into(gw.at[i, j, k, c], sib.at[i, j, k])
        return 0

    lax.fori_loop(0, 16, sweep, 0)
    wires.start(16, gw.at[1 - x, :, 1 - y, c], diag, over_y)
    wires.start(18, gw.at[x, :, 1 - y, c], side.at[1], over_y)
    gv_ref[...] = jnp.zeros_like(gv_ref)
    for h in range(2):
        cols = slice(h * half, (h + 1) * half)
        gv_ref[2:3, cols] = jnp.sum(dq_ref[h].astype(F32), axis=0, keepdims=True)
        gv_ref[3:4, cols] = jnp.sum(dv_ref[h].astype(F32), axis=0, keepdims=True)
    tubes = jnp.where(mask_ref[...] > 0, token_ref[...], patch_ref[...].astype(F32))
    centred = tubes - mean_rows(tubes)
    scale = lax.rsqrt(mean_rows(centred * centred) + 1e-6)
    xh = centred * scale
    wires.arrive(16, diag)

    def sweep_two(m, _):
        add_into(gw.at[1 - x, m, y, c], diag.at[m])
        return 0

    lax.fori_loop(0, 4, sweep_two, 0)
    wires.start(17, gw.at[1 - x, :, y, c], side.at[0], over_x)
    for n in range(3):
        settle(n + 1, lined[n][z])
    for n in range(2):
        wires.arrive(12 + n, landing.at[spans[n]])
    da = da_ref[...] + landing[...].astype(F32)
    gv_ref[0:1] = jnp.sum(da * xh, axis=0, keepdims=True)
    gv_ref[1:2] = jnp.sum(da, axis=0, keepdims=True)
    e = da * vec_ref[0:1]
    dx = dx1_ref[...] + scale * (e - mean_rows(e) - xh * mean_rows(e * xh))
    masked = mask_ref[...] > 0
    pg_ref[...] = jnp.where(masked, 0.0, dx).astype(BF)
    gv_ref[4:5] = jnp.sum(jnp.where(masked, dx, 0.0), axis=0, keepdims=True)
    wires.arrive(17, side.at[0])
    wires.arrive(18, side.at[1])

    def sweep_three(m, _):
        both = side[0, m].astype(F32) + side[1, m].astype(F32)
        part = gw.at[x, m, y, c]
        part[...] = (part[...].astype(F32) + both).astype(BF)
        return 0

    lax.fori_loop(0, 4, sweep_three, 0)
    along(0, lambda t: gw.at[x, t, y, c])
    settle(0, gw[x, z, y, c])
    wires.drain()


def last(a, b, dq, dk, dv, wa, patches, mask, token, vectors, dx1, lined):
    rows, width = a.shape
    own_rows = lined[0].shape[1]
    widths = [wa.shape[2], *[t.shape[2] for t in lined]]
    w = widths[0]
    return pl.pallas_call(
        last_kernel,
        out_shape=[
            jax.ShapeDtypeStruct((rows, width), BF),
            jax.ShapeDtypeStruct((8, width), F32),
            *[jax.ShapeDtypeStruct((own_rows, n), F32) for n in widths],
        ],
        in_specs=[in_vmem()] * 14,
        out_specs=[in_vmem()] * 6,
        scratch_shapes=[
            pltpu.VMEM((2, 4, 2, 2, own_rows, w), BF),
            pltpu.VMEM((2, 4, 2, own_rows, w), BF),
            pltpu.VMEM((4, own_rows, w), BF),
            pltpu.VMEM((2, 4, own_rows, w), BF),
            pltpu.VMEM((rows, width), F32),
            pltpu.VMEM((rows, width), BF),
            pltpu.VMEM((rows, width), BF),
            *[pltpu.VMEM((3, own_rows, n), BF) for n in widths],
            pltpu.SemaphoreType.DMA((19,)),
            pltpu.SemaphoreType.DMA((19,)),
        ],
        compiler_params=params(collective_id=1, has_side_effects=True),
        name="last",
    )(a, b, dq, dk, dv, wa, patches, mask, token, vectors, dx1, *lined)


def lamb_kernel(*refs):
    masters, firsts, seconds, totals = (refs[4 * n : 4 * n + 4] for n in range(4))
    head_ref, tail_ref, hidden_ref, vec_ref, vfirst_ref, vsecond_ref = refs[16:22]
    moments, squares, weights, copies = (refs[22 + 4 * n : 26 + 4 * n] for n in range(4))
    token_ref, bias_ref, vm_ref, vs_ref, vw_ref, norm_ref = refs[38:44]
    updates = refs[44:48]
    held, came, final, send_sem, recv_sem = refs[48:]
    x, z, y, c = place()
    lines, over_x, over_y, sibling = neighbours()
    wires = Wires(send_sem, recv_sem)
    greet()
    correct = 1.0 - 0.5**STEP

    def terms(weight, moment, square, grad):
        moment_new = 0.5 * moment + 0.5 * grad
        square_new = 0.5 * square + 0.5 * grad * grad
        update = moment_new / correct / (jnp.sqrt(square_new / correct) + 1e-06) + 0.01 * weight
        return moment_new, square_new, update

    def whole_sum(values):
        return jnp.sum(jnp.sum(values, axis=0, keepdims=True), axis=1, keepdims=True)

    lane = lax.broadcasted_iota(jnp.int32, (1, vec_ref.shape[1]), 1)
    row = jnp.zeros((1, vec_ref.shape[1]), F32)
    for n in range(4):
        weight = masters[n][...]
        moment, square, update = terms(weight, firsts[n][...], seconds[n][...], totals[n][...])
        moments[n][...] = moment
        squares[n][...] = square
        updates[n][...] = update
        row = jnp.where(lane == 2 * n, whole_sum(weight * weight), row)
        row = jnp.where(lane == 2 * n + 1, whole_sum(update * update), row)
    held[0, 0:4] = head_ref[0:4]
    held[0, 4:7] = tail_ref[0:3]
    held[0, 7:11] = hidden_ref[...]
    held[0, 11:12] = tail_ref[3:4]
    held[0, 12:13] = head_ref[4:5]
    held[0, 13:14] = row
    held[0, 14:] = jnp.zeros((2, vec_ref.shape[1]), F32)
    for n, other in enumerate((sibling, over_x, over_y)):
        wires.start(n, held.at[n], came.at[n], other)
        wires.arrive(n, came.at[n])
        both = held[n] + came[n]
        if n < 2:
            held[n + 1] = both
        else:
            final[z] = both
    for k in (1, 2, 3):
        wires.start(2 + k, final.at[z], final.at[z], lines[k - 1])
    for k in (1, 2, 3):
        wires.arrive(2 + k, final.at[lax.rem(z + 4 - k, 4)])
    total = final[0] + final[1] + final[2] + final[3]
    norms = jnp.sqrt(total[13:14])
    for n in range(4):
        size, length = norms[:, 2 * n : 2 * n + 1], norms[:, 2 * n + 1 : 2 * n + 2]
        norm_ref[n : n + 1, 0:1] = size
        norm_ref[n : n + 1, 1:2] = length
        renewed = masters[n][...] - 0.5 * size / (length + 1e-06) * updates[n][...]
        weights[n][...] = renewed
        copies[n][...] = renewed.astype(BF)
    grad = total[0:12]
    vectors = vec_ref[...]
    moment, square, update = terms(vectors, vfirst_ref[...], vsecond_ref[...], grad)
    vm_ref[...] = moment
    vs_ref[...] = square
    size = jnp.sqrt(jnp.sum(vectors * vectors, axis=-1, keepdims=True))
    length = jnp.sqrt(jnp.sum(update * update, axis=-1, keepdims=True))
    vw_ref[...] = vectors - 0.5 * size / (length + 1e-06) * update
    token_ref[...] = total[12:13]
    bias_ref[...] = total[11:12]
    wires.drain()


def lamb(masters, firsts, seconds, totals, head, tail, hidden, vectors, vfirst, vsecond):
    full = [jax.ShapeDtypeStruct(m.shape, F32) for m in masters]
    width = vectors.shape[1]
    flat = jax.ShapeDtypeStruct((1, width), F32)
    like = jax.ShapeDtypeStruct(vectors.shape, F32)
    return pl.pallas_call(
        lamb_kernel,
        out_shape=[
            *full,
            *full,
            *full,
            *[jax.ShapeDtypeStruct(m.shape, BF) for m in masters],
            flat,
            flat,
            like,
            like,
            like,
            jax.ShapeDtypeStruct((4, 2), F32),
        ],
        in_specs=[in_vmem()] * 22,
        out_specs=[in_vmem()] * 22,
        scratch_shapes=[
            *[pltpu.VMEM(m.shape, F32) for m in masters],
            pltpu.VMEM((3, 16, width), F32),
            pltpu.VMEM((3, 16, width), F32),
            pltpu.VMEM((4, 16, width), F32),
            pltpu.SemaphoreType.DMA((6,)),
            pltpu.SemaphoreType.DMA((6,)),
        ],
        compiler_params=params(collective_id=4, has_side_effects=True),
        name="lamb",
    )(*masters, *firsts, *seconds, *totals, head, tail, hidden, vectors, vfirst, vsecond)


def lamb_terms(weight, moment, square, gradient):
    moment_new = 0.5 * moment + 0.5 * gradient
    square_new = 0.5 * square + 0.5 * gradient * gradient
    correct = 1.0 - 0.5**STEP
    update = moment_new / correct / (jnp.sqrt(square_new / correct) + 1e-06) + 0.01 * weight
    return (
        moment_new,
        square_new,
        update,
        jnp.stack([jnp.sum(weight * weight), jnp.sum(update * update)]),
    )


def lamb_apply(weight, update, norms):
    renewed = weight - 0.5 * norms[0] / (norms[1] + 1e-06) * update
    return (renewed, renewed.astype(BF))


def per_device(
    patches,
    cube_mask,
    mask_token,
    cotangent,
    vectors,
    vector_first,
    vector_second,
    attend_master,
    attend_first,
    attend_second,
    mixing_master,
    mixing_first,
    mixing_second,
    expand_master,
    expand_first,
    expand_second,
    shrink_master,
    shrink_first,
    shrink_second,
):
    clips, rows, width = patches.shape
    axis = lax.axis_size("dp")
    own_rows = attend_master.shape[0]
    direct = axis == 16 and lax.axis_size("mp") == 2
    masters = [
        attend_master.reshape(own_rows, -1),
        mixing_master,
        expand_master,
        shrink_master,
    ]
    shards = [m.astype(BF) for m in masters]
    mask, token, dy = cube_mask.reshape(rows, 1), mask_token[None], cotangent[0]
    firsts = [attend_first.reshape(own_rows, -1), mixing_first, expand_first, shrink_first]
    seconds = [attend_second.reshape(own_rows, -1), mixing_second, expand_second, shrink_second]
    if direct:
        *wholes, q, k, v, a1, a1_other = first(shards, patches[0], mask, token, vectors)
        wa = wholes[0].reshape(2, width, -1)
        o, o_low, p, *rest = attend(q, k, v, wholes[1:])
        wm, we, ws = (w.reshape(2, width, -1) for w in rest)
        block_out, dx1, do, gm, ge, gs, gu, gv = middle(
            patches[0], mask, token, o_low, dy, vectors, wm, we, ws
        )
        dq, dk, dv, ts, te, tm = attend_back(q, k, v, do, o, p, [gs, ge, gm], own_rows)
        patch_grad, head, *totals = last(
            a1, a1_other, dq, dk, dv, wa, patches[0], mask, token, vectors, dx1, [tm, te, ts]
        )
        done = lamb(
            masters, firsts, seconds, totals, head, gv, gu.reshape(4, width), vectors, vector_first, vector_second
        )
        results = []
        for n in range(4):
            group = [done[n], done[4 + n], done[8 + n], done[12 + n]]
            if n == 0:
                group = [g.reshape(attend_master.shape) for g in group]
            results.extend(group)
        token_grad, bias_grad, *vector_results = done[16:]
        return (
            block_out[None],
            patch_grad[None],
            token_grad[0],
            bias_grad[0],
            *results,
            *vector_results,
        )
    swap = [(0, 1), (1, 0)]
    chosen = mask > 0
    x = jnp.where(chosen, token, patches[0].astype(F32))
    centred = x - mean_rows(x)
    scale = lax.rsqrt(mean_rows(centred * centred) + 1e-6)
    wa, wm, we, ws = (
        lax.all_gather(lax.all_gather(s, "dp", axis=0, tiled=True), "mp", axis=0) for s in shards
    )
    a1 = (centred * scale * vectors[0] + vectors[1]).astype(BF)
    a1_other = lax.ppermute(a1, "mp", swap)
    q, k, v = project(a1, a1_other, wa, vectors[2:4])
    o, o_low, p = attend(q, k, v, [])
    block_out, dx1, do, gm, ge, gs, gu, gv = middle(
        patches[0], mask, token, o_low, dy, vectors, wm, we, ws
    )
    dq, dk, dv = attend_back(q, k, v, do, o, p, [], own_rows)
    da1, da1_send, ga, gqv = unproject(a1, a1_other, dq, dk, dv, wa)
    da1 = da1 + lax.ppermute(da1_send, "mp", swap).astype(F32)
    totals = []
    for g in (ga, gm, ge, gs):
        g = lax.psum_scatter(g, "mp", scatter_dimension=0, tiled=True)
        totals.append(lax.psum_scatter(g[0].astype(F32), "dp", scatter_dimension=0, tiled=True))
    xh = centred * scale
    e = da1 * vectors[0]
    dx = dx1 + scale * (e - mean_rows(e) - xh * mean_rows(e * xh))
    patch_grad = jnp.where(chosen, 0.0, dx).astype(BF)
    token_part = jnp.sum(jnp.where(chosen, dx, 0.0), axis=0)
    vector_part = jnp.concatenate(
        [
            jnp.sum(da1 * xh, axis=0)[None],
            jnp.sum(da1, axis=0)[None],
            gqv[0:2],
            gv[0:3],
            gu.reshape(4, width),
            gv[3:4],
        ],
        axis=0,
    )
    terms = [lamb_terms(w, m, s, g) for w, m, s, g in zip(masters, firsts, seconds, totals)]
    squares = jnp.stack([t[3] for t in terms])
    vector_total, token_grad, square_total = lax.psum(
        (vector_part, token_part, squares), ("dp", "mp")
    )
    trust_norms = jnp.sqrt(square_total)
    results = []
    for n, (w, t) in enumerate(zip(masters, terms)):
        group = [t[0], t[1], *lamb_apply(w, t[2], trust_norms[n])]
        if n == 0:
            group = [g.reshape(attend_master.shape) for g in group]
        results.extend(group)
    vector_moment = 0.5 * vector_first + 0.5 * vector_total
    vector_square = 0.5 * vector_second + 0.5 * vector_total * vector_total
    correct = 1.0 - 0.5**STEP
    vector_update = (
        vector_moment / correct / (jnp.sqrt(vector_square / correct) + 1e-06) + 0.01 * vectors
    )
    row_weight = jnp.sqrt(jnp.sum(vectors * vectors, axis=-1, keepdims=True))
    row_update = jnp.sqrt(jnp.sum(vector_update * vector_update, axis=-1, keepdims=True))
    vector_weight = vectors - 0.5 * row_weight / (row_update + 1e-06) * vector_update
    return (
        block_out[None],
        patch_grad[None],
        token_grad,
        vector_total[11],
        *results,
        vector_moment,
        vector_square,
        vector_weight,
        trust_norms,
    )


def solution(mesh):
    rows = P("dp", "mp", None)
    flat = P("dp", "mp")
    deep = P("dp", None, "mp")
    copied = P()
    return jax.shard_map(
        per_device,
        mesh=mesh,
        in_specs=(rows, flat, copied, rows, copied, copied, copied, *[deep] * 3, *[flat] * 9),
        out_specs=(rows, rows, copied, copied, *[deep] * 4, *[flat] * 12, *[copied] * 4),
        check_vma=False,
    )
```

```python
import functools

import jax
import jax.numpy as jnp
from jax import lax
from jax.experimental import pallas as pl
from jax.experimental.pallas import tpu as pltpu
from jax.sharding import PartitionSpec as P

HD = 64
PAIR = 2 * HD
STEP = 5
BF = jnp.bfloat16
F32 = jnp.float32
NN = (((1,), (0,)), ((), ()))
NT = (((1,), (1,)), ((), ()))
TN = (((0,), (0,)), ((), ()))
LOG2E = 1.4426950408889634
MESH = pl.DeviceIdType.MESH
VMEM_LIMIT = 60 * 2**20


def dot(a, b, dims=NN):
    return lax.dot_general(a, b, dims, preferred_element_type=F32)


def params(**kw):
    return pltpu.CompilerParams(vmem_limit_bytes=VMEM_LIMIT, **kw)


def anywhere():
    return pl.BlockSpec(memory_space=pl.ANY)


def in_vmem():
    return pl.BlockSpec(memory_space=pltpu.VMEM)


def place():
    dp, x = lax.axis_index("dp"), lax.axis_index("mp")
    return x, dp // 4, lax.rem(dp // 2, 2), lax.rem(dp, 2)


def device(x, z, y, c):
    return ((z * 2 + y) * 2 + c, x)


def neighbours():
    x, z, y, c = place()
    lines = [device(x, lax.rem(z + k, 4), y, c) for k in (1, 2, 3)]
    return lines, device(1 - x, z, y, c), device(x, z, 1 - y, c), device(x, z, y, 1 - c)


def greet():
    lines, over_x, over_y, sibling = neighbours()
    barrier = pltpu.get_barrier_semaphore()
    for other in (*lines, over_x, over_y, sibling):
        pl.semaphore_signal(barrier, inc=1, device_id=other, device_id_type=MESH)
    pl.semaphore_wait(barrier, 6)


class Wires:
    def __init__(self, send_sem, recv_sem):
        self.send_sem, self.recv_sem = send_sem, recv_sem
        self.started = []

    def copy(self, slot, src, dst, other):
        return pltpu.make_async_remote_copy(
            src_ref=src,
            dst_ref=dst,
            send_sem=self.send_sem.at[slot],
            recv_sem=self.recv_sem.at[slot],
            device_id=other,
            device_id_type=MESH,
        )

    def start(self, slot, src, dst, other):
        self.copy(slot, src, dst, other).start()
        self.started.append((slot, src))

    def send(self, slot, whole, part, other):
        self.copy(slot, whole.at[part], whole.at[part], other).start()
        self.started.append((slot, whole, part))

    def arrive(self, slot, dst):
        x, z, y, c = place()
        self.copy(slot, dst, dst, device(x, z, y, 1 - c)).wait_recv()

    def sent(self, slot, src):
        x, z, y, c = place()
        self.copy(slot, src, src, device(x, z, y, 1 - c)).wait_send()

    def drain(self):
        for slot, src, *part in self.started:
            self.sent(slot, src.at[part[0]] if part else src)


ALL = slice(None)


def first_kernel(*refs):
    masters, (patch_ref, flag_ref, token_ref, vec_ref) = refs[:4], refs[4:8]
    wa_out, wm, we, ws, q_out, k_out, v_out, a1_out, other_out, mask_ref = refs[8:18]
    wa, landing, a1_ref, q_ref, k_ref, v_ref, sa, sm, se, ss, own_sem, put_sem, send_sem, recv_sem = refs[18:]
    x, z, y, c = place()
    lines, over_x, over_y, sibling = neighbours()
    wires = Wires(send_sem, recv_sem)
    rows = a1_ref.shape[0]
    cut = rows // 32 * 16
    halves = (pl.ds(0, cut), pl.ds(cut, rows - cut))
    width = wa.shape[-1] // 3
    for n in range(3):
        sa[:, n * width : (n + 1) * width] = masters[0][n].astype(BF)
    for shard, master in zip((sm, se, ss), masters[1:]):
        shard[...] = master[...].astype(BF)
    puts = []

    def put(src, dst):
        copy = pltpu.make_async_copy(src, dst, put_sem.at[len(puts)])
        copy.start()
        puts.append(copy)

    greet()

    def back(k):
        return lax.rem(z + 4 - k, 4)

    own = [pltpu.make_async_copy(sa, wa.at[x, z, y, c], own_sem.at[0])]
    for n, (shard, whole) in enumerate(((sm, wm), (se, we), (ss, ws))):
        own.append(pltpu.make_async_copy(shard, whole.at[x, z, y, c], own_sem.at[n + 1]))
    for copy in own:
        copy.start()
    for k in (1, 2, 3):
        wires.start(k - 1, sa, wa.at[x, z, y, c], lines[k - 1])
    wires.start(3, sa, wa.at[x, z, y, c], over_x)
    wires.start(7, sa, wa.at[x, z, y, c], over_y)

    flags = jnp.broadcast_to(flag_ref[...].astype(F32), (PAIR, rows))
    mask_ref[...] = flags.T[:, :1]
    tubes = tubes_of(patch_ref, mask_ref, token_ref)
    centred = tubes - mean_rows(tubes)
    scale = lax.rsqrt(mean_rows(centred * centred) + 1e-6)
    a1_ref[...] = (centred * scale * vec_ref[0:1] + vec_ref[1:2]).astype(BF)
    wires.start(19, a1_ref.at[halves[0]], landing.at[halves[0]], over_x)
    put(a1_ref, a1_out)

    for k in (1, 2, 3):
        part = wa.at[x, back(k), y, c]
        wires.arrive(k - 1, part)
        wires.start(3 + k, part, part, over_x)
        wires.start(7 + k, part, part, over_y)
    wires.start(20, a1_ref.at[halves[1]], landing.at[halves[1]], over_x)
    for copy in own:
        copy.wait()
    line = wa.at[x, ALL, y, c]
    wires.start(15, line, line, sibling)
    others = ((sm, wm), (se, we), (ss, ws))
    for n, (shard, whole) in enumerate(others):
        for k in (1, 2, 3):
            wires.start(21 + 3 * n + k - 1, shard, whole.at[x, z, y, c], lines[k - 1])
    for k in range(4):
        part = wa.at[1 - x, back(k), y, c]
        wires.arrive(3 + k, part)
        wires.start(11 + k, part, part, over_y)
    for n in range(2):
        shard, whole = others[n]
        wires.start(30 + 4 * n, shard, whole.at[x, z, y, c], over_y)
    line = wa.at[1 - x, ALL, y, c]
    wires.start(16, line, line, sibling)
    for k in range(4):
        wires.arrive(7 + k, wa.at[x, back(k), 1 - y, c])
    line = wa.at[x, ALL, 1 - y, c]
    wires.start(17, line, line, sibling)

    def pass_on(n):
        whole = others[n][1]
        for k in (1, 2, 3):
            part = whole.at[x, back(k), y, c]
            wires.arrive(21 + 3 * n + k - 1, part)
            wires.start(30 + 4 * n + k, part, part, over_y)

    pass_on(0)
    for k in range(4):
        wires.arrive(11 + k, wa.at[1 - x, back(k), 1 - y, c])
    line = wa.at[1 - x, ALL, 1 - y, c]
    wires.start(18, line, line, sibling)
    for n, (i, j) in enumerate(((x, y), (1 - x, y), (x, 1 - y), (1 - x, 1 - y))):
        wires.arrive(15 + n, wa.at[i, ALL, j, 1 - c])
    out_copy = pltpu.make_async_copy(wa, wa_out, own_sem.at[0])
    out_copy.start()

    depth = a1_ref.shape[1]

    def weight(h, n):
        return wa[h, :, :, :, :, n * width : (n + 1) * width].reshape(depth, width)

    def keys_values(h, source, span):
        k_ref[h, span] = dot(source, weight(h, 1)).astype(BF)
        values = dot(source, weight(h, 2)) + vec_ref[3:4, h * width : (h + 1) * width]
        v_ref[h, span] = values.astype(BF)

    for h in range(2):
        queries = dot(a1_ref[...], weight(h, 0)) + vec_ref[2:3, h * width : (h + 1) * width]
        q_ref[h] = (queries.astype(BF).astype(F32) * HD**-0.5).astype(BF)
        put(q_ref.at[h], q_out.at[h])
        keys_values(h, a1_ref[...], pl.ds(0, rows))
        for ref, out in ((k_ref, k_out), (v_ref, v_out)):
            put(ref.at[h, pl.ds(0, rows)], out.at[h, pl.ds(0, rows)])
    pass_on(1)
    for n in range(2):
        wires.arrive(19 + n, landing.at[halves[n]])
        part = landing[halves[n]]
        put(landing.at[halves[n]], other_out.at[halves[n]])
        span = pl.ds(rows + (cut if n else 0), part.shape[0])
        for h in range(2):
            keys_values(h, part, span)
            for ref, out in ((k_ref, k_out), (v_ref, v_out)):
                put(ref.at[h, span], out.at[h, span])
    for n in range(2):
        for k in range(4):
            wires.arrive(30 + 4 * n + k, others[n][1].at[x, back(k), 1 - y, c])
    for k in (1, 2, 3):
        wires.arrive(27 + k - 1, ws.at[x, back(k), y, c])
    out_copy.wait()
    for copy in puts:
        copy.wait()
    wires.drain()


def first(masters, patches, flags, token, vectors):
    rows, width = patches.shape
    half = width // 2
    own_rows = masters[1].shape[0]
    shards = [(own_rows, 3 * half), *[m.shape for m in masters[1:]]]
    gathered = [(2, 4, 2, 2, *s) for s in shards]
    wholes = [jax.ShapeDtypeStruct(g, BF) for g in gathered]
    keys = jax.ShapeDtypeStruct((2, 2 * rows, half), BF)
    flat = jax.ShapeDtypeStruct((rows, width), BF)
    return pl.pallas_call(
        first_kernel,
        out_shape=[
            *wholes,
            jax.ShapeDtypeStruct((2, rows, half), BF),
            keys,
            keys,
            flat,
            flat,
            jax.ShapeDtypeStruct((rows, 1), F32),
        ],
        in_specs=[in_vmem()] * 8,
        out_specs=[anywhere()] * 9 + [in_vmem()],
        scratch_shapes=[
            pltpu.VMEM(gathered[0], BF),
            pltpu.VMEM((rows, width), BF),
            pltpu.VMEM((rows, width), BF),
            pltpu.VMEM((2, rows, half), BF),
            pltpu.VMEM((2, 2 * rows, half), BF),
            pltpu.VMEM((2, 2 * rows, half), BF),
            *[pltpu.VMEM(s, BF) for s in shards],
            pltpu.SemaphoreType.DMA((4,)),
            pltpu.SemaphoreType.DMA((17,)),
            pltpu.SemaphoreType.DMA((38,)),
            pltpu.SemaphoreType.DMA((38,)),
        ],
        compiler_params=params(collective_id=0, has_side_effects=True),
        name="first",
    )(*masters, patches, flags, token, vectors)


def add_into(dst, other):
    dst[...] = (dst[...].astype(F32) + other[...].astype(F32)).astype(BF)


def project_kernel(mine_ref, other_ref, w_ref, bias_ref, q_ref, k_ref, v_ref):
    rows = mine_ref.shape[0]
    half = w_ref.shape[2] // 3
    for h in range(2):
        cols = slice(h * half, (h + 1) * half)
        queries = dot(mine_ref[...], w_ref[h, :, :half]) + bias_ref[0:1, cols]
        q_ref[h] = (queries.astype(BF).astype(F32) * HD**-0.5).astype(BF)
        for part, ref in ((0, mine_ref), (1, other_ref)):
            span = slice(part * rows, (part + 1) * rows)
            k_ref[h, span] = dot(ref[...], w_ref[h, :, half : 2 * half]).astype(BF)
            v_ref[h, span] = (dot(ref[...], w_ref[h, :, 2 * half :]) + bias_ref[1:2, cols]).astype(BF)


def project(mine, other, weight, bias):
    rows, width = mine.shape
    keys = jax.ShapeDtypeStruct((2, 2 * rows, width // 2), BF)
    return pl.pallas_call(
        project_kernel,
        out_shape=[jax.ShapeDtypeStruct((2, rows, width // 2), BF), keys, keys],
        in_specs=[in_vmem()] * 4,
        out_specs=[in_vmem()] * 3,
        compiler_params=params(),
        name="project",
    )(mine, other, weight, bias)


def half_lanes():
    lane = lax.broadcasted_iota(jnp.int32, (1, PAIR), 1)
    return lane < HD, lane >= HD


def row_blocks(rows):
    cut = (rows // 2 + 15) // 16 * 16
    return ((0, cut), (cut, rows))


def key_parts(keys):
    cut = keys // 2 // 256 * 256
    return ((0, cut), (cut, keys))


def attend_pair(q_ref, k_ref, v_ref, o_ref, low_ref, inv_ref, p_ref):
    sides = half_lanes()
    k, v = k_ref[0], v_ref[0]
    parts = key_parts(k.shape[0])
    for a, b in row_blocks(q_ref.shape[1]):
        q = q_ref[0, a:b]
        outs, invs = [], []
        for h in range(2):
            q_h = jnp.where(sides[h], q, jnp.zeros_like(q))
            v_h = jnp.where(sides[h], v, jnp.ones_like(v))
            scores = [dot(q_h, k[c:d], NT) for c, d in parts]
            tops = [jnp.max(s, axis=-1, keepdims=True) for s in scores]
            top = functools.reduce(jnp.maximum, tops) * LOG2E
            out = None
            for s, (c, d) in zip(scores, parts):
                p = jnp.exp2(s * LOG2E - top).astype(BF)
                p_ref[h, a:b, c:d] = p
                more = dot(p, v_h[c:d])
                out = more if out is None else out + more
            spare = HD if h == 0 else 0
            inv = 1.0 / out[:, spare : spare + 1]
            outs.append(out * inv)
            invs.append(inv)
        o = jnp.where(sides[0], *outs)
        o_ref[0, a:b] = o
        low_ref[0, a:b] = o.astype(BF)
        inv_ref[0, a:b] = jnp.where(sides[0], *invs)


def attend_kernel(*refs):
    outs, (wm, we, ws, send_sem, recv_sem) = refs[6:10], refs[10:]
    i = pl.program_id(0)
    x, z, y, c = place()
    lines, over_x, over_y, sibling = neighbours()
    wires = Wires(send_sem, recv_sem)
    here, side, flank, across = (x, ALL, y, c), (1 - x, ALL, y, c), (x, ALL, 1 - y, c), (1 - x, ALL, 1 - y, c)

    send = wires.send

    @pl.when(i == 0)
    def _():
        greet()
        send(0, wm, here, over_x)
        send(1, we, here, over_x)
        send(2, ws, here, over_y)
        send(3, ws, here, over_x)
        send(4, wm, flank, over_x)
        send(5, wm, here, sibling)
        send(6, wm, flank, sibling)
        send(7, we, here, sibling)
        send(8, we, flank, sibling)
        send(9, ws, here, sibling)

    @pl.when(i == 2)
    def _():
        wires.arrive(0, wm.at[side])
        send(10, wm, side, sibling)
        wires.arrive(1, we.at[side])
        send(11, we, side, over_y)
        send(12, we, side, sibling)

    @pl.when(i == 4)
    def _():
        wires.arrive(3, ws.at[side])
        send(13, ws, side, over_y)
        send(14, ws, side, sibling)
        wires.arrive(2, ws.at[flank])
        send(15, ws, flank, sibling)
        wires.arrive(4, wm.at[across])
        send(16, wm, across, sibling)

    attend_pair(*refs[:3], *outs)

    @pl.when(i == pl.num_programs(0) - 1)
    def _():
        wires.arrive(11, we.at[across])
        send(17, we, across, sibling)
        wires.arrive(13, ws.at[across])
        send(18, ws, across, sibling)
        for slot, whole, (a, b) in (
            (5, wm, (x, y)),
            (6, wm, (x, 1 - y)),
            (7, we, (x, y)),
            (8, we, (x, 1 - y)),
            (9, ws, (x, y)),
            (10, wm, (1 - x, y)),
            (12, we, (1 - x, y)),
            (14, ws, (1 - x, y)),
            (15, ws, (x, 1 - y)),
            (16, wm, (1 - x, 1 - y)),
            (17, we, (1 - x, 1 - y)),
            (18, ws, (1 - x, 1 - y)),
        ):
            wires.arrive(slot, whole.at[a, ALL, b, 1 - c])
        wires.drain()


def attend(q, k, v, wholes):
    _, rows, half = q.shape
    keys = k.shape[1]
    per = half // PAIR
    of_q = pl.BlockSpec((1, rows, PAIR), lambda i: (i // per, 0, lax.rem(i, per)))
    of_k = pl.BlockSpec((1, keys, PAIR), lambda i: (i // per, 0, lax.rem(i, per)))
    shapes = [
        jax.ShapeDtypeStruct(q.shape, F32),
        jax.ShapeDtypeStruct(q.shape, BF),
        jax.ShapeDtypeStruct(q.shape, F32),
        jax.ShapeDtypeStruct((4 * per, rows, keys), BF),
    ]
    of_p = pl.BlockSpec((2, rows, keys), lambda i: (i, 0, 0))
    common = dict(grid=(2 * per,), name="attend")
    if not wholes:
        return pl.pallas_call(
            attend_pair,
            in_specs=[of_q, of_k, of_k],
            out_specs=[of_q, of_q, of_q, of_p],
            out_shape=shapes,
            compiler_params=params(),
            **common,
        )(q, k, v)
    return pl.pallas_call(
        attend_kernel,
        in_specs=[of_q, of_k, of_k, *[anywhere()] * 3],
        out_specs=[of_q, of_q, of_q, of_p, *[anywhere()] * 3],
        out_shape=[*shapes, *[jax.ShapeDtypeStruct(w.shape, BF) for w in wholes]],
        input_output_aliases={3: 4, 4: 5, 5: 6},
        scratch_shapes=[pltpu.SemaphoreType.DMA((19,)), pltpu.SemaphoreType.DMA((19,))],
        compiler_params=params(collective_id=2, has_side_effects=True),
        **common,
    )(q, k, v, *wholes)


def attend_back_pair(q_ref, k_ref, v_ref, do_ref, o_ref, p_ref, dq_ref, dk_ref, dv_ref):
    sides = half_lanes()
    k, v = k_ref[0], v_ref[0]
    parts = key_parts(k.shape[0])
    grad_k = [[None] * 2 for _ in parts]
    grad_v = [[None] * 2 for _ in parts]

    def plus(total, more):
        return more if total is None else total + more

    for a, b in row_blocks(q_ref.shape[1]):
        q, do = q_ref[0, a:b], do_ref[0, a:b]
        prod = do.astype(F32) * o_ref[0, a:b]
        q_t, do_t = q.T, do.T
        outs = []
        for h in range(2):
            do_h = jnp.where(sides[h], do, jnp.zeros_like(do))
            row_dot = jnp.sum(jnp.where(sides[h], prod, 0.0), axis=-1, keepdims=True)
            out = None
            rows = slice(h * HD, (h + 1) * HD)
            for n, (c, d) in enumerate(parts):
                p = p_ref[h, a:b, c:d]
                grad_p = dot(do_h, v[c:d], NT)
                ds = (p.astype(F32) * (grad_p - row_dot)).astype(BF)
                out = plus(out, dot(ds, k[c:d]))
                grad_k[n][h] = plus(grad_k[n][h], dot(q_t[rows], ds))
                grad_v[n][h] = plus(grad_v[n][h], dot(do_t[rows], p))
            outs.append(out)
        dq_ref[0, a:b] = (jnp.where(sides[0], *outs) * HD**-0.5).astype(BF)
    for n, (c, d) in enumerate(parts):
        dk_ref[0, c:d] = jnp.concatenate(grad_k[n], axis=0).T.astype(BF)
        dv_ref[0, c:d] = jnp.concatenate(grad_v[n], axis=0).T.astype(BF)


def attend_back_kernel(*refs):
    ins, grads = refs[:6], refs[6:9]
    outs, totals = refs[9:12], refs[12:15]
    refs = refs[15:]
    mine, sib, diag, side = refs[:3], refs[3:6], refs[6:9], refs[9:12]
    own_sem, send_sem, recv_sem = refs[12:]
    i = pl.program_id(0)
    x, z, y, c = place()
    lines, over_x, over_y, sibling = neighbours()
    wires = Wires(send_sem, recv_sem)

    def keep(n):
        return pltpu.make_async_copy(grads[n].at[:, :, :, c], mine[n], own_sem.at[n])

    def after_sibling(n):
        keep(n).wait()
        wires.arrive(5 * n, sib[n])

        def sweep(m, _):
            part = (m // 8, lax.rem(m // 2, 4), lax.rem(m, 2))
            add_into(mine[n].at[part], sib[n].at[part])
            return 0

        lax.fori_loop(0, 16, sweep, 0)
        wires.start(5 * n + 1, mine[n].at[1 - x, pl.ds(0, 2), 1 - y], diag[n].at[0], over_x)
        wires.start(5 * n + 2, mine[n].at[1 - x, pl.ds(2, 2), 1 - y], diag[n].at[1], over_y)

    def after_diagonal(n):
        wires.arrive(5 * n + 1, diag[n].at[0])
        wires.arrive(5 * n + 2, diag[n].at[1])

        def sweep(m, _):
            add_into(mine[n].at[x, m, 1 - y], diag[n].at[0, m])
            add_into(mine[n].at[1 - x, 2 + m, y], diag[n].at[1, m])
            return 0

        lax.fori_loop(0, 2, sweep, 0)
        wires.start(5 * n + 3, mine[n].at[1 - x, :, y], side[n].at[0], over_x)
        wires.start(5 * n + 4, mine[n].at[x, :, 1 - y], side[n].at[1], over_y)

    def after_sides(n):
        wires.arrive(5 * n + 3, side[n].at[0])
        wires.arrive(5 * n + 4, side[n].at[1])

        def sweep(m, _):
            both = side[n][0, m].astype(F32) + side[n][1, m].astype(F32)
            totals[n][m] = (mine[n][x, m, y].astype(F32) + both).astype(BF)
            return 0

        lax.fori_loop(0, 4, sweep, 0)

    @pl.when(i == 0)
    def _():
        greet()
        for n in range(3):
            keep(n).start()
            wires.start(5 * n, grads[n].at[:, :, :, 1 - c], sib[n], sibling)

    @pl.when(i == 1)
    def _():
        after_sibling(0)

    @pl.when(i == 2)
    def _():
        after_sibling(1)
        after_diagonal(0)
        after_sibling(2)

    @pl.when(i == 4)
    def _():
        after_diagonal(1)
        after_diagonal(2)

    attend_back_pair(*ins, *outs)

    @pl.when(i == pl.num_programs(0) - 1)
    def _():
        for n in range(3):
            after_sides(n)
        for n in range(3):
            wires.sent(5 * n, grads[n].at[:, :, :, 1 - c])
            wires.sent(5 * n + 1, mine[n].at[1 - x, pl.ds(0, 2), 1 - y])
            wires.sent(5 * n + 2, mine[n].at[1 - x, pl.ds(2, 2), 1 - y])
            wires.sent(5 * n + 3, mine[n].at[1 - x, :, y])
            wires.sent(5 * n + 4, mine[n].at[x, :, 1 - y])


def attend_back(q, k, v, do, o, p, grads, own_rows):
    _, rows, half = q.shape
    keys = k.shape[1]
    per = half // PAIR
    of_q = pl.BlockSpec((1, rows, PAIR), lambda i: (i // per, 0, lax.rem(i, per)))
    of_k = pl.BlockSpec((1, keys, PAIR), lambda i: (i // per, 0, lax.rem(i, per)))
    of_p = pl.BlockSpec((2, rows, keys), lambda i: (i, 0, 0))
    shapes = [
        jax.ShapeDtypeStruct(q.shape, BF),
        jax.ShapeDtypeStruct(k.shape, BF),
        jax.ShapeDtypeStruct(k.shape, BF),
    ]
    common = dict(grid=(2 * per,), name="attend_back")
    if not grads:
        return pl.pallas_call(
            attend_back_pair,
            in_specs=[of_q, of_k, of_k, of_q, of_q, of_p],
            out_specs=[of_q, of_k, of_k],
            out_shape=shapes,
            compiler_params=params(),
            **common,
        )(q, k, v, do, o, p)
    widths = [g.shape[-1] for g in grads]
    lined = [(4, own_rows, w) for w in widths]
    return pl.pallas_call(
        attend_back_kernel,
        in_specs=[of_q, of_k, of_k, of_q, of_q, of_p, *[anywhere()] * 3],
        out_specs=[of_q, of_k, of_k, *[pl.BlockSpec(t, lambda i: (0, 0, 0)) for t in lined]],
        out_shape=[*shapes, *[jax.ShapeDtypeStruct(t, BF) for t in lined]],
        scratch_shapes=[
            *[pltpu.VMEM((2, 4, 2, own_rows, w), BF) for w in widths],
            *[pltpu.VMEM((2, 4, 2, own_rows, w), BF) for w in widths],
            *[pltpu.VMEM((2, 2, own_rows, w), BF) for w in widths],
            *[pltpu.VMEM((2, 4, own_rows, w), BF) for w in widths],
            pltpu.SemaphoreType.DMA((3,)),
            pltpu.SemaphoreType.DMA((15,)),
            pltpu.SemaphoreType.DMA((15,)),
        ],
        compiler_params=params(collective_id=3, has_side_effects=True),
        **common,
    )(q, k, v, do, o, p, *[g.reshape(2, 4, 2, 2, own_rows, w) for g, w in zip(grads, widths)])


def normal_parts(h):
    z = jnp.abs(h) * 0.7071067811865476
    t = 1.0 / (1.0 + 0.3275911 * z)
    bell = jnp.exp(-z * z)
    poly = t * (
        0.254829592
        + t * (-0.284496736 + t * (1.421413741 + t * (-1.453152027 + t * 1.061405429)))
    )
    tail = 0.5 * poly * bell
    return jnp.where(h < 0, tail, 1.0 - tail), bell * 0.3989422804014327


def mean_rows(values):
    return jnp.mean(values, axis=-1, keepdims=True)


def tubes_of(patch_ref, mask_ref, token_ref):
    return jnp.where(mask_ref[...] > 0, token_ref[...][None], patch_ref[...].astype(F32))


def middle_kernel(
    patch_ref,
    mask_ref,
    token_ref,
    o_ref,
    inv_ref,
    dy_ref,
    vec_ref,
    wm_ref,
    we_ref,
    ws_ref,
    out_ref,
    dx1_ref,
    do_ref,
    gm_ref,
    ge_ref,
    gs_ref,
    gv_ref,
    x1_ref,
    a2_ref,
    acc_ref,
    da2_ref,
):
    i = pl.program_id(0)

    @pl.when(i == 0)
    def _():
        x1 = tubes_of(patch_ref, mask_ref, token_ref) + vec_ref[4:5]
        for h in range(2):
            x1 = x1 + dot(o_ref[h], wm_ref[h], NT)
        x1_ref[...] = x1
        centred = x1 - mean_rows(x1)
        scale = lax.rsqrt(mean_rows(centred * centred) + 1e-6)
        a2_ref[...] = (centred * scale * vec_ref[5:6] + vec_ref[6:7]).astype(BF)
        acc_ref[...] = x1 + vec_ref[11:12]
        da2_ref[...] = jnp.zeros_like(da2_ref)

    a2, dy = a2_ref[...], dy_ref[...]
    we, ws = we_ref[0], ws_ref[0]
    hidden = dot(a2, we) + vec_ref[pl.ds(7 + i, 1)]
    cdf, density = normal_parts(hidden)
    u = (hidden * cdf).astype(BF)
    du = dot(dy, ws)
    dh = (du * (cdf + hidden * density)).astype(BF)
    acc_ref[...] += dot(u, ws, NT)
    da2_ref[...] += dot(dh, we, NT)
    gs_ref[0] = dot(dy, u, TN).astype(BF)
    ge_ref[0] = dot(a2, dh, TN).astype(BF)
    gv_ref[pl.ds(4 + i, 1)] = jnp.sum(dh.astype(F32), axis=0, keepdims=True)

    @pl.when(i == pl.num_programs(0) - 1)
    def _():
        out_ref[...] = acc_ref[...].astype(BF)
        x1 = x1_ref[...]
        top = dy_ref[...].astype(F32)
        centred = x1 - mean_rows(x1)
        scale = lax.rsqrt(mean_rows(centred * centred) + 1e-6)
        xh = centred * scale
        da2 = da2_ref[...]
        e = da2 * vec_ref[5:6]
        dx1 = top + scale * (e - mean_rows(e) - xh * mean_rows(e * xh))
        dx1_ref[...] = dx1
        dxb = dx1.astype(BF)
        for h in range(2):
            do_ref[h] = (dot(dxb, wm_ref[h]) * inv_ref[h]).astype(BF)
            gm_ref[h] = dot(dxb, o_ref[h], TN).astype(BF)
        gv_ref[0:1] = jnp.sum(dxb.astype(F32), axis=0, keepdims=True)
        gv_ref[1:2] = jnp.sum(da2 * xh, axis=0, keepdims=True)
        gv_ref[2:3] = jnp.sum(da2, axis=0, keepdims=True)
        gv_ref[3:4] = jnp.sum(top, axis=0, keepdims=True)


def middle(patches, mask, token, o, inv, dy, vectors, wm, we, ws):
    rows, width = patches.shape
    hidden = we.shape[2]
    block = width
    per = hidden // block
    steps = 2 * per
    of_w = pl.BlockSpec((1, width, block), lambda i: (i // per, 0, lax.rem(i, per)))

    def whole(shape):
        return pl.BlockSpec(shape, lambda i: (0,) * len(shape))

    return pl.pallas_call(
        middle_kernel,
        grid=(steps,),
        in_specs=[
            whole((rows, width)),
            whole((rows, 1)),
            whole(token.shape),
            whole(o.shape),
            whole(o.shape),
            whole((rows, width)),
            whole(vectors.shape),
            whole(wm.shape),
            of_w,
            of_w,
        ],
        out_specs=[
            whole((rows, width)),
            whole((rows, width)),
            whole(o.shape),
            whole(wm.shape),
            of_w,
            of_w,
            whole((8, width)),
        ],
        out_shape=[
            jax.ShapeDtypeStruct((rows, width), BF),
            jax.ShapeDtypeStruct((rows, width), F32),
            jax.ShapeDtypeStruct(o.shape, BF),
            jax.ShapeDtypeStruct(wm.shape, BF),
            jax.ShapeDtypeStruct(we.shape, BF),
            jax.ShapeDtypeStruct(ws.shape, BF),
            jax.ShapeDtypeStruct((8, width), F32),
        ],
        scratch_shapes=[
            pltpu.VMEM((rows, width), F32),
            pltpu.VMEM((rows, width), BF),
            pltpu.VMEM((rows, width), F32),
            pltpu.VMEM((rows, width), F32),
        ],
        compiler_params=params(),
        name="middle",
    )(patches, mask, token, o, inv, dy, vectors, wm, we, ws)


def unproject_kernel(
    mine_ref, other_ref, dq_ref, dk_ref, dv_ref, w_ref, da_ref, send_ref, gw_ref, gv_ref
):
    rows = mine_ref.shape[0]
    half = w_ref.shape[2] // 3
    da, send = None, None
    gv_ref[...] = jnp.zeros_like(gv_ref)
    for h in range(2):
        cols = slice(h * half, (h + 1) * half)
        dq, dk, dv = dq_ref[h], dk_ref[h], dv_ref[h]
        wq, wk, wv = (w_ref[h, :, n * half : (n + 1) * half] for n in range(3))
        mine = dot(dq, wq, NT) + dot(dk[:rows], wk, NT) + dot(dv[:rows], wv, NT)
        other = dot(dk[rows:], wk, NT) + dot(dv[rows:], wv, NT)
        da = mine if da is None else da + mine
        send = other if send is None else send + other
        a, b = mine_ref[...], other_ref[...]
        gw_ref[h, :, :half] = dot(a, dq, TN).astype(BF)
        gw_ref[h, :, half : 2 * half] = (dot(a, dk[:rows], TN) + dot(b, dk[rows:], TN)).astype(BF)
        gw_ref[h, :, 2 * half :] = (dot(a, dv[:rows], TN) + dot(b, dv[rows:], TN)).astype(BF)
        gv_ref[0:1, cols] = jnp.sum(dq.astype(F32), axis=0, keepdims=True)
        gv_ref[1:2, cols] = jnp.sum(dv.astype(F32), axis=0, keepdims=True)
    da_ref[...] = da
    send_ref[...] = send.astype(BF)


def unproject(mine, other, dq, dk, dv, weight):
    rows, width = mine.shape
    return pl.pallas_call(
        unproject_kernel,
        out_shape=[
            jax.ShapeDtypeStruct((rows, width), F32),
            jax.ShapeDtypeStruct((rows, width), BF),
            jax.ShapeDtypeStruct(weight.shape, BF),
            jax.ShapeDtypeStruct((8, width), F32),
        ],
        in_specs=[in_vmem()] * 6,
        out_specs=[in_vmem()] * 4,
        compiler_params=params(),
        name="unproject",
    )(mine, other, dq, dk, dv, weight)


def lamb_parts(weight, moment, square, grad):
    correct = 1.0 - 0.5**STEP
    moment_new = 0.5 * moment + 0.5 * grad
    square_new = 0.5 * square + 0.5 * grad * grad
    update = moment_new / correct / (jnp.sqrt(square_new / correct) + 1e-06) + 0.01 * weight
    return moment_new, square_new, update


def whole_sum(values):
    return jnp.sum(jnp.sum(values, axis=0, keepdims=True), axis=1, keepdims=True)


def last_kernel(*refs):
    sources, refs = refs[:8], refs[8:]
    (mask_ref, token_ref, vec_ref, tail_ref), refs = refs[:4], refs[4:]
    lined, refs = refs[:3], refs[3:]
    masters, firsts, seconds, refs = refs[:4], refs[4:8], refs[8:12], refs[12:]
    pg_ref, vtotal_ref, stotal_ref, *totals = refs[:7]
    refs = refs[7:]
    loaded, refs = refs[:8], refs[8:]
    dk_ref, dv_ref, w_ref, a_ref, b_ref, dq_ref, patch_ref, dx1_ref = loaded
    gw, sib, diag, side, da_ref, send_ref, landing = refs[:7]
    far, refs = refs[7:11], refs[11:]
    held, came, final, square_ref, square_line, load_sem, send_sem, recv_sem = refs
    x, z, y, c = place()
    lines, over_x, over_y, sibling = neighbours()
    wires = Wires(send_sem, recv_sem)
    rows, depth = a_ref.shape
    half = w_ref.shape[2] // 3
    cut = rows // 32 * 16
    spans = (pl.ds(0, cut), pl.ds(cut, rows - cut))
    loads = [pltpu.make_async_copy(s, d, load_sem.at[n]) for n, (s, d) in enumerate(zip(sources, loaded))]
    for load in loads:
        load.start()

    def flipped(code):
        def flip(v, bit):
            return 1 - v if bit else v

        return device(flip(x, code // 4), z, flip(y, code // 2 % 2), flip(c, code % 2))

    barrier = pltpu.get_barrier_semaphore()
    for other in (*lines, *[flipped(code) for code in range(1, 8)]):
        pl.semaphore_signal(barrier, inc=1, device_id=other, device_id_type=MESH)
    pl.semaphore_wait(barrier, 10)

    def ahead(k):
        return lax.rem(z + k, 4)

    for n in range(3):
        for k in (1, 2, 3):
            wires.start(3 * n + 3 + k - 1, lined[n].at[ahead(k)], far[n + 1].at[k - 1], lines[k - 1])

    def settle(n, own):
        total = own.astype(F32)
        for k in range(3):
            wires.arrive(3 * n + k, far[n].at[k])
            total = total + far[n][k].astype(F32)
        if n:
            totals[n][...] = total
        else:
            for part in range(3):
                totals[n][part] = total[:, part * half : (part + 1) * half]

    lane = lax.broadcasted_iota(jnp.int32, (8, PAIR), 1)
    squares = jnp.zeros((8, PAIR), F32)

    def add_squares(squares, n, pick):
        weight = masters[n][pick]
        update = lamb_parts(weight, firsts[n][pick], seconds[n][pick], totals[n][pick])[2]
        squares = squares + jnp.where(lane == 2 * n, whole_sum(weight * weight), 0.0)
        return squares + jnp.where(lane == 2 * n + 1, whole_sum(update * update), 0.0)

    def columns(n):
        return slice(n * half, (n + 1) * half)

    for n in range(3):
        loads[n].wait()
    for n, (start, size) in enumerate(((rows, cut), (rows + cut, rows - cut))):
        span = pl.ds(start, size)
        send = None
        for h in range(2):
            part = dot(dk_ref[h, span], w_ref[h, :, columns(1)], NT) + dot(dv_ref[h, span], w_ref[h, :, columns(2)], NT)
            send = part if send is None else send + part
        send_ref[spans[n]] = send.astype(BF)
        wires.start(12 + n, send_ref.at[spans[n]], landing.at[spans[n]], over_x)
    for n in range(3, 6):
        loads[n].wait()
    a, b = a_ref[...], b_ref[...]
    own, other = pl.ds(0, rows), pl.ds(rows, rows)

    def weight_grad(h, n):
        if n == 0:
            grad = dot(a, dq_ref[h], TN)
        else:
            ref = dk_ref if n == 1 else dv_ref
            grad = dot(a, ref[h, own], TN) + dot(b, ref[h, other], TN)
        gw[h, :, :, :, :, columns(n)] = grad.astype(BF).reshape(4, 2, 2, -1, half)

    def with_sibling(h, slot):
        wires.arrive(slot, sib.at[h])

        def sweep(m, _):
            add_into(gw.at[h, m // 2, lax.rem(m, 2), c], sib.at[h, m // 2, lax.rem(m, 2)])
            return 0

        lax.fori_loop(0, 8, sweep, 0)

    for n in range(3):
        weight_grad(1 - x, n)
    wires.start(14, gw.at[1 - x, :, :, 1 - c], sib.at[1 - x], sibling)
    weight_grad(x, 0)
    weight_grad(x, 1)
    with_sibling(1 - x, 14)
    order = (1, 2, 3, 0)
    for k in order:
        wires.start(16 + k, gw.at[1 - x, ahead(k), 1 - y, c], diag.at[ahead(k)], over_y)
    weight_grad(x, 2)
    wires.start(15, gw.at[x, :, :, 1 - c], sib.at[x], sibling)
    da = None
    for h in range(2):
        part = (
            dot(dq_ref[h], w_ref[h, :, columns(0)], NT)
            + dot(dk_ref[h, own], w_ref[h, :, columns(1)], NT)
            + dot(dv_ref[h, own], w_ref[h, :, columns(2)], NT)
        )
        da = part if da is None else da + part
    da_ref[...] = da
    with_sibling(x, 15)
    wires.start(24, gw.at[x, :, 1 - y, c], side.at[1], over_y)
    for k in order:
        wires.arrive(16 + k, diag.at[ahead(k)])
        part = gw.at[1 - x, ahead(k), y, c]
        add_into(part, diag.at[ahead(k)])
        wires.start(20 + k, part, side.at[0, ahead(k)], over_x)
    held[0] = jnp.zeros(held.shape[1:], F32)
    for h in range(2):
        held[0, 2:3, columns(h)] = jnp.sum(dq_ref[h].astype(F32), axis=0, keepdims=True)
        held[0, 3:4, columns(h)] = jnp.sum(dv_ref[h].astype(F32), axis=0, keepdims=True)
    held[0, 4:7] = tail_ref[0:3]
    held[0, 7:11] = tail_ref[4:8]
    held[0, 11:12] = tail_ref[3:4]
    for n in (1, 2, 3):
        settle(n, lined[n - 1][z])
        squares = add_squares(squares, n, ...)
    for n in range(6, 8):
        loads[n].wait()
    tubes = tubes_of(patch_ref, mask_ref, token_ref)
    centred = tubes - mean_rows(tubes)
    scale = lax.rsqrt(mean_rows(centred * centred) + 1e-6)
    xh = centred * scale
    for n in range(2):
        wires.arrive(12 + n, landing.at[spans[n]])
    da = da_ref[...] + landing[...].astype(F32)
    held[0, 0:1] = jnp.sum(da * xh, axis=0, keepdims=True)
    held[0, 1:2] = jnp.sum(da, axis=0, keepdims=True)
    e = da * vec_ref[0:1]
    dx = dx1_ref[...] + scale * (e - mean_rows(e) - xh * mean_rows(e * xh))
    masked = mask_ref[...] > 0
    pg_ref[...] = jnp.where(masked, 0.0, dx).astype(BF)
    held[0, 12:13] = jnp.sum(jnp.where(masked, dx, 0.0), axis=0, keepdims=True)
    wires.start(25, held.at[0], came.at[0], sibling)
    wires.arrive(24, side.at[1])

    def with_sides(k):
        wires.arrive(20 + k, side.at[0, ahead(k)])
        both = side[0, ahead(k)].astype(F32) + side[1, ahead(k)].astype(F32)
        part = gw.at[x, ahead(k), y, c]
        part[...] = (part[...].astype(F32) + both).astype(BF)
        if k:
            wires.start(k - 1, part, far[0].at[k - 1], lines[k - 1])

    with_sides(1)
    wires.arrive(25, came.at[0])
    held[1] = held[0] + came[0]
    wires.start(26, held.at[1], came.at[1], over_x)
    with_sides(2)
    wires.arrive(26, came.at[1])
    held[2] = held[1] + came[1]
    wires.start(27, held.at[2], came.at[2], over_y)
    with_sides(3)
    with_sides(0)
    wires.arrive(27, came.at[2])
    final[z] = held[2] + came[2]
    for k in (1, 2, 3):
        wires.start(27 + k, final.at[z], final.at[z], lines[k - 1])
    settle(0, gw[x, z, y, c])
    for part in range(3):
        squares = add_squares(squares, 0, part)
    me = x * 4 + y * 2 + c
    square_ref[me] = squares
    for code in range(1, 8):
        wires.start(30 + code, square_ref.at[me], square_ref.at[me], flipped(code))
    for k in (1, 2, 3):
        wires.arrive(27 + k, final.at[ahead(4 - k)])
    vtotal_ref[...] = final[0] + final[1] + final[2] + final[3]

    def flip_index(code):
        return sum((1 - v if bit else v) * w for v, bit, w in ((x, code // 4, 4), (y, code // 2 % 2, 2), (c, code % 2, 1)))

    for code in range(1, 8):
        wires.arrive(30 + code, square_ref.at[flip_index(code)])
    total = square_ref[0]
    for n in range(1, 8):
        total = total + square_ref[n]
    square_line[z] = total
    for k in (1, 2, 3):
        wires.start(37 + k, square_line.at[z], square_line.at[z], lines[k - 1])
    for k in (1, 2, 3):
        wires.arrive(37 + k, square_line.at[ahead(4 - k)])
    stotal_ref[...] = square_line[0] + square_line[1] + square_line[2] + square_line[3]
    wires.drain()


def last(a, b, dq, dk, dv, wa, patches, mask, token, vectors, tail, dx1, lined, masters, firsts, seconds):
    rows, width = a.shape
    own_rows = lined[0].shape[1]
    widths = [wa.shape[2], *[t.shape[2] for t in lined]]
    w = widths[0]
    big = [dk, dv, wa, a, b, dq, patches, dx1]
    return pl.pallas_call(
        last_kernel,
        out_shape=[
            jax.ShapeDtypeStruct((rows, width), BF),
            jax.ShapeDtypeStruct((16, width), F32),
            jax.ShapeDtypeStruct((8, PAIR), F32),
            *[jax.ShapeDtypeStruct(m.shape, F32) for m in masters],
        ],
        in_specs=[anywhere()] * 8 + [in_vmem()] * 19,
        out_specs=[in_vmem()] * 7,
        scratch_shapes=[
            *[pltpu.VMEM(v.shape, v.dtype) for v in big],
            pltpu.VMEM((2, 4, 2, 2, own_rows, w), BF),
            pltpu.VMEM((2, 4, 2, own_rows, w), BF),
            pltpu.VMEM((4, own_rows, w), BF),
            pltpu.VMEM((2, 4, own_rows, w), BF),
            pltpu.VMEM((rows, width), F32),
            pltpu.VMEM((rows, width), BF),
            pltpu.VMEM((rows, width), BF),
            *[pltpu.VMEM((3, own_rows, n), BF) for n in widths],
            pltpu.VMEM((3, 16, width), F32),
            pltpu.VMEM((3, 16, width), F32),
            pltpu.VMEM((4, 16, width), F32),
            pltpu.VMEM((8, 8, PAIR), F32),
            pltpu.VMEM((4, 8, PAIR), F32),
            pltpu.SemaphoreType.DMA((8,)),
            pltpu.SemaphoreType.DMA((41,)),
            pltpu.SemaphoreType.DMA((41,)),
        ],
        compiler_params=params(collective_id=1, has_side_effects=True),
        name="last",
    )(*big, mask, token, vectors, tail, *lined, *masters, *firsts, *seconds)


def lamb_kernel(*refs):
    masters, firsts, seconds, totals = (refs[4 * n : 4 * n + 4] for n in range(4))
    grad_ref, square_ref, vec_ref, vfirst_ref, vsecond_ref = refs[16:21]
    moments, squares, weights, copies = (refs[21 + 4 * n : 25 + 4 * n] for n in range(4))
    token_ref, bias_ref, vm_ref, vs_ref, vw_ref, norm_ref = refs[37:43]
    norms = jnp.sqrt(square_ref[0:1])
    for n in range(4):
        size, length = norms[:, 2 * n : 2 * n + 1], norms[:, 2 * n + 1 : 2 * n + 2]
        norm_ref[n : n + 1, 0:1] = size
        norm_ref[n : n + 1, 1:2] = length
        step = 0.5 * size / (length + 1e-06)
        for pick in range(3) if n == 0 else (...,):
            weight = masters[n][pick]
            moment, square, update = lamb_parts(weight, firsts[n][pick], seconds[n][pick], totals[n][pick])
            moments[n][pick] = moment
            squares[n][pick] = square
            renewed = weight - step * update
            weights[n][pick] = renewed
            copies[n][pick] = renewed.astype(BF)
    vectors = vec_ref[...]
    moment, square, update = lamb_parts(vectors, vfirst_ref[...], vsecond_ref[...], grad_ref[0:12])
    vm_ref[...] = moment
    vs_ref[...] = square
    size = jnp.sqrt(jnp.sum(vectors * vectors, axis=-1, keepdims=True))
    length = jnp.sqrt(jnp.sum(update * update, axis=-1, keepdims=True))
    vw_ref[...] = vectors - 0.5 * size / (length + 1e-06) * update
    token_ref[...] = grad_ref[12:13].reshape(token_ref.shape)
    bias_ref[...] = grad_ref[11:12].reshape(bias_ref.shape)


def lamb(masters, firsts, seconds, totals, grad, squares, vectors, vfirst, vsecond):
    full = [jax.ShapeDtypeStruct(m.shape, F32) for m in masters]
    flat = jax.ShapeDtypeStruct((vectors.shape[1],), F32)
    like = jax.ShapeDtypeStruct(vectors.shape, F32)
    return pl.pallas_call(
        lamb_kernel,
        out_shape=[
            *full,
            *full,
            *full,
            *[jax.ShapeDtypeStruct(m.shape, BF) for m in masters],
            flat,
            flat,
            like,
            like,
            like,
            jax.ShapeDtypeStruct((4, 2), F32),
        ],
        in_specs=[in_vmem()] * 21,
        out_specs=[in_vmem()] * 22,
        compiler_params=params(),
        name="lamb",
    )(*masters, *firsts, *seconds, *totals, grad, squares, vectors, vfirst, vsecond)


def lamb_terms(weight, moment, square, gradient):
    moment_new = 0.5 * moment + 0.5 * gradient
    square_new = 0.5 * square + 0.5 * gradient * gradient
    correct = 1.0 - 0.5**STEP
    update = moment_new / correct / (jnp.sqrt(square_new / correct) + 1e-06) + 0.01 * weight
    return (
        moment_new,
        square_new,
        update,
        jnp.stack([jnp.sum(weight * weight), jnp.sum(update * update)]),
    )


def lamb_apply(weight, update, norms):
    renewed = weight - 0.5 * norms[0] / (norms[1] + 1e-06) * update
    return (renewed, renewed.astype(BF))


def per_device(
    patches,
    cube_mask,
    mask_token,
    cotangent,
    vectors,
    vector_first,
    vector_second,
    attend_master,
    attend_first,
    attend_second,
    mixing_master,
    mixing_first,
    mixing_second,
    expand_master,
    expand_first,
    expand_second,
    shrink_master,
    shrink_first,
    shrink_second,
):
    clips, rows, width = patches.shape
    axis = lax.axis_size("dp")
    own_rows = attend_master.shape[0]
    direct = axis == 16 and lax.axis_size("mp") == 2
    dy = cotangent[0]

    def lead(v):
        return v.transpose(1, 0, 2)

    if direct:
        masters = [lead(attend_master), mixing_master, expand_master, shrink_master]
        firsts = [lead(attend_first), mixing_first, expand_first, shrink_first]
        seconds = [lead(attend_second), mixing_second, expand_second, shrink_second]
        *wholes, q, k, v, a1, a1_other, mask = first(masters, patches[0], cube_mask, mask_token, vectors)
        wa = wholes[0].reshape(2, width, -1)
        o, o_low, inv, p, *rest = attend(q, k, v, wholes[1:])
        wm, we, ws = (w.reshape(2, width, -1) for w in rest)
        block_out, dx1, do, gm, ge, gs, tail = middle(
            patches[0], mask, mask_token, o_low, inv, dy, vectors, wm, we, ws
        )
        dq, dk, dv, ts, te, tm = attend_back(q, k, v, do, o, p, [gs, ge, gm], own_rows)
        patch_grad, grad, squares, *totals = last(
            a1,
            a1_other,
            dq,
            dk,
            dv,
            wa,
            patches[0],
            mask,
            mask_token,
            vectors,
            tail,
            dx1,
            [tm, te, ts],
            masters,
            firsts,
            seconds,
        )
        done = lamb(masters, firsts, seconds, totals, grad, squares, vectors, vector_first, vector_second)
        results = []
        for n in range(4):
            group = [done[n], done[4 + n], done[8 + n], done[12 + n]]
            results.extend([lead(g) for g in group] if n == 0 else group)
        return (block_out[None], patch_grad[None], done[16], done[17], *results, *done[18:])
    masters = [attend_master.reshape(own_rows, -1), mixing_master, expand_master, shrink_master]
    firsts = [attend_first.reshape(own_rows, -1), mixing_first, expand_first, shrink_first]
    seconds = [attend_second.reshape(own_rows, -1), mixing_second, expand_second, shrink_second]
    shards = [m.astype(BF) for m in masters]
    mask, token = cube_mask.reshape(rows, 1).astype(F32), mask_token[None]
    swap = [(0, 1), (1, 0)]
    chosen = mask > 0
    x = jnp.where(chosen, token, patches[0].astype(F32))
    centred = x - mean_rows(x)
    scale = lax.rsqrt(mean_rows(centred * centred) + 1e-6)
    wa, wm, we, ws = (
        lax.all_gather(lax.all_gather(s, "dp", axis=0, tiled=True), "mp", axis=0) for s in shards
    )
    a1 = (centred * scale * vectors[0] + vectors[1]).astype(BF)
    a1_other = lax.ppermute(a1, "mp", swap)
    q, k, v = project(a1, a1_other, wa, vectors[2:4])
    o, o_low, inv, p = attend(q, k, v, [])
    block_out, dx1, do, gm, ge, gs, gv = middle(
        patches[0], mask, mask_token, o_low, inv, dy, vectors, wm, we, ws
    )
    dq, dk, dv = attend_back(q, k, v, do, o, p, [], own_rows)
    da1, da1_send, ga, gqv = unproject(a1, a1_other, dq, dk, dv, wa)
    da1 = da1 + lax.ppermute(da1_send, "mp", swap).astype(F32)
    totals = []
    for g in (ga, gm, ge, gs):
        g = lax.psum_scatter(g, "mp", scatter_dimension=0, tiled=True)
        totals.append(lax.psum_scatter(g[0].astype(F32), "dp", scatter_dimension=0, tiled=True))
    xh = centred * scale
    e = da1 * vectors[0]
    dx = dx1 + scale * (e - mean_rows(e) - xh * mean_rows(e * xh))
    patch_grad = jnp.where(chosen, 0.0, dx).astype(BF)
    token_part = jnp.sum(jnp.where(chosen, dx, 0.0), axis=0)
    vector_part = jnp.concatenate(
        [
            jnp.sum(da1 * xh, axis=0)[None],
            jnp.sum(da1, axis=0)[None],
            gqv[0:2],
            gv[0:3],
            gv[4:8],
            gv[3:4],
        ],
        axis=0,
    )
    terms = [lamb_terms(w, m, s, g) for w, m, s, g in zip(masters, firsts, seconds, totals)]
    squares = jnp.stack([t[3] for t in terms])
    vector_total, token_grad, square_total = lax.psum(
        (vector_part, token_part, squares), ("dp", "mp")
    )
    trust_norms = jnp.sqrt(square_total)
    results = []
    for n, (w, t) in enumerate(zip(masters, terms)):
        group = [t[0], t[1], *lamb_apply(w, t[2], trust_norms[n])]
        if n == 0:
            group = [g.reshape(attend_master.shape) for g in group]
        results.extend(group)
    vector_moment = 0.5 * vector_first + 0.5 * vector_total
    vector_square = 0.5 * vector_second + 0.5 * vector_total * vector_total
    correct = 1.0 - 0.5**STEP
    vector_update = (
        vector_moment / correct / (jnp.sqrt(vector_square / correct) + 1e-06) + 0.01 * vectors
    )
    row_weight = jnp.sqrt(jnp.sum(vectors * vectors, axis=-1, keepdims=True))
    row_update = jnp.sqrt(jnp.sum(vector_update * vector_update, axis=-1, keepdims=True))
    vector_weight = vectors - 0.5 * row_weight / (row_update + 1e-06) * vector_update
    return (
        block_out[None],
        patch_grad[None],
        token_grad,
        vector_total[11],
        *results,
        vector_moment,
        vector_square,
        vector_weight,
        trust_norms,
    )


def solution(mesh):
    rows = P("dp", "mp", None)
    flat = P("dp", "mp")
    deep = P("dp", None, "mp")
    copied = P()
    return jax.shard_map(
        per_device,
        mesh=mesh,
        in_specs=(rows, flat, copied, rows, copied, copied, copied, *[deep] * 3, *[flat] * 9),
        out_specs=(rows, rows, copied, copied, *[deep] * 4, *[flat] * 12, *[copied] * 4),
        check_vma=False,
    )
```

```python
import functools

import jax
import jax.numpy as jnp
from jax import lax
from jax.experimental import pallas as pl
from jax.experimental.pallas import tpu as pltpu
from jax.sharding import PartitionSpec as P

HD = 64
PAIR = 2 * HD
STEP = 5
BF = jnp.bfloat16
F32 = jnp.float32
NN = (((1,), (0,)), ((), ()))
NT = (((1,), (1,)), ((), ()))
TN = (((0,), (0,)), ((), ()))
LOG2E = 1.4426950408889634
MESH = pl.DeviceIdType.MESH
VMEM_LIMIT = 60 * 2**20


def dot(a, b, dims=NN):
    return lax.dot_general(a, b, dims, preferred_element_type=F32)


def params(**kw):
    return pltpu.CompilerParams(vmem_limit_bytes=VMEM_LIMIT, **kw)


def anywhere():
    return pl.BlockSpec(memory_space=pl.ANY)


def in_vmem():
    return pl.BlockSpec(memory_space=pltpu.VMEM)


def place():
    dp, x = lax.axis_index("dp"), lax.axis_index("mp")
    return x, dp // 4, lax.rem(dp // 2, 2), lax.rem(dp, 2)


def device(x, z, y, c):
    return ((z * 2 + y) * 2 + c, x)


def neighbours():
    x, z, y, c = place()
    lines = [device(x, lax.rem(z + k, 4), y, c) for k in (1, 2, 3)]
    return lines, device(1 - x, z, y, c), device(x, z, 1 - y, c), device(x, z, y, 1 - c)


def greet():
    lines, over_x, over_y, sibling = neighbours()
    barrier = pltpu.get_barrier_semaphore()
    for other in (*lines, over_x, over_y, sibling):
        pl.semaphore_signal(barrier, inc=1, device_id=other, device_id_type=MESH)
    pl.semaphore_wait(barrier, 6)


class Wires:
    def __init__(self, send_sem, recv_sem):
        self.send_sem, self.recv_sem = send_sem, recv_sem
        self.started = []

    def copy(self, slot, src, dst, other):
        return pltpu.make_async_remote_copy(
            src_ref=src,
            dst_ref=dst,
            send_sem=self.send_sem.at[slot],
            recv_sem=self.recv_sem.at[slot],
            device_id=other,
            device_id_type=MESH,
        )

    def start(self, slot, src, dst, other):
        self.copy(slot, src, dst, other).start()
        self.started.append((slot, src))

    def send(self, slot, whole, part, other):
        self.copy(slot, whole.at[part], whole.at[part], other).start()
        self.started.append((slot, whole, part))

    def arrive(self, slot, dst):
        x, z, y, c = place()
        self.copy(slot, dst, dst, device(x, z, y, 1 - c)).wait_recv()

    def sent(self, slot, src):
        x, z, y, c = place()
        self.copy(slot, src, src, device(x, z, y, 1 - c)).wait_send()

    def drain(self):
        for slot, src, *part in self.started:
            self.sent(slot, src.at[part[0]] if part else src)


ALL = slice(None)


def greet_near():
    _, *near = neighbours()
    barrier = pltpu.get_barrier_semaphore()
    for other in near:
        pl.semaphore_signal(barrier, inc=1, device_id=other, device_id_type=MESH)
    pl.semaphore_wait(barrier, 3)


def first_kernel(*refs):
    masters, (patch_ref, flag_ref, token_ref, vec_ref) = refs[:4], refs[4:8]
    wa_out, wm, we, ws, q_out, k_out, v_out, a1_out, other_out, mask_ref = refs[8:18]
    wa, landing, a1_ref, q_ref, k_ref, v_ref, sa, sm, se, ss, own_sem, put_sem, send_sem, recv_sem = refs[18:]
    x, z, y, c = place()
    lines, over_x, over_y, sibling = neighbours()
    wires = Wires(send_sem, recv_sem)
    rows = a1_ref.shape[0]
    cut = rows // 64 * 16
    halves = (pl.ds(0, cut), pl.ds(cut, rows - cut))
    width = wa.shape[-1] // 3
    for n in range(3):
        sa[:, n * width : (n + 1) * width] = masters[0][n].astype(BF)
    for shard, master in zip((sm, se, ss), masters[1:]):
        shard[...] = master[...].astype(BF)
    puts = []

    def put(src, dst):
        copy = pltpu.make_async_copy(src, dst, put_sem.at[len(puts)])
        copy.start()
        puts.append(copy)

    greet()

    def back(k):
        return lax.rem(z + 4 - k, 4)

    own = [pltpu.make_async_copy(sa, wa.at[x, z, y, c], own_sem.at[0])]
    for n, (shard, whole) in enumerate(((sm, wm), (se, we), (ss, ws))):
        own.append(pltpu.make_async_copy(shard, whole.at[x, z, y, c], own_sem.at[n + 1]))
    for copy in own:
        copy.start()
    for k in (1, 2, 3):
        wires.start(k - 1, sa, wa.at[x, z, y, c], lines[k - 1])
    wires.start(3, sa, wa.at[x, z, y, c], over_x)
    wires.start(7, sa, wa.at[x, z, y, c], over_y)
    others = ((sm, wm), (se, we), (ss, ws))
    for n in range(2):
        shard, whole = others[n]
        wires.start(30 + 4 * n, shard, whole.at[x, z, y, c], over_y)

    flags = jnp.broadcast_to(flag_ref[...].astype(F32), (PAIR, rows))
    mask_ref[...] = flags.T[:, :1]
    tubes = tubes_of(patch_ref, mask_ref, token_ref)
    centred = tubes - mean_rows(tubes)
    scale = lax.rsqrt(mean_rows(centred * centred) + 1e-6)
    a1_ref[...] = (centred * scale * vec_ref[0:1] + vec_ref[1:2]).astype(BF)
    wires.start(19, a1_ref.at[halves[0]], landing.at[halves[0]], over_x)
    put(a1_ref, a1_out)

    for k in (1, 2, 3):
        part = wa.at[x, back(k), y, c]
        wires.arrive(k - 1, part)
        wires.start(3 + k, part, part, over_x)
        wires.start(7 + k, part, part, over_y)
    for copy in own:
        copy.wait()
    line = wa.at[x, ALL, y, c]
    wires.start(15, line, line, sibling)
    wires.start(20, a1_ref.at[halves[1]], landing.at[halves[1]], over_x)
    for n, (shard, whole) in enumerate(others):
        for k in (1, 2, 3):
            wires.start(21 + 3 * n + k - 1, shard, whole.at[x, z, y, c], lines[k - 1])
    for k in range(4):
        part = wa.at[1 - x, back(k), y, c]
        wires.arrive(3 + k, part)
        wires.start(11 + k, part, part, over_y)
    line = wa.at[1 - x, ALL, y, c]
    wires.start(16, line, line, sibling)
    for k in range(4):
        wires.arrive(7 + k, wa.at[x, back(k), 1 - y, c])
    line = wa.at[x, ALL, 1 - y, c]
    wires.start(17, line, line, sibling)

    def pass_on(n):
        whole = others[n][1]
        for k in (1, 2, 3):
            part = whole.at[x, back(k), y, c]
            wires.arrive(21 + 3 * n + k - 1, part)
            wires.start(30 + 4 * n + k, part, part, over_y)

    for k in range(4):
        wires.arrive(11 + k, wa.at[1 - x, back(k), 1 - y, c])
    line = wa.at[1 - x, ALL, 1 - y, c]
    wires.start(18, line, line, sibling)
    pass_on(0)
    for n, (i, j) in enumerate(((x, y), (1 - x, y), (x, 1 - y), (1 - x, 1 - y))):
        wires.arrive(15 + n, wa.at[i, ALL, j, 1 - c])
    out_copy = pltpu.make_async_copy(wa, wa_out, own_sem.at[0])
    out_copy.start()

    depth = a1_ref.shape[1]

    def weight(h, n):
        return wa[h, :, :, :, :, n * width : (n + 1) * width].reshape(depth, width)

    def keys_values(h, source, span):
        k_ref[h, span] = dot(source, weight(h, 1)).astype(BF)
        values = dot(source, weight(h, 2)) + vec_ref[3:4, h * width : (h + 1) * width]
        v_ref[h, span] = values.astype(BF)

    for h in range(2):
        queries = dot(a1_ref[...], weight(h, 0)) + vec_ref[2:3, h * width : (h + 1) * width]
        q_ref[h] = (queries.astype(BF).astype(F32) * HD**-0.5).astype(BF)
        put(q_ref.at[h], q_out.at[h])
        keys_values(h, a1_ref[...], pl.ds(0, rows))
        for ref, out in ((k_ref, k_out), (v_ref, v_out)):
            put(ref.at[h, pl.ds(0, rows)], out.at[h, pl.ds(0, rows)])
    pass_on(1)
    for n in range(2):
        wires.arrive(19 + n, landing.at[halves[n]])
        part = landing[halves[n]]
        put(landing.at[halves[n]], other_out.at[halves[n]])
        span = pl.ds(rows + (cut if n else 0), part.shape[0])
        for h in range(2):
            keys_values(h, part, span)
            for ref, out in ((k_ref, k_out), (v_ref, v_out)):
                put(ref.at[h, span], out.at[h, span])
    for n in range(2):
        for k in range(4):
            wires.arrive(30 + 4 * n + k, others[n][1].at[x, back(k), 1 - y, c])
    for k in (1, 2, 3):
        wires.arrive(27 + k - 1, ws.at[x, back(k), y, c])
    out_copy.wait()
    for copy in puts:
        copy.wait()
    wires.drain()


def first(masters, patches, flags, token, vectors):
    rows, width = patches.shape
    half = width // 2
    own_rows = masters[1].shape[0]
    shards = [(own_rows, 3 * half), *[m.shape for m in masters[1:]]]
    gathered = [(2, 4, 2, 2, *s) for s in shards]
    wholes = [jax.ShapeDtypeStruct(g, BF) for g in gathered]
    keys = jax.ShapeDtypeStruct((2, 2 * rows, half), BF)
    flat = jax.ShapeDtypeStruct((rows, width), BF)
    return pl.pallas_call(
        first_kernel,
        out_shape=[
            *wholes,
            jax.ShapeDtypeStruct((2, rows, half), BF),
            keys,
            keys,
            flat,
            flat,
            jax.ShapeDtypeStruct((rows, 1), F32),
        ],
        in_specs=[in_vmem()] * 8,
        out_specs=[anywhere()] * 9 + [in_vmem()],
        scratch_shapes=[
            pltpu.VMEM(gathered[0], BF),
            pltpu.VMEM((rows, width), BF),
            pltpu.VMEM((rows, width), BF),
            pltpu.VMEM((2, rows, half), BF),
            pltpu.VMEM((2, 2 * rows, half), BF),
            pltpu.VMEM((2, 2 * rows, half), BF),
            *[pltpu.VMEM(s, BF) for s in shards],
            pltpu.SemaphoreType.DMA((4,)),
            pltpu.SemaphoreType.DMA((17,)),
            pltpu.SemaphoreType.DMA((38,)),
            pltpu.SemaphoreType.DMA((38,)),
        ],
        compiler_params=params(collective_id=0, has_side_effects=True),
        name="first",
    )(*masters, patches, flags, token, vectors)


def add_into(dst, other):
    dst[...] = (dst[...].astype(F32) + other[...].astype(F32)).astype(BF)


def project_kernel(mine_ref, other_ref, w_ref, bias_ref, q_ref, k_ref, v_ref):
    rows = mine_ref.shape[0]
    half = w_ref.shape[2] // 3
    for h in range(2):
        cols = slice(h * half, (h + 1) * half)
        queries = dot(mine_ref[...], w_ref[h, :, :half]) + bias_ref[0:1, cols]
        q_ref[h] = (queries.astype(BF).astype(F32) * HD**-0.5).astype(BF)
        for part, ref in ((0, mine_ref), (1, other_ref)):
            span = slice(part * rows, (part + 1) * rows)
            k_ref[h, span] = dot(ref[...], w_ref[h, :, half : 2 * half]).astype(BF)
            v_ref[h, span] = (dot(ref[...], w_ref[h, :, 2 * half :]) + bias_ref[1:2, cols]).astype(BF)


def project(mine, other, weight, bias):
    rows, width = mine.shape
    keys = jax.ShapeDtypeStruct((2, 2 * rows, width // 2), BF)
    return pl.pallas_call(
        project_kernel,
        out_shape=[jax.ShapeDtypeStruct((2, rows, width // 2), BF), keys, keys],
        in_specs=[in_vmem()] * 4,
        out_specs=[in_vmem()] * 3,
        compiler_params=params(),
        name="project",
    )(mine, other, weight, bias)


def half_lanes():
    lane = lax.broadcasted_iota(jnp.int32, (1, PAIR), 1)
    return lane < HD, lane >= HD


def row_blocks(rows):
    cut = (rows // 2 + 15) // 16 * 16
    return ((0, cut), (cut, rows))


def key_parts(keys):
    cut = keys // 2 // 256 * 256
    return ((0, cut), (cut, keys))


def attend_pair(q_ref, k_ref, v_ref, o_ref, low_ref, inv_ref, p_ref):
    sides = half_lanes()
    k, v = k_ref[0], v_ref[0]
    parts = key_parts(k.shape[0])
    for a, b in row_blocks(q_ref.shape[1]):
        q = q_ref[0, a:b]
        outs, invs = [], []
        for h in range(2):
            q_h = jnp.where(sides[h], q, jnp.zeros_like(q))
            v_h = jnp.where(sides[h], v, jnp.ones_like(v))
            scores = [dot(q_h, k[c:d], NT) for c, d in parts]
            tops = [jnp.max(s, axis=-1, keepdims=True) for s in scores]
            top = functools.reduce(jnp.maximum, tops) * LOG2E
            out = None
            for s, (c, d) in zip(scores, parts):
                p = jnp.exp2(s * LOG2E - top).astype(BF)
                p_ref[h, a:b, c:d] = p
                more = dot(p, v_h[c:d])
                out = more if out is None else out + more
            spare = HD if h == 0 else 0
            inv = 1.0 / out[:, spare : spare + 1]
            outs.append(out * inv)
            invs.append(inv)
        o = jnp.where(sides[0], *outs)
        o_ref[0, a:b] = o
        low_ref[0, a:b] = o.astype(BF)
        inv_ref[0, a:b] = jnp.where(sides[0], *invs)


def attend_kernel(*refs):
    outs, (wm, we, ws, send_sem, recv_sem) = refs[6:10], refs[10:]
    i = pl.program_id(0)
    x, z, y, c = place()
    lines, over_x, over_y, sibling = neighbours()
    wires = Wires(send_sem, recv_sem)
    here, side, flank, across = (x, ALL, y, c), (1 - x, ALL, y, c), (x, ALL, 1 - y, c), (1 - x, ALL, 1 - y, c)
    low, high = pl.ds(0, 2), pl.ds(2, 2)
    near_here, far_here = (x, low, y, c), (x, high, y, c)
    near_side, far_side = (1 - x, low, y, c), (1 - x, high, y, c)
    near_across, far_across = (1 - x, low, 1 - y, c), (1 - x, high, 1 - y, c)

    send = wires.send

    @pl.when(i == 0)
    def _():
        greet_near()
        send(0, we, near_here, over_x)
        send(15, we, far_here, over_x)
        send(1, ws, here, over_y)
        send(2, wm, here, over_x)
        send(3, wm, flank, over_x)
        send(4, wm, here, sibling)
        send(5, wm, flank, sibling)
        send(6, we, here, sibling)
        send(7, we, flank, sibling)
        send(8, ws, here, sibling)

    @pl.when(i == 2)
    def _():
        wires.arrive(0, we.at[near_side])
        send(9, we, near_side, over_y)

    @pl.when(i == 4)
    def _():
        wires.arrive(15, we.at[far_side])
        send(16, we, far_side, over_y)
        send(10, we, side, sibling)
        wires.arrive(1, ws.at[flank])
        send(11, ws, flank, sibling)

    @pl.when(i == 5)
    def _():
        wires.arrive(2, wm.at[side])
        send(12, wm, side, sibling)

    attend_pair(*refs[:3], *outs)

    @pl.when(i == pl.num_programs(0) - 1)
    def _():
        wires.arrive(3, wm.at[across])
        send(13, wm, across, sibling)
        wires.arrive(9, we.at[near_across])
        wires.arrive(16, we.at[far_across])
        send(14, we, across, sibling)
        for slot, whole, (a, b) in (
            (4, wm, (x, y)),
            (5, wm, (x, 1 - y)),
            (6, we, (x, y)),
            (7, we, (x, 1 - y)),
            (8, ws, (x, y)),
            (10, we, (1 - x, y)),
            (11, ws, (x, 1 - y)),
            (12, wm, (1 - x, y)),
            (13, wm, (1 - x, 1 - y)),
            (14, we, (1 - x, 1 - y)),
        ):
            wires.arrive(slot, whole.at[a, ALL, b, 1 - c])
        wires.drain()


def attend(q, k, v, wholes):
    _, rows, half = q.shape
    keys = k.shape[1]
    per = half // PAIR
    of_q = pl.BlockSpec((1, rows, PAIR), lambda i: (i // per, 0, lax.rem(i, per)))
    of_k = pl.BlockSpec((1, keys, PAIR), lambda i: (i // per, 0, lax.rem(i, per)))
    shapes = [
        jax.ShapeDtypeStruct(q.shape, F32),
        jax.ShapeDtypeStruct(q.shape, BF),
        jax.ShapeDtypeStruct(q.shape, F32),
        jax.ShapeDtypeStruct((4 * per, rows, keys), BF),
    ]
    of_p = pl.BlockSpec((2, rows, keys), lambda i: (i, 0, 0))
    common = dict(grid=(2 * per,), name="attend")
    if not wholes:
        return pl.pallas_call(
            attend_pair,
            in_specs=[of_q, of_k, of_k],
            out_specs=[of_q, of_q, of_q, of_p],
            out_shape=shapes,
            compiler_params=params(),
            **common,
        )(q, k, v)
    return pl.pallas_call(
        attend_kernel,
        in_specs=[of_q, of_k, of_k, *[anywhere()] * 3],
        out_specs=[of_q, of_q, of_q, of_p, *[anywhere()] * 3],
        out_shape=[*shapes, *[jax.ShapeDtypeStruct(w.shape, BF) for w in wholes]],
        input_output_aliases={3: 4, 4: 5, 5: 6},
        scratch_shapes=[pltpu.SemaphoreType.DMA((17,)), pltpu.SemaphoreType.DMA((17,))],
        compiler_params=params(collective_id=2, has_side_effects=True),
        **common,
    )(q, k, v, *wholes)


def attend_back_pair(q_ref, k_ref, v_ref, do_ref, o_ref, p_ref, dq_ref, dk_ref, dv_ref):
    sides = half_lanes()
    k, v = k_ref[0], v_ref[0]
    parts = key_parts(k.shape[0])
    grad_k = [[None] * 2 for _ in parts]
    grad_v = [[None] * 2 for _ in parts]

    def plus(total, more):
        return more if total is None else total + more

    for a, b in row_blocks(q_ref.shape[1]):
        q, do = q_ref[0, a:b], do_ref[0, a:b]
        prod = do.astype(F32) * o_ref[0, a:b]
        q_t, do_t = q.T, do.T
        outs = []
        for h in range(2):
            do_h = jnp.where(sides[h], do, jnp.zeros_like(do))
            row_dot = jnp.sum(jnp.where(sides[h], prod, 0.0), axis=-1, keepdims=True)
            out = None
            rows = slice(h * HD, (h + 1) * HD)
            for n, (c, d) in enumerate(parts):
                p = p_ref[h, a:b, c:d]
                grad_p = dot(do_h, v[c:d], NT)
                ds = (p.astype(F32) * (grad_p - row_dot)).astype(BF)
                out = plus(out, dot(ds, k[c:d]))
                grad_k[n][h] = plus(grad_k[n][h], dot(q_t[rows], ds))
                grad_v[n][h] = plus(grad_v[n][h], dot(do_t[rows], p))
            outs.append(out)
        dq_ref[0, a:b] = (jnp.where(sides[0], *outs) * HD**-0.5).astype(BF)
    for n, (c, d) in enumerate(parts):
        dk_ref[0, c:d] = jnp.concatenate(grad_k[n], axis=0).T.astype(BF)
        dv_ref[0, c:d] = jnp.concatenate(grad_v[n], axis=0).T.astype(BF)


def attend_back_kernel(*refs):
    ins, (mine, early_side, early_far, grad_m) = refs[:6], refs[6:10]
    outs, total_s, total_e, total_m = refs[10:13], refs[13], refs[14], refs[15]
    here, away, side_y, side_x, diag = refs[16:21]
    zown, zfar, last_x, last_y, last_d = refs[21:26]
    here_m, sib_m, diag_m, side_m = refs[26:30]
    own_sem, send_sem, recv_sem = refs[30:]
    i = pl.program_id(0)
    x, z, y, c = place()
    lines, over_x, over_y, sibling = neighbours()
    over_xy = device(1 - x, z, 1 - y, c)
    wires = Wires(send_sem, recv_sem)
    width = here.shape[-1]

    def own():
        pairs = (
            (early_far, zfar.at[0]),
            (mine.at[:, :, 0, z], zown),
            (early_side, side_y),
            (mine.at[x, :, 1, :, y], here),
            (mine.at[1 - x, :, 1, :, y], away),
            (grad_m.at[:, :, :, c], here_m),
        )
        return [pltpu.make_async_copy(a, b, own_sem.at[n]) for n, (a, b) in enumerate(pairs)]

    def along_z(h, n):
        def sweep(m, _):
            b, j = m // 2, lax.rem(m, 2)
            total = zown[n, b, j].astype(F32)
            for k in range(3):
                total = total + zfar[h, b, k, j].astype(F32)
            zown[n, b, j] = total.astype(BF)
            return 0

        lax.fori_loop(0, 4, sweep, 0)

    def far_source(b, k):
        return mine.at[1 - x, b, 0, lax.rem(z + k, 4)]

    expand_diag = mine.at[1 - x, :, 1, :, 1 - y]

    @pl.when(i == 0)
    def _():
        copies = own()
        for copy in copies:
            copy.start()
        barrier = pltpu.get_barrier_semaphore()
        for other in (*lines, over_x, over_y, sibling, over_xy):
            pl.semaphore_signal(barrier, inc=1, device_id=other, device_id_type=MESH)
        pl.semaphore_wait(barrier, 7)
        wires.start(0, grad_m.at[:, :, :, 1 - c], sib_m, sibling)
        wires.start(1, expand_diag, diag, over_y)
        for b in range(2):
            for k in (1, 2, 3):
                wires.start(10 + 3 * b + k, far_source(b, k), zfar.at[1, b, k - 1], lines[k - 1])
        for copy in copies:
            copy.wait()
        along_z(0, x)

    @pl.when(i == 1)
    def _():
        wires.arrive(0, sib_m)

        def sweep(m, _):
            part = (m // 8, lax.rem(m // 2, 4), lax.rem(m, 2))
            add_into(here_m.at[part], sib_m.at[part])
            return 0

        lax.fori_loop(0, 16, sweep, 0)
        wires.start(2, here_m.at[1 - x, :, 1 - y], diag_m, over_y)
        wires.start(3, zown.at[x, :, 1 - y], last_y, over_y)
        wires.start(4, here_m.at[x, :, 1 - y], side_m.at[1], over_y)

    @pl.when(i == 3)
    def _():
        wires.arrive(1, diag)

        def sweep(m, _):
            add_into(away.at[m // 4, lax.rem(m, 4)], diag.at[m // 4, lax.rem(m, 4)])
            return 0

        lax.fori_loop(0, 8, sweep, 0)
        wires.start(5, away, side_x, over_x)

    @pl.when(i == 4)
    def _():
        wires.arrive(2, diag_m)

        def sweep(m, _):
            add_into(here_m.at[1 - x, m, y], diag_m.at[m])
            return 0

        lax.fori_loop(0, 4, sweep, 0)
        wires.start(6, here_m.at[1 - x, :, y], side_m.at[0], over_x)

    @pl.when(i == 5)
    def _():
        for b in range(2):
            for k in (1, 2, 3):
                wires.arrive(10 + 3 * b + k, zfar.at[1, b, k - 1])
        along_z(1, 1 - x)
        wires.start(7, zown.at[1 - x, :, y], last_x, over_x)
        wires.start(8, zown.at[1 - x, :, 1 - y], last_d, over_xy)

    attend_back_pair(*ins, *outs)

    @pl.when(i == pl.num_programs(0) - 1)
    def _():
        wires.arrive(5, side_x)

        def sweep(m, _):
            part = (m // 4, lax.rem(m, 4))
            both = side_x[part].astype(F32) + side_y[part].astype(F32)
            total_e[part] = (here[part].astype(F32) + both).astype(BF)
            return 0

        lax.fori_loop(0, 8, sweep, 0)
        wires.arrive(4, side_m.at[1])
        wires.arrive(6, side_m.at[0])
        for n in range(4):
            both = side_m[0, n].astype(F32) + side_m[1, n].astype(F32)
            total_m[n] = (here_m[x, n, y].astype(F32) + both).astype(BF)
        wires.arrive(3, last_y)
        wires.arrive(7, last_x)
        wires.arrive(8, last_d)
        for b in range(2):
            one = zown[x, b, y].astype(F32) + last_y[b].astype(F32)
            two = last_x[b].astype(F32) + last_d[b].astype(F32)
            total_s[:, b * width : (b + 1) * width] = one + two
        wires.sent(0, grad_m.at[:, :, :, 1 - c])
        wires.sent(1, expand_diag)
        wires.sent(2, here_m.at[1 - x, :, 1 - y])
        wires.sent(3, zown.at[x, :, 1 - y])
        wires.sent(4, here_m.at[x, :, 1 - y])
        wires.sent(5, away)
        wires.sent(6, here_m.at[1 - x, :, y])
        wires.sent(7, zown.at[1 - x, :, y])
        wires.sent(8, zown.at[1 - x, :, 1 - y])
        for b in range(2):
            for k in (1, 2, 3):
                wires.sent(10 + 3 * b + k, far_source(b, k))


def attend_back(q, k, v, do, o, p, grads):
    _, rows, half = q.shape
    keys = k.shape[1]
    per = half // PAIR
    of_q = pl.BlockSpec((1, rows, PAIR), lambda i: (i // per, 0, lax.rem(i, per)))
    of_k = pl.BlockSpec((1, keys, PAIR), lambda i: (i // per, 0, lax.rem(i, per)))
    of_p = pl.BlockSpec((2, rows, keys), lambda i: (i, 0, 0))
    shapes = [
        jax.ShapeDtypeStruct(q.shape, BF),
        jax.ShapeDtypeStruct(k.shape, BF),
        jax.ShapeDtypeStruct(k.shape, BF),
    ]
    common = dict(grid=(2 * per,), name="attend_back")
    if not grads:
        return pl.pallas_call(
            attend_back_pair,
            in_specs=[of_q, of_k, of_k, of_q, of_q, of_p],
            out_specs=[of_q, of_k, of_k],
            out_shape=shapes,
            compiler_params=params(),
            **common,
        )(q, k, v, do, o, p)
    mine, grad_m = grads[0], grads[3]
    parts, unit = mine.shape[1], mine.shape[5:]
    lined = (parts, 4, *unit)
    own_rows, w = grad_m.shape[4:]
    lined_m = (4, own_rows, w)
    totals = [
        jax.ShapeDtypeStruct((own_rows, parts * unit[1]), F32),
        jax.ShapeDtypeStruct(lined, BF),
        jax.ShapeDtypeStruct(lined_m, BF),
    ]
    return pl.pallas_call(
        attend_back_kernel,
        in_specs=[of_q, of_k, of_k, of_q, of_q, of_p, *[anywhere()] * 4],
        out_specs=[of_q, of_k, of_k, *[pl.BlockSpec(t.shape, lambda i, t=t: (0,) * t.ndim) for t in totals]],
        out_shape=[*shapes, *totals],
        scratch_shapes=[
            *[pltpu.VMEM(lined, BF)] * 5,
            pltpu.VMEM((2, parts, 2, *unit), BF),
            pltpu.VMEM((2, parts, 3, 2, *unit), BF),
            *[pltpu.VMEM((parts, *unit), BF)] * 3,
            pltpu.VMEM((2, 4, 2, own_rows, w), BF),
            pltpu.VMEM((2, 4, 2, own_rows, w), BF),
            pltpu.VMEM(lined_m, BF),
            pltpu.VMEM((2, *lined_m), BF),
            pltpu.SemaphoreType.DMA((6,)),
            pltpu.SemaphoreType.DMA((17,)),
            pltpu.SemaphoreType.DMA((17,)),
        ],
        compiler_params=params(collective_id=3, has_side_effects=True),
        **common,
    )(q, k, v, do, o, p, *grads)


def normal_parts(h):
    z = jnp.abs(h) * 0.7071067811865476
    t = 1.0 / (1.0 + 0.3275911 * z)
    bell = jnp.exp(-z * z)
    poly = t * (
        0.254829592
        + t * (-0.284496736 + t * (1.421413741 + t * (-1.453152027 + t * 1.061405429)))
    )
    tail = 0.5 * poly * bell
    return jnp.where(h < 0, tail, 1.0 - tail), bell * 0.3989422804014327


def mean_rows(values):
    return jnp.mean(values, axis=-1, keepdims=True)


def tubes_of(patch_ref, mask_ref, token_ref):
    return jnp.where(mask_ref[...] > 0, token_ref[...][None], patch_ref[...].astype(F32))


class Middle:
    def __init__(self, ins, outs, scratch):
        self.patch, self.mask, self.token, self.o, self.inv, self.dy, self.vec, self.wm = ins
        self.out, self.dx1, self.do, self.gm, self.gv = outs
        self.x1, self.a2, self.acc, self.da2 = scratch

    def open(self):
        x1 = tubes_of(self.patch, self.mask, self.token) + self.vec[4:5]
        for h in range(2):
            x1 = x1 + dot(self.o[h], self.wm[h], NT)
        self.x1[...] = x1
        centred = x1 - mean_rows(x1)
        scale = lax.rsqrt(mean_rows(centred * centred) + 1e-6)
        self.a2[...] = (centred * scale * self.vec[5:6] + self.vec[6:7]).astype(BF)
        self.acc[...] = x1 + self.vec[11:12]
        self.da2[...] = jnp.zeros_like(self.da2)

    def block(self, n, we, ws, keep, hook):
        a2, dy = self.a2[...], self.dy[...]
        hidden = dot(a2, we) + self.vec[pl.ds(7 + n, 1)]
        cdf, density = normal_parts(hidden)
        u = (hidden * cdf).astype(BF)
        du = dot(dy, ws)
        dh = (du * (cdf + hidden * density)).astype(BF)
        self.gv[pl.ds(4 + n, 1)] = jnp.sum(dh.astype(F32), axis=0, keepdims=True)
        keep(0, dot(dy, u, TN).astype(BF))
        keep(1, dot(a2, dh, TN).astype(BF))
        hook()
        self.acc[...] += dot(u, ws, NT)
        self.da2[...] += dot(dh, we, NT)

    def close(self):
        self.out[...] = self.acc[...].astype(BF)
        x1, top, da2 = self.x1[...], self.dy[...].astype(F32), self.da2[...]
        centred = x1 - mean_rows(x1)
        scale = lax.rsqrt(mean_rows(centred * centred) + 1e-6)
        xh = centred * scale
        e = da2 * self.vec[5:6]
        dx1 = top + scale * (e - mean_rows(e) - xh * mean_rows(e * xh))
        self.dx1[...] = dx1
        dxb = dx1.astype(BF)
        for h in range(2):
            self.do[h] = (dot(dxb, self.wm[h]) * self.inv[h]).astype(BF)
            self.gm[h] = dot(dxb, self.o[h], TN).astype(BF)
        self.gv[0:1] = jnp.sum(dxb.astype(F32), axis=0, keepdims=True)
        self.gv[1:2] = jnp.sum(da2 * xh, axis=0, keepdims=True)
        self.gv[2:3] = jnp.sum(da2, axis=0, keepdims=True)
        self.gv[3:4] = jnp.sum(top, axis=0, keepdims=True)


def middle_plain_kernel(*refs):
    we_ref, ws_ref = refs[8:10]
    ge_ref, gs_ref = refs[15:17]
    body = Middle(refs[:8], refs[10:15], refs[17:])
    i = pl.program_id(0)
    pl.when(i == 0)(body.open)

    def keep(n, grad):
        (gs_ref, ge_ref)[n][0] = grad

    body.block(i, we_ref[0], ws_ref[0], keep, lambda: None)
    pl.when(i == pl.num_programs(0) - 1)(body.close)


def middle_kernel(*refs):
    we_ref, ws_in = refs[8:10]
    body = Middle(refs[:8], refs[10:15], refs[18:22])
    mine, early_side, early_far = refs[15:18]
    ws, raw, sib, load_sem, put_sem, send_sem, recv_sem = refs[22:]
    i = pl.program_id(0)
    x, z, y, c = place()
    lines, over_x, over_y, sibling = neighbours()
    wires = Wires(send_sem, recv_sem)
    width = raw.shape[-1]
    half = lax.rem(x + i // 2, 2)
    part = lax.rem(i, 2)

    def cols(n):
        return pl.ds(n * width, width)

    def load():
        return pltpu.make_async_copy(ws_in.at[x], ws.at[x], load_sem)

    def put(n):
        h = x if n < 2 else 1 - x
        return pltpu.make_async_copy(raw.at[n % 2, :, :, :, c], mine.at[h, n % 2], put_sem.at[n % 2])

    def to_sibling(n):
        return raw.at[n % 2, :, :, :, 1 - c]

    def offer(n):
        wires.copy(10 + n, to_sibling(n), sib.at[n % 2], sibling).start()

    def finish(n):
        slot = n % 2
        wires.arrive(10 + n, sib.at[slot])
        wires.sent(10 + n, to_sibling(n))

        def sweep(m, _):
            at = (m // 8, lax.rem(m // 2, 4), lax.rem(m, 2))
            add_into(raw.at[slot, at[0], at[1], at[2], c], sib.at[slot, at[0], at[1], at[2]])
            return 0

        lax.fori_loop(0, 16, sweep, 0)
        put(n).start()

    def far_source(n, k):
        return mine.at[x, n, 0, lax.rem(z + k, 4)]

    def send_far(n):
        for k in (1, 2, 3):
            wires.start(14 + 3 * n + k, far_source(n, k), early_far.at[n, k - 1], lines[k - 1])

    def across(n, core):
        return ws.at[1 - x, :, 1 - y, core, :, cols(n)]

    def side(n, core):
        return ws.at[1 - x, :, y, core, :, cols(n)]

    def own_part(n):
        return ws_in.at[x, :, y, c, :, cols(n)]

    @pl.when(i == 0)
    def _():
        load().start()
        greet()
        for n, slot in enumerate((0, 9)):
            wires.start(slot, own_part(n), ws.at[x, :, y, c, :, cols(n)], over_x)
        body.open()
        load().wait()

    @pl.when(i == 2)
    def _():
        wires.arrive(3, side(0, 1 - c))
        wires.arrive(4, across(0, 1 - c))

    @pl.when(i == 3)
    def _():
        wires.arrive(7, side(1, 1 - c))
        wires.arrive(5, across(1, 1 - c))

    def hook():
        @pl.when(i == 0)
        def _():
            wires.arrive(0, side(0, c))
            wires.start(1, side(0, c), side(0, c), over_y)
            wires.start(3, side(0, c), side(0, c), sibling)
            offer(0)

        @pl.when(i == 1)
        def _():
            finish(0)
            offer(1)
            wires.arrive(9, side(1, c))
            wires.start(2, side(1, c), side(1, c), over_y)
            wires.start(7, side(1, c), side(1, c), sibling)
            wires.arrive(1, across(0, c))
            wires.start(4, across(0, c), across(0, c), sibling)
            put(0).wait()
            send_far(0)

        @pl.when(i == 2)
        def _():
            finish(1)
            offer(2)
            wires.arrive(2, across(1, c))
            wires.start(5, across(1, c), across(1, c), sibling)
            put(1).wait()
            send_far(1)
            wires.start(6, mine.at[x, :, 1, :, 1 - y], early_side, over_y)

        @pl.when(i == 3)
        def _():
            finish(2)
            offer(3)

    def keep(n, grad):
        raw[part, n] = grad.reshape(raw.shape[2:])

    weight = ws[half, :, :, :, :, pl.ds(pl.multiple_of(part * width, width), width)].reshape(-1, width)
    body.block(half * 2 + part, we_ref[0], weight, keep, hook)

    @pl.when(i == pl.num_programs(0) - 1)
    def _():
        body.close()
        put(2).wait()
        finish(3)
        wires.arrive(6, early_side)
        for n in range(2):
            for k in (1, 2, 3):
                wires.arrive(14 + 3 * n + k, early_far.at[n, k - 1])
                wires.sent(14 + 3 * n + k, far_source(n, k))
        for n in range(2):
            wires.sent((0, 9)[n], own_part(n))
            wires.sent(1 + n, side(n, c))
            wires.sent((3, 7)[n], side(n, c))
            wires.sent(4 + n, across(n, c))
        wires.sent(6, mine.at[x, :, 1, :, 1 - y])
        put(3).wait()


def middle(patches, mask, token, o, inv, dy, vectors, wm, we, ws, direct):
    rows, width = patches.shape
    hidden = we.shape[2]
    per = hidden // width

    def whole(shape):
        return pl.BlockSpec(shape, lambda i: (0,) * len(shape))

    def of_w(i):
        turn = i // per
        if direct:
            turn = lax.rem(turn + lax.axis_index("mp"), 2)
        return (turn, 0, lax.rem(i, per))

    by_block = pl.BlockSpec((1, width, width), of_w)
    ins = [patches, mask, token, o, inv, dy, vectors, wm, we, ws]
    shapes = [
        jax.ShapeDtypeStruct((rows, width), BF),
        jax.ShapeDtypeStruct((rows, width), F32),
        jax.ShapeDtypeStruct(o.shape, BF),
        jax.ShapeDtypeStruct(wm.shape, BF),
        jax.ShapeDtypeStruct((8, width), F32),
    ]
    in_specs = [pl.BlockSpec(v.shape, lambda i, v=v: (0,) * v.ndim, pipeline_mode=pl.Buffered(1)) for v in ins[:8]]
    out_specs = [whole(v.shape) for v in shapes]
    scratch = [
        pltpu.VMEM((rows, width), F32),
        pltpu.VMEM((rows, width), BF),
        pltpu.VMEM((rows, width), F32),
        pltpu.VMEM((rows, width), F32),
    ]
    common = dict(grid=(2 * per,), name="middle")
    if not direct:
        return pl.pallas_call(
            middle_plain_kernel,
            in_specs=[*in_specs, by_block, by_block],
            out_specs=[*out_specs, by_block, by_block],
            out_shape=[*shapes, *[jax.ShapeDtypeStruct(we.shape, BF)] * 2],
            scratch_shapes=scratch,
            compiler_params=params(),
            **common,
        )(*ins)
    own_rows = ws.shape[4]
    unit = (own_rows, width)
    return pl.pallas_call(
        middle_kernel,
        in_specs=[*in_specs, by_block, anywhere()],
        out_specs=[*out_specs, *[anywhere()] * 3],
        out_shape=[
            *shapes,
            jax.ShapeDtypeStruct((2, per, 2, 4, 2, *unit), BF),
            jax.ShapeDtypeStruct((per, 4, *unit), BF),
            jax.ShapeDtypeStruct((per, 3, 2, *unit), BF),
        ],
        scratch_shapes=[
            *scratch,
            pltpu.VMEM(ws.shape, BF),
            pltpu.VMEM((2, 2, 4, 2, 2, *unit), BF),
            pltpu.VMEM((2, 2, 4, 2, *unit), BF),
            pltpu.SemaphoreType.DMA,
            pltpu.SemaphoreType.DMA((2,)),
            pltpu.SemaphoreType.DMA((21,)),
            pltpu.SemaphoreType.DMA((21,)),
        ],
        compiler_params=params(collective_id=4, has_side_effects=True),
        **common,
    )(*ins)


def unproject_kernel(
    mine_ref, other_ref, dq_ref, dk_ref, dv_ref, w_ref, da_ref, send_ref, gw_ref, gv_ref
):
    rows = mine_ref.shape[0]
    half = w_ref.shape[2] // 3
    da, send = None, None
    gv_ref[...] = jnp.zeros_like(gv_ref)
    for h in range(2):
        cols = slice(h * half, (h + 1) * half)
        dq, dk, dv = dq_ref[h], dk_ref[h], dv_ref[h]
        wq, wk, wv = (w_ref[h, :, n * half : (n + 1) * half] for n in range(3))
        mine = dot(dq, wq, NT) + dot(dk[:rows], wk, NT) + dot(dv[:rows], wv, NT)
        other = dot(dk[rows:], wk, NT) + dot(dv[rows:], wv, NT)
        da = mine if da is None else da + mine
        send = other if send is None else send + other
        a, b = mine_ref[...], other_ref[...]
        gw_ref[h, :, :half] = dot(a, dq, TN).astype(BF)
        gw_ref[h, :, half : 2 * half] = (dot(a, dk[:rows], TN) + dot(b, dk[rows:], TN)).astype(BF)
        gw_ref[h, :, 2 * half :] = (dot(a, dv[:rows], TN) + dot(b, dv[rows:], TN)).astype(BF)
        gv_ref[0:1, cols] = jnp.sum(dq.astype(F32), axis=0, keepdims=True)
        gv_ref[1:2, cols] = jnp.sum(dv.astype(F32), axis=0, keepdims=True)
    da_ref[...] = da
    send_ref[...] = send.astype(BF)


def unproject(mine, other, dq, dk, dv, weight):
    rows, width = mine.shape
    return pl.pallas_call(
        unproject_kernel,
        out_shape=[
            jax.ShapeDtypeStruct((rows, width), F32),
            jax.ShapeDtypeStruct((rows, width), BF),
            jax.ShapeDtypeStruct(weight.shape, BF),
            jax.ShapeDtypeStruct((8, width), F32),
        ],
        in_specs=[in_vmem()] * 6,
        out_specs=[in_vmem()] * 4,
        compiler_params=params(),
        name="unproject",
    )(mine, other, dq, dk, dv, weight)


def lamb_parts(weight, moment, square, grad):
    correct = 1.0 - 0.5**STEP
    moment_new = 0.5 * moment + 0.5 * grad
    square_new = 0.5 * square + 0.5 * grad * grad
    update = moment_new / correct / (jnp.sqrt(square_new / correct) + 1e-06) + 0.01 * weight
    return moment_new, square_new, update


def whole_sum(values):
    return jnp.sum(jnp.sum(values, axis=0, keepdims=True), axis=1, keepdims=True)


def last_kernel(*refs):
    sources, refs = refs[:8], refs[8:]
    (mask_ref, token_ref, vec_ref, tail_ref), refs = refs[:4], refs[4:]
    (total_s, lined, lined_m), refs = refs[:3], refs[3:]
    masters, firsts, seconds, refs = refs[:4], refs[4:8], refs[8:12], refs[12:]
    pg_ref, early_ref, late_ref, *totals = refs[:6]
    totals.append(total_s)
    refs = refs[6:]
    loaded, refs = refs[:8], refs[8:]
    dk_ref, dv_ref, w_ref, a_ref, b_ref, dq_ref, patch_ref, dx1_ref = loaded
    gw, sib, diag, side, da_ref, send_ref, landing = refs[:7]
    far, refs = refs[7:10], refs[10:]
    held, came, final, late, late_line, load_sem, send_sem, recv_sem = refs
    x, z, y, c = place()
    lines, over_x, over_y, sibling = neighbours()
    wires = Wires(send_sem, recv_sem)
    rows, depth = a_ref.shape
    half = w_ref.shape[2] // 3
    cut = rows // 32 * 16
    spans = (pl.ds(0, cut), pl.ds(cut, rows - cut))
    loads = [pltpu.make_async_copy(s, d, load_sem.at[n]) for n, (s, d) in enumerate(zip(sources, loaded))]
    for load in loads:
        load.start()

    def flipped(code):
        def flip(v, bit):
            return 1 - v if bit else v

        return device(flip(x, code // 4), z, flip(y, code // 2 % 2), flip(c, code % 2))

    barrier = pltpu.get_barrier_semaphore()
    for other in (*lines, *[flipped(code) for code in range(1, 8)]):
        pl.semaphore_signal(barrier, inc=1, device_id=other, device_id_type=MESH)
    pl.semaphore_wait(barrier, 10)

    def ahead(k):
        return lax.rem(z + k, 4)

    for k in (1, 2, 3):
        wires.start(3 + k - 1, lined_m.at[ahead(k)], far[1].at[k - 1], lines[k - 1])
        wires.start(6 + k - 1, lined.at[:, ahead(k)], far[2].at[k - 1], lines[k - 1])

    def settle(n, own):
        total = own.astype(F32)
        for k in range(3):
            wires.arrive(3 * n + k, far[n].at[k])
            total = total + far[n][k].astype(F32)
        if n == 0:
            for part in range(3):
                totals[n][part] = total[:, part * half : (part + 1) * half]
        elif n == 1:
            totals[n][...] = total
        else:
            for part in range(total.shape[0]):
                totals[2][:, part * depth : (part + 1) * depth] = total[part]

    lane = lax.broadcasted_iota(jnp.int32, (8, PAIR), 1)
    squares = jnp.zeros((8, PAIR), F32)

    def add_squares(squares, n, pick):
        weight = masters[n][pick]
        update = lamb_parts(weight, firsts[n][pick], seconds[n][pick], totals[n][pick])[2]
        squares = squares + jnp.where(lane == 2 * n, whole_sum(weight * weight), 0.0)
        return squares + jnp.where(lane == 2 * n + 1, whole_sum(update * update), 0.0)

    def columns(n):
        return slice(n * half, (n + 1) * half)

    for n in range(3):
        loads[n].wait()
    for n, (start, size) in enumerate(((rows, cut), (rows + cut, rows - cut))):
        span = pl.ds(start, size)
        send = None
        for h in range(2):
            part = dot(dk_ref[h, span], w_ref[h, :, columns(1)], NT) + dot(dv_ref[h, span], w_ref[h, :, columns(2)], NT)
            send = part if send is None else send + part
        send_ref[spans[n]] = send.astype(BF)
        wires.start(12 + n, send_ref.at[spans[n]], landing.at[spans[n]], over_x)
    for n in range(3, 6):
        loads[n].wait()
    held[0] = jnp.zeros(held.shape[1:], F32)
    for h in range(2):
        held[0, 2:3, columns(h)] = jnp.sum(dq_ref[h].astype(F32), axis=0, keepdims=True)
        held[0, 3:4, columns(h)] = jnp.sum(dv_ref[h].astype(F32), axis=0, keepdims=True)
    held[0, 4:7] = tail_ref[0:3]
    held[0, 7:11] = tail_ref[4:8]
    held[0, 11:12] = tail_ref[3:4]
    wires.start(25, held.at[0], came.at[0], sibling)
    a, b = a_ref[...], b_ref[...]
    own, other = pl.ds(0, rows), pl.ds(rows, rows)

    def weight_grad(h, n):
        if n == 0:
            grad = dot(a, dq_ref[h], TN)
        else:
            ref = dk_ref if n == 1 else dv_ref
            grad = dot(a, ref[h, own], TN) + dot(b, ref[h, other], TN)
        gw[h, :, :, :, :, columns(n)] = grad.astype(BF).reshape(4, 2, 2, -1, half)

    def with_sibling(h, slot):
        wires.arrive(slot, sib.at[h])

        def sweep(m, _):
            add_into(gw.at[h, m // 2, lax.rem(m, 2), c], sib.at[h, m // 2, lax.rem(m, 2)])
            return 0

        lax.fori_loop(0, 8, sweep, 0)

    for n in range(3):
        weight_grad(1 - x, n)
    wires.start(14, gw.at[1 - x, :, :, 1 - c], sib.at[1 - x], sibling)
    wires.arrive(25, came.at[0])
    held[1] = held[0] + came[0]
    wires.start(26, held.at[1], came.at[1], over_y)
    weight_grad(x, 0)
    weight_grad(x, 1)
    with_sibling(1 - x, 14)
    order = (1, 2, 3, 0)
    for k in order:
        wires.start(16 + k, gw.at[1 - x, ahead(k), 1 - y, c], diag.at[ahead(k)], over_y)
    wires.arrive(26, came.at[1])
    held[2] = held[1] + came[1]
    wires.start(27, held.at[2], came.at[2], over_x)
    weight_grad(x, 2)
    wires.start(15, gw.at[x, :, :, 1 - c], sib.at[x], sibling)
    da = None
    for h in range(2):
        part = (
            dot(dq_ref[h], w_ref[h, :, columns(0)], NT)
            + dot(dk_ref[h, own], w_ref[h, :, columns(1)], NT)
            + dot(dv_ref[h, own], w_ref[h, :, columns(2)], NT)
        )
        da = part if da is None else da + part
    da_ref[...] = da
    with_sibling(x, 15)
    wires.start(24, gw.at[x, :, 1 - y, c], side.at[1], over_y)
    for k in order:
        wires.arrive(16 + k, diag.at[ahead(k)])
        part = gw.at[1 - x, ahead(k), y, c]
        add_into(part, diag.at[ahead(k)])
        wires.start(20 + k, part, side.at[0, ahead(k)], over_x)
    settle(1, lined_m[z])
    settle(2, lined[:, z])
    for n in (1, 2, 3):
        squares = add_squares(squares, n, ...)
    for n in range(6, 8):
        loads[n].wait()
    tubes = tubes_of(patch_ref, mask_ref, token_ref)
    centred = tubes - mean_rows(tubes)
    scale = lax.rsqrt(mean_rows(centred * centred) + 1e-6)
    xh = centred * scale
    for n in range(2):
        wires.arrive(12 + n, landing.at[spans[n]])
    da = da_ref[...] + landing[...].astype(F32)
    me = x * 4 + y * 2 + c
    deep = depth // PAIR

    def late_row(n, values):
        for j in range(deep):
            late[me, n * deep + j : n * deep + j + 1] = values[:, j * PAIR : (j + 1) * PAIR]

    late_row(0, jnp.sum(da * xh, axis=0, keepdims=True))
    late_row(1, jnp.sum(da, axis=0, keepdims=True))
    e = da * vec_ref[0:1]
    dx = dx1_ref[...] + scale * (e - mean_rows(e) - xh * mean_rows(e * xh))
    masked = mask_ref[...] > 0
    pg_ref[...] = jnp.where(masked, 0.0, dx).astype(BF)
    late_row(2, jnp.sum(jnp.where(masked, dx, 0.0), axis=0, keepdims=True))
    wires.arrive(27, came.at[2])
    final[z] = held[2] + came[2]
    for k in (1, 2, 3):
        wires.start(27 + k, final.at[z], final.at[z], lines[k - 1])
    wires.arrive(24, side.at[1])

    def with_sides(k):
        wires.arrive(20 + k, side.at[0, ahead(k)])
        both = side[0, ahead(k)].astype(F32) + side[1, ahead(k)].astype(F32)
        part = gw.at[x, ahead(k), y, c]
        part[...] = (part[...].astype(F32) + both).astype(BF)
        if k:
            wires.start(k - 1, part, far[0].at[k - 1], lines[k - 1])

    for k in order:
        with_sides(k)
    for k in (1, 2, 3):
        wires.arrive(27 + k, final.at[ahead(4 - k)])
    early_ref[...] = final[0] + final[1] + final[2] + final[3]
    settle(0, gw[x, z, y, c])
    for part in range(3):
        squares = add_squares(squares, 0, part)
    late[me, 3 * deep : 3 * deep + 1] = squares[0:1]
    late[me, 3 * deep + 1 :] = jnp.zeros((late.shape[1] - 3 * deep - 1, PAIR), F32)
    for code in range(1, 8):
        wires.start(30 + code, late.at[me], late.at[me], flipped(code))

    def flip_index(code):
        return sum((1 - v if bit else v) * w for v, bit, w in ((x, code // 4, 4), (y, code // 2 % 2, 2), (c, code % 2, 1)))

    for code in range(1, 8):
        wires.arrive(30 + code, late.at[flip_index(code)])
    total = late[0]
    for n in range(1, 8):
        total = total + late[n]
    late_line[z] = total
    for k in (1, 2, 3):
        wires.start(37 + k, late_line.at[z], late_line.at[z], lines[k - 1])
    for k in (1, 2, 3):
        wires.arrive(37 + k, late_line.at[ahead(4 - k)])
    late_ref[...] = late_line[0] + late_line[1] + late_line[2] + late_line[3]
    wires.drain()


def last(a, b, dq, dk, dv, wa, patches, mask, token, vectors, tail, dx1, sums, masters, firsts, seconds):
    rows, width = a.shape
    lined, lined_m = sums[1:]
    own_rows, w = lined_m.shape[1], wa.shape[2]
    far = [(own_rows, w), lined_m.shape[1:], (lined.shape[0], *lined.shape[2:])]
    late = (3 * (width // PAIR) + 8) // 8 * 8
    big = [dk, dv, wa, a, b, dq, patches, dx1]
    return pl.pallas_call(
        last_kernel,
        out_shape=[
            jax.ShapeDtypeStruct((rows, width), BF),
            jax.ShapeDtypeStruct((16, width), F32),
            jax.ShapeDtypeStruct((late, PAIR), F32),
            *[jax.ShapeDtypeStruct(m.shape, F32) for m in masters[:3]],
        ],
        in_specs=[anywhere()] * 8 + [in_vmem()] * 19,
        out_specs=[in_vmem()] * 6,
        scratch_shapes=[
            *[pltpu.VMEM(v.shape, v.dtype) for v in big],
            pltpu.VMEM((2, 4, 2, 2, own_rows, w), BF),
            pltpu.VMEM((2, 4, 2, own_rows, w), BF),
            pltpu.VMEM((4, own_rows, w), BF),
            pltpu.VMEM((2, 4, own_rows, w), BF),
            pltpu.VMEM((rows, width), F32),
            pltpu.VMEM((rows, width), BF),
            pltpu.VMEM((rows, width), BF),
            *[pltpu.VMEM((3, *f), BF) for f in far],
            pltpu.VMEM((3, 16, width), F32),
            pltpu.VMEM((3, 16, width), F32),
            pltpu.VMEM((4, 16, width), F32),
            pltpu.VMEM((8, late, PAIR), F32),
            pltpu.VMEM((4, late, PAIR), F32),
            pltpu.SemaphoreType.DMA((8,)),
            pltpu.SemaphoreType.DMA((41,)),
            pltpu.SemaphoreType.DMA((41,)),
        ],
        compiler_params=params(collective_id=1, has_side_effects=True),
        name="last",
    )(*big, mask, token, vectors, tail, *sums, *masters, *firsts, *seconds)


def lamb_kernel(*refs):
    masters, firsts, seconds, totals = (refs[4 * n : 4 * n + 4] for n in range(4))
    grad_ref, late_ref, vec_ref, vfirst_ref, vsecond_ref = refs[16:21]
    moments, squares, weights, copies = (refs[21 + 4 * n : 25 + 4 * n] for n in range(4))
    token_ref, bias_ref, vm_ref, vs_ref, vw_ref, norm_ref = refs[37:43]
    deep = vec_ref.shape[1] // PAIR

    def late_row(n):
        return jnp.concatenate([late_ref[n * deep + j : n * deep + j + 1] for j in range(deep)], axis=1)

    norms = jnp.sqrt(late_ref[3 * deep : 3 * deep + 1])
    for n in range(4):
        size, length = norms[:, 2 * n : 2 * n + 1], norms[:, 2 * n + 1 : 2 * n + 2]
        norm_ref[n : n + 1, 0:1] = size
        norm_ref[n : n + 1, 1:2] = length
        step = 0.5 * size / (length + 1e-06)
        for pick in range(3) if n == 0 else (...,):
            weight = masters[n][pick]
            moment, square, update = lamb_parts(weight, firsts[n][pick], seconds[n][pick], totals[n][pick])
            moments[n][pick] = moment
            squares[n][pick] = square
            renewed = weight - step * update
            weights[n][pick] = renewed
            copies[n][pick] = renewed.astype(BF)
    vectors = vec_ref[...]
    grad = jnp.concatenate([late_row(0), late_row(1), grad_ref[2:12]], axis=0)
    moment, square, update = lamb_parts(vectors, vfirst_ref[...], vsecond_ref[...], grad)
    vm_ref[...] = moment
    vs_ref[...] = square
    size = jnp.sqrt(jnp.sum(vectors * vectors, axis=-1, keepdims=True))
    length = jnp.sqrt(jnp.sum(update * update, axis=-1, keepdims=True))
    vw_ref[...] = vectors - 0.5 * size / (length + 1e-06) * update
    token_ref[...] = late_row(2).reshape(token_ref.shape)
    bias_ref[...] = grad_ref[11:12].reshape(bias_ref.shape)


def lamb(masters, firsts, seconds, totals, grad, squares, vectors, vfirst, vsecond):
    full = [jax.ShapeDtypeStruct(m.shape, F32) for m in masters]
    flat = jax.ShapeDtypeStruct((vectors.shape[1],), F32)
    like = jax.ShapeDtypeStruct(vectors.shape, F32)
    return pl.pallas_call(
        lamb_kernel,
        out_shape=[
            *full,
            *full,
            *full,
            *[jax.ShapeDtypeStruct(m.shape, BF) for m in masters],
            flat,
            flat,
            like,
            like,
            like,
            jax.ShapeDtypeStruct((4, 2), F32),
        ],
        in_specs=[in_vmem()] * 21,
        out_specs=[in_vmem()] * 22,
        compiler_params=params(),
        name="lamb",
    )(*masters, *firsts, *seconds, *totals, grad, squares, vectors, vfirst, vsecond)


def lamb_terms(weight, moment, square, gradient):
    moment_new = 0.5 * moment + 0.5 * gradient
    square_new = 0.5 * square + 0.5 * gradient * gradient
    correct = 1.0 - 0.5**STEP
    update = moment_new / correct / (jnp.sqrt(square_new / correct) + 1e-06) + 0.01 * weight
    return (
        moment_new,
        square_new,
        update,
        jnp.stack([jnp.sum(weight * weight), jnp.sum(update * update)]),
    )


def lamb_apply(weight, update, norms):
    renewed = weight - 0.5 * norms[0] / (norms[1] + 1e-06) * update
    return (renewed, renewed.astype(BF))


def per_device(
    patches,
    cube_mask,
    mask_token,
    cotangent,
    vectors,
    vector_first,
    vector_second,
    attend_master,
    attend_first,
    attend_second,
    mixing_master,
    mixing_first,
    mixing_second,
    expand_master,
    expand_first,
    expand_second,
    shrink_master,
    shrink_first,
    shrink_second,
):
    clips, rows, width = patches.shape
    axis = lax.axis_size("dp")
    own_rows = attend_master.shape[0]
    direct = axis == 16 and lax.axis_size("mp") == 2
    dy = cotangent[0]

    def lead(v):
        return v.transpose(1, 0, 2)

    if direct:
        masters = [lead(attend_master), mixing_master, expand_master, shrink_master]
        firsts = [lead(attend_first), mixing_first, expand_first, shrink_first]
        seconds = [lead(attend_second), mixing_second, expand_second, shrink_second]
        *wholes, q, k, v, a1, a1_other, mask = first(masters, patches[0], cube_mask, mask_token, vectors)
        wa = wholes[0].reshape(2, width, -1)
        o, o_low, inv, p, *rest = attend(q, k, v, wholes[1:])
        wm, we = (w.reshape(2, width, -1) for w in rest[:2])
        block_out, dx1, do, gm, tail, *grads = middle(
            patches[0], mask, mask_token, o_low, inv, dy, vectors, wm, we, rest[2], True
        )
        dq, dk, dv, *sums = attend_back(q, k, v, do, o, p, [*grads, gm.reshape(rest[0].shape)])
        patch_grad, early, late, *totals = last(
            a1,
            a1_other,
            dq,
            dk,
            dv,
            wa,
            patches[0],
            mask,
            mask_token,
            vectors,
            tail,
            dx1,
            sums,
            masters,
            firsts,
            seconds,
        )
        totals.append(sums[0])
        done = lamb(masters, firsts, seconds, totals, early, late, vectors, vector_first, vector_second)
        results = []
        for n in range(4):
            group = [done[n], done[4 + n], done[8 + n], done[12 + n]]
            results.extend([lead(g) for g in group] if n == 0 else group)
        return (block_out[None], patch_grad[None], done[16], done[17], *results, *done[18:])
    masters = [attend_master.reshape(own_rows, -1), mixing_master, expand_master, shrink_master]
    firsts = [attend_first.reshape(own_rows, -1), mixing_first, expand_first, shrink_first]
    seconds = [attend_second.reshape(own_rows, -1), mixing_second, expand_second, shrink_second]
    shards = [m.astype(BF) for m in masters]
    mask, token = cube_mask.reshape(rows, 1).astype(F32), mask_token[None]
    swap = [(0, 1), (1, 0)]
    chosen = mask > 0
    x = jnp.where(chosen, token, patches[0].astype(F32))
    centred = x - mean_rows(x)
    scale = lax.rsqrt(mean_rows(centred * centred) + 1e-6)
    wa, wm, we, ws = (
        lax.all_gather(lax.all_gather(s, "dp", axis=0, tiled=True), "mp", axis=0) for s in shards
    )
    a1 = (centred * scale * vectors[0] + vectors[1]).astype(BF)
    a1_other = lax.ppermute(a1, "mp", swap)
    q, k, v = project(a1, a1_other, wa, vectors[2:4])
    o, o_low, inv, p = attend(q, k, v, [])
    block_out, dx1, do, gm, gv, ge, gs = middle(
        patches[0], mask, mask_token, o_low, inv, dy, vectors, wm, we, ws, False
    )
    dq, dk, dv = attend_back(q, k, v, do, o, p, [])
    da1, da1_send, ga, gqv = unproject(a1, a1_other, dq, dk, dv, wa)
    da1 = da1 + lax.ppermute(da1_send, "mp", swap).astype(F32)
    totals = []
    for g in (ga, gm, ge, gs):
        g = lax.psum_scatter(g, "mp", scatter_dimension=0, tiled=True)
        totals.append(lax.psum_scatter(g[0].astype(F32), "dp", scatter_dimension=0, tiled=True))
    xh = centred * scale
    e = da1 * vectors[0]
    dx = dx1 + scale * (e - mean_rows(e) - xh * mean_rows(e * xh))
    patch_grad = jnp.where(chosen, 0.0, dx).astype(BF)
    token_part = jnp.sum(jnp.where(chosen, dx, 0.0), axis=0)
    vector_part = jnp.concatenate(
        [
            jnp.sum(da1 * xh, axis=0)[None],
            jnp.sum(da1, axis=0)[None],
            gqv[0:2],
            gv[0:3],
            gv[4:8],
            gv[3:4],
        ],
        axis=0,
    )
    terms = [lamb_terms(w, m, s, g) for w, m, s, g in zip(masters, firsts, seconds, totals)]
    squares = jnp.stack([t[3] for t in terms])
    vector_total, token_grad, square_total = lax.psum(
        (vector_part, token_part, squares), ("dp", "mp")
    )
    trust_norms = jnp.sqrt(square_total)
    results = []
    for n, (w, t) in enumerate(zip(masters, terms)):
        group = [t[0], t[1], *lamb_apply(w, t[2], trust_norms[n])]
        if n == 0:
            group = [g.reshape(attend_master.shape) for g in group]
        results.extend(group)
    vector_moment = 0.5 * vector_first + 0.5 * vector_total
    vector_square = 0.5 * vector_second + 0.5 * vector_total * vector_total
    correct = 1.0 - 0.5**STEP
    vector_update = (
        vector_moment / correct / (jnp.sqrt(vector_square / correct) + 1e-06) + 0.01 * vectors
    )
    row_weight = jnp.sqrt(jnp.sum(vectors * vectors, axis=-1, keepdims=True))
    row_update = jnp.sqrt(jnp.sum(vector_update * vector_update, axis=-1, keepdims=True))
    vector_weight = vectors - 0.5 * row_weight / (row_update + 1e-06) * vector_update
    return (
        block_out[None],
        patch_grad[None],
        token_grad,
        vector_total[11],
        *results,
        vector_moment,
        vector_square,
        vector_weight,
        trust_norms,
    )


def solution(mesh):
    rows = P("dp", "mp", None)
    flat = P("dp", "mp")
    deep = P("dp", None, "mp")
    copied = P()
    return jax.shard_map(
        per_device,
        mesh=mesh,
        in_specs=(rows, flat, copied, rows, copied, copied, copied, *[deep] * 3, *[flat] * 9),
        out_specs=(rows, rows, copied, copied, *[deep] * 4, *[flat] * 12, *[copied] * 4),
        check_vma=False,
    )
```

```python
import functools

import jax
import jax.numpy as jnp
from jax import lax
from jax.experimental import pallas as pl
from jax.experimental.pallas import tpu as pltpu
from jax.sharding import PartitionSpec as P

HD = 64
PAIR = 2 * HD
STEP = 5
BF = jnp.bfloat16
F32 = jnp.float32
NN = (((1,), (0,)), ((), ()))
NT = (((1,), (1,)), ((), ()))
TN = (((0,), (0,)), ((), ()))
LOG2E = 1.4426950408889634
MESH = pl.DeviceIdType.MESH
VMEM_LIMIT = 60 * 2**20


def dot(a, b, dims=NN):
    return lax.dot_general(a, b, dims, preferred_element_type=F32)


def params(**kw):
    return pltpu.CompilerParams(vmem_limit_bytes=VMEM_LIMIT, **kw)


def anywhere():
    return pl.BlockSpec(memory_space=pl.ANY)


def in_vmem():
    return pl.BlockSpec(memory_space=pltpu.VMEM)


def place():
    dp, x = lax.axis_index("dp"), lax.axis_index("mp")
    return x, dp // 4, lax.rem(dp // 2, 2), lax.rem(dp, 2)


def device(x, z, y, c):
    return ((z * 2 + y) * 2 + c, x)


def neighbours():
    x, z, y, c = place()
    lines = [device(x, lax.rem(z + k, 4), y, c) for k in (1, 2, 3)]
    return lines, device(1 - x, z, y, c), device(x, z, 1 - y, c), device(x, z, y, 1 - c)


def greet():
    lines, over_x, over_y, sibling = neighbours()
    barrier = pltpu.get_barrier_semaphore()
    for other in (*lines, over_x, over_y, sibling):
        pl.semaphore_signal(barrier, inc=1, device_id=other, device_id_type=MESH)
    pl.semaphore_wait(barrier, 6)


class Wires:
    def __init__(self, send_sem, recv_sem):
        self.send_sem, self.recv_sem = send_sem, recv_sem
        self.started = []

    def copy(self, slot, src, dst, other):
        return pltpu.make_async_remote_copy(
            src_ref=src,
            dst_ref=dst,
            send_sem=self.send_sem.at[slot],
            recv_sem=self.recv_sem.at[slot],
            device_id=other,
            device_id_type=MESH,
        )

    def start(self, slot, src, dst, other):
        self.copy(slot, src, dst, other).start()
        self.started.append((slot, src))

    def send(self, slot, whole, part, other):
        self.copy(slot, whole.at[part], whole.at[part], other).start()
        self.started.append((slot, whole, part))

    def arrive(self, slot, dst):
        x, z, y, c = place()
        self.copy(slot, dst, dst, device(x, z, y, 1 - c)).wait_recv()

    def sent(self, slot, src):
        x, z, y, c = place()
        self.copy(slot, src, src, device(x, z, y, 1 - c)).wait_send()

    def drain(self):
        for slot, src, *part in self.started:
            self.sent(slot, src.at[part[0]] if part else src)


ALL = slice(None)


def greet_near():
    _, *near = neighbours()
    barrier = pltpu.get_barrier_semaphore()
    for other in near:
        pl.semaphore_signal(barrier, inc=1, device_id=other, device_id_type=MESH)
    pl.semaphore_wait(barrier, 3)


def first_kernel(*refs):
    masters, (patch_ref, flag_ref, token_ref, vec_ref) = refs[:4], refs[4:8]
    wa_out, wm, we, ws, q_out, k_out, v_out, a1_out, other_out, mask_ref = refs[8:18]
    wa, landing, a1_ref, q_ref, k_ref, v_ref, sa, sm, se, ss, own_sem, put_sem, send_sem, recv_sem = refs[18:]
    x, z, y, c = place()
    lines, over_x, over_y, sibling = neighbours()
    wires = Wires(send_sem, recv_sem)
    rows = a1_ref.shape[0]
    cut = rows // 64 * 16
    halves = (pl.ds(0, cut), pl.ds(cut, rows - cut))
    width = wa.shape[-1] // 3
    for n in range(3):
        sa[:, n * width : (n + 1) * width] = masters[0][n].astype(BF)
    for shard, master in zip((sm, se, ss), masters[1:]):
        shard[...] = master[...].astype(BF)
    puts = []

    def put(src, dst):
        copy = pltpu.make_async_copy(src, dst, put_sem.at[len(puts)])
        copy.start()
        puts.append(copy)

    greet()

    def back(k):
        return lax.rem(z + 4 - k, 4)

    own = [pltpu.make_async_copy(sa, wa.at[x, z, y, c], own_sem.at[0])]
    for n, (shard, whole) in enumerate(((sm, wm), (se, we), (ss, ws))):
        own.append(pltpu.make_async_copy(shard, whole.at[x, z, y, c], own_sem.at[n + 1]))
    for copy in own:
        copy.start()
    for k in (1, 2, 3):
        wires.start(k - 1, sa, wa.at[x, z, y, c], lines[k - 1])
    wires.start(3, sa, wa.at[x, z, y, c], over_x)
    wires.start(7, sa, wa.at[x, z, y, c], over_y)
    others = ((sm, wm), (se, we), (ss, ws))
    for n in range(2):
        shard, whole = others[n]
        wires.start(30 + 4 * n, shard, whole.at[x, z, y, c], over_y)

    flags = jnp.broadcast_to(flag_ref[...].astype(F32), (PAIR, rows))
    mask_ref[...] = flags.T[:, :1]
    tubes = tubes_of(patch_ref, mask_ref, token_ref)
    centred = tubes - mean_rows(tubes)
    scale = lax.rsqrt(mean_rows(centred * centred) + 1e-6)
    a1_ref[...] = (centred * scale * vec_ref[0:1] + vec_ref[1:2]).astype(BF)
    wires.start(19, a1_ref.at[halves[0]], landing.at[halves[0]], over_x)
    put(a1_ref, a1_out)

    for k in (1, 2, 3):
        part = wa.at[x, back(k), y, c]
        wires.arrive(k - 1, part)
        wires.start(3 + k, part, part, over_x)
        wires.start(7 + k, part, part, over_y)
    for copy in own:
        copy.wait()
    line = wa.at[x, ALL, y, c]
    wires.start(15, line, line, sibling)
    wires.start(20, a1_ref.at[halves[1]], landing.at[halves[1]], over_x)
    for n, (shard, whole) in enumerate(others):
        for k in (1, 2, 3):
            wires.start(21 + 3 * n + k - 1, shard, whole.at[x, z, y, c], lines[k - 1])
    for k in range(4):
        part = wa.at[1 - x, back(k), y, c]
        wires.arrive(3 + k, part)
        wires.start(11 + k, part, part, over_y)
    line = wa.at[1 - x, ALL, y, c]
    wires.start(16, line, line, sibling)
    for k in range(4):
        wires.arrive(7 + k, wa.at[x, back(k), 1 - y, c])
    line = wa.at[x, ALL, 1 - y, c]
    wires.start(17, line, line, sibling)

    depth = a1_ref.shape[1]

    def columns(h):
        return pl.ds(pl.multiple_of(h * width, PAIR), width)

    def weight(h, n):
        return wa[h, :, :, :, :, n * width : (n + 1) * width].reshape(depth, width)

    def keys_values(h, source, span):
        k_ref[h, span] = dot(source, weight(h, 1)).astype(BF)
        values = dot(source, weight(h, 2)) + vec_ref[3:4, columns(h)]
        v_ref[h, span] = values.astype(BF)

    def project_own(h):
        queries = dot(a1_ref[...], weight(h, 0)) + vec_ref[2:3, columns(h)]
        q_ref[h] = (queries.astype(BF).astype(F32) * HD**-0.5).astype(BF)
        put(q_ref.at[h], q_out.at[h])
        keys_values(h, a1_ref[...], pl.ds(0, rows))
        for ref, out in ((k_ref, k_out), (v_ref, v_out)):
            put(ref.at[h, pl.ds(0, rows)], out.at[h, pl.ds(0, rows)])

    for slot, j in ((15, y), (17, 1 - y)):
        wires.arrive(slot, wa.at[x, ALL, j, 1 - c])
    project_own(x)

    def pass_on(n):
        whole = others[n][1]
        for k in (1, 2, 3):
            part = whole.at[x, back(k), y, c]
            wires.arrive(21 + 3 * n + k - 1, part)
            wires.start(30 + 4 * n + k, part, part, over_y)

    for k in range(4):
        wires.arrive(11 + k, wa.at[1 - x, back(k), 1 - y, c])
    line = wa.at[1 - x, ALL, 1 - y, c]
    wires.start(18, line, line, sibling)
    pass_on(0)
    for slot, j in ((16, y), (18, 1 - y)):
        wires.arrive(slot, wa.at[1 - x, ALL, j, 1 - c])
    out_copy = pltpu.make_async_copy(wa, wa_out, own_sem.at[0])
    out_copy.start()
    project_own(1 - x)
    pass_on(1)
    for n in range(2):
        wires.arrive(19 + n, landing.at[halves[n]])
        part = landing[halves[n]]
        put(landing.at[halves[n]], other_out.at[halves[n]])
        span = pl.ds(rows + (cut if n else 0), part.shape[0])
        for h in range(2):
            keys_values(h, part, span)
            for ref, out in ((k_ref, k_out), (v_ref, v_out)):
                put(ref.at[h, span], out.at[h, span])
    for n in range(2):
        for k in range(4):
            wires.arrive(30 + 4 * n + k, others[n][1].at[x, back(k), 1 - y, c])
    for k in (1, 2, 3):
        wires.arrive(27 + k - 1, ws.at[x, back(k), y, c])
    out_copy.wait()
    for copy in puts:
        copy.wait()
    wires.drain()


def first(masters, patches, flags, token, vectors):
    rows, width = patches.shape
    half = width // 2
    own_rows = masters[1].shape[0]
    shards = [(own_rows, 3 * half), *[m.shape for m in masters[1:]]]
    gathered = [(2, 4, 2, 2, *s) for s in shards]
    wholes = [jax.ShapeDtypeStruct(g, BF) for g in gathered]
    keys = jax.ShapeDtypeStruct((2, 2 * rows, half), BF)
    flat = jax.ShapeDtypeStruct((rows, width), BF)
    return pl.pallas_call(
        first_kernel,
        out_shape=[
            *wholes,
            jax.ShapeDtypeStruct((2, rows, half), BF),
            keys,
            keys,
            flat,
            flat,
            jax.ShapeDtypeStruct((rows, 1), F32),
        ],
        in_specs=[in_vmem()] * 8,
        out_specs=[anywhere()] * 9 + [in_vmem()],
        scratch_shapes=[
            pltpu.VMEM(gathered[0], BF),
            pltpu.VMEM((rows, width), BF),
            pltpu.VMEM((rows, width), BF),
            pltpu.VMEM((2, rows, half), BF),
            pltpu.VMEM((2, 2 * rows, half), BF),
            pltpu.VMEM((2, 2 * rows, half), BF),
            *[pltpu.VMEM(s, BF) for s in shards],
            pltpu.SemaphoreType.DMA((4,)),
            pltpu.SemaphoreType.DMA((17,)),
            pltpu.SemaphoreType.DMA((38,)),
            pltpu.SemaphoreType.DMA((38,)),
        ],
        compiler_params=params(collective_id=0, has_side_effects=True),
        name="first",
    )(*masters, patches, flags, token, vectors)


def add_into(dst, other):
    dst[...] = (dst[...].astype(F32) + other[...].astype(F32)).astype(BF)


def project_kernel(mine_ref, other_ref, w_ref, bias_ref, q_ref, k_ref, v_ref):
    rows = mine_ref.shape[0]
    half = w_ref.shape[2] // 3
    for h in range(2):
        cols = slice(h * half, (h + 1) * half)
        queries = dot(mine_ref[...], w_ref[h, :, :half]) + bias_ref[0:1, cols]
        q_ref[h] = (queries.astype(BF).astype(F32) * HD**-0.5).astype(BF)
        for part, ref in ((0, mine_ref), (1, other_ref)):
            span = slice(part * rows, (part + 1) * rows)
            k_ref[h, span] = dot(ref[...], w_ref[h, :, half : 2 * half]).astype(BF)
            v_ref[h, span] = (dot(ref[...], w_ref[h, :, 2 * half :]) + bias_ref[1:2, cols]).astype(BF)


def project(mine, other, weight, bias):
    rows, width = mine.shape
    keys = jax.ShapeDtypeStruct((2, 2 * rows, width // 2), BF)
    return pl.pallas_call(
        project_kernel,
        out_shape=[jax.ShapeDtypeStruct((2, rows, width // 2), BF), keys, keys],
        in_specs=[in_vmem()] * 4,
        out_specs=[in_vmem()] * 3,
        compiler_params=params(),
        name="project",
    )(mine, other, weight, bias)


def half_lanes():
    lane = lax.broadcasted_iota(jnp.int32, (1, PAIR), 1)
    return lane < HD, lane >= HD


def row_blocks(rows):
    cut = (rows // 2 + 15) // 16 * 16
    return ((0, cut), (cut, rows))


def key_parts(keys):
    cut = keys // 2 // 256 * 256
    return ((0, cut), (cut, keys))


def attend_pair(q_ref, k_ref, v_ref, o_ref, low_ref, inv_ref, p_ref):
    sides = half_lanes()
    k, v = k_ref[0], v_ref[0]
    parts = key_parts(k.shape[0])
    for a, b in row_blocks(q_ref.shape[1]):
        q = q_ref[0, a:b]
        outs, invs = [], []
        for h in range(2):
            q_h = jnp.where(sides[h], q, jnp.zeros_like(q))
            v_h = jnp.where(sides[h], v, jnp.ones_like(v))
            scores = [dot(q_h, k[c:d], NT) for c, d in parts]
            tops = [jnp.max(s, axis=-1, keepdims=True) for s in scores]
            top = functools.reduce(jnp.maximum, tops) * LOG2E
            out = None
            for s, (c, d) in zip(scores, parts):
                p = jnp.exp2(s * LOG2E - top).astype(BF)
                p_ref[h, a:b, c:d] = p
                more = dot(p, v_h[c:d])
                out = more if out is None else out + more
            spare = HD if h == 0 else 0
            inv = 1.0 / out[:, spare : spare + 1]
            outs.append(out * inv)
            invs.append(inv)
        o = jnp.where(sides[0], *outs)
        o_ref[0, a:b] = o
        low_ref[0, a:b] = o.astype(BF)
        inv_ref[0, a:b] = jnp.where(sides[0], *invs)


def attend_kernel(*refs):
    outs, (wm, we, ws, send_sem, recv_sem) = refs[6:10], refs[10:]
    i = pl.program_id(0)
    x, z, y, c = place()
    lines, over_x, over_y, sibling = neighbours()
    wires = Wires(send_sem, recv_sem)
    here, side, flank, across = (x, ALL, y, c), (1 - x, ALL, y, c), (x, ALL, 1 - y, c), (1 - x, ALL, 1 - y, c)
    low, high = pl.ds(0, 2), pl.ds(2, 2)
    near_here, far_here = (x, low, y, c), (x, high, y, c)
    near_side, far_side = (1 - x, low, y, c), (1 - x, high, y, c)
    near_across, far_across = (1 - x, low, 1 - y, c), (1 - x, high, 1 - y, c)

    send = wires.send

    @pl.when(i == 0)
    def _():
        greet_near()
        send(0, we, near_here, over_x)
        send(15, we, far_here, over_x)
        send(1, ws, here, over_y)
        send(2, wm, here, over_x)
        send(3, wm, flank, over_x)
        send(4, wm, here, sibling)
        send(5, wm, flank, sibling)
        send(6, we, here, sibling)
        send(7, we, flank, sibling)
        send(8, ws, here, sibling)

    @pl.when(i == 2)
    def _():
        wires.arrive(0, we.at[near_side])
        send(9, we, near_side, over_y)

    @pl.when(i == 4)
    def _():
        wires.arrive(15, we.at[far_side])
        send(16, we, far_side, over_y)
        send(10, we, side, sibling)
        wires.arrive(1, ws.at[flank])
        send(11, ws, flank, sibling)

    @pl.when(i == 5)
    def _():
        wires.arrive(2, wm.at[side])
        send(12, wm, side, sibling)

    attend_pair(*refs[:3], *outs)

    @pl.when(i == pl.num_programs(0) - 1)
    def _():
        wires.arrive(3, wm.at[across])
        send(13, wm, across, sibling)
        wires.arrive(9, we.at[near_across])
        wires.arrive(16, we.at[far_across])
        send(14, we, across, sibling)
        for slot, whole, (a, b) in (
            (4, wm, (x, y)),
            (5, wm, (x, 1 - y)),
            (6, we, (x, y)),
            (7, we, (x, 1 - y)),
            (8, ws, (x, y)),
            (10, we, (1 - x, y)),
            (11, ws, (x, 1 - y)),
            (12, wm, (1 - x, y)),
            (13, wm, (1 - x, 1 - y)),
            (14, we, (1 - x, 1 - y)),
        ):
            wires.arrive(slot, whole.at[a, ALL, b, 1 - c])
        wires.drain()


def attend(q, k, v, wholes):
    _, rows, half = q.shape
    keys = k.shape[1]
    per = half // PAIR
    of_q = pl.BlockSpec((1, rows, PAIR), lambda i: (i // per, 0, lax.rem(i, per)))
    of_k = pl.BlockSpec((1, keys, PAIR), lambda i: (i // per, 0, lax.rem(i, per)))
    shapes = [
        jax.ShapeDtypeStruct(q.shape, F32),
        jax.ShapeDtypeStruct(q.shape, BF),
        jax.ShapeDtypeStruct(q.shape, F32),
        jax.ShapeDtypeStruct((4 * per, rows, keys), BF),
    ]
    of_p = pl.BlockSpec((2, rows, keys), lambda i: (i, 0, 0))
    common = dict(grid=(2 * per,), name="attend")
    if not wholes:
        return pl.pallas_call(
            attend_pair,
            in_specs=[of_q, of_k, of_k],
            out_specs=[of_q, of_q, of_q, of_p],
            out_shape=shapes,
            compiler_params=params(),
            **common,
        )(q, k, v)
    return pl.pallas_call(
        attend_kernel,
        in_specs=[of_q, of_k, of_k, *[anywhere()] * 3],
        out_specs=[of_q, of_q, of_q, of_p, *[anywhere()] * 3],
        out_shape=[*shapes, *[jax.ShapeDtypeStruct(w.shape, BF) for w in wholes]],
        input_output_aliases={3: 4, 4: 5, 5: 6},
        scratch_shapes=[pltpu.SemaphoreType.DMA((17,)), pltpu.SemaphoreType.DMA((17,))],
        compiler_params=params(collective_id=2, has_side_effects=True),
        **common,
    )(q, k, v, *wholes)


def attend_back_pair(q_ref, k_ref, v_ref, do_ref, o_ref, p_ref, dq_ref, dk_ref, dv_ref):
    sides = half_lanes()
    k, v = k_ref[0], v_ref[0]
    parts = key_parts(k.shape[0])
    grad_k = [[None] * 2 for _ in parts]
    grad_v = [[None] * 2 for _ in parts]

    def plus(total, more):
        return more if total is None else total + more

    for a, b in row_blocks(q_ref.shape[1]):
        q, do = q_ref[0, a:b], do_ref[0, a:b]
        prod = do.astype(F32) * o_ref[0, a:b]
        q_t, do_t = q.T, do.T
        outs = []
        for h in range(2):
            do_h = jnp.where(sides[h], do, jnp.zeros_like(do))
            row_dot = jnp.sum(jnp.where(sides[h], prod, 0.0), axis=-1, keepdims=True)
            out = None
            rows = slice(h * HD, (h + 1) * HD)
            for n, (c, d) in enumerate(parts):
                p = p_ref[h, a:b, c:d]
                grad_p = dot(do_h, v[c:d], NT)
                ds = (p.astype(F32) * (grad_p - row_dot)).astype(BF)
                out = plus(out, dot(ds, k[c:d]))
                grad_k[n][h] = plus(grad_k[n][h], dot(q_t[rows], ds))
                grad_v[n][h] = plus(grad_v[n][h], dot(do_t[rows], p))
            outs.append(out)
        dq_ref[0, a:b] = (jnp.where(sides[0], *outs) * HD**-0.5).astype(BF)
    for n, (c, d) in enumerate(parts):
        dk_ref[0, c:d] = jnp.concatenate(grad_k[n], axis=0).T.astype(BF)
        dv_ref[0, c:d] = jnp.concatenate(grad_v[n], axis=0).T.astype(BF)


def attend_back_kernel(*refs):
    ins, (mine, early_side, early_far, grad_m) = refs[:6], refs[6:10]
    outs, total_s, total_e, total_m = refs[10:13], refs[13], refs[14], refs[15]
    here, away, side_y, side_x, diag = refs[16:21]
    zown, zfar, last_x, last_y, last_d = refs[21:26]
    here_m, sib_m, diag_m, side_m = refs[26:30]
    own_sem, send_sem, recv_sem = refs[30:]
    i = pl.program_id(0)
    x, z, y, c = place()
    lines, over_x, over_y, sibling = neighbours()
    over_xy = device(1 - x, z, 1 - y, c)
    wires = Wires(send_sem, recv_sem)
    width = here.shape[-1]

    def own():
        pairs = (
            (early_far, zfar.at[0]),
            (mine.at[:, :, 0, z], zown),
            (early_side, side_y),
            (mine.at[x, :, 1, :, y], here),
            (mine.at[1 - x, :, 1, :, y], away),
            (grad_m.at[:, :, :, c], here_m),
        )
        return [pltpu.make_async_copy(a, b, own_sem.at[n]) for n, (a, b) in enumerate(pairs)]

    def along_z(h, n, b):
        def sweep(j, _):
            total = zown[n, b, j].astype(F32)
            for k in range(3):
                total = total + zfar[h, b, k, j].astype(F32)
            zown[n, b, j] = total.astype(BF)
            return 0

        lax.fori_loop(0, 2, sweep, 0)

    def spread(b, slot):
        for k in (1, 2, 3):
            wires.arrive(10 + 3 * b + k, zfar.at[1, b, k - 1])
        along_z(1, 1 - x, b)
        wires.start(slot, zown.at[1 - x, b, y], last_x.at[b], over_x)
        wires.start(slot + 1, zown.at[1 - x, b, 1 - y], last_d.at[b], over_xy)

    def to_x(b, slot):
        def sweep(m, _):
            add_into(away.at[b, m], diag.at[b, m])
            return 0

        lax.fori_loop(0, 4, sweep, 0)
        wires.start(slot, away.at[b], side_x.at[b], over_x)

    def far_source(b, k):
        return mine.at[1 - x, b, 0, lax.rem(z + k, 4)]

    expand_diag = [mine.at[1 - x, b, 1, :, 1 - y] for b in range(2)]

    @pl.when(i == 0)
    def _():
        copies = own()
        for copy in copies:
            copy.start()
        barrier = pltpu.get_barrier_semaphore()
        for other in (*lines, over_x, over_y, sibling, over_xy):
            pl.semaphore_signal(barrier, inc=1, device_id=other, device_id_type=MESH)
        pl.semaphore_wait(barrier, 7)
        wires.start(0, grad_m.at[:, :, :, 1 - c], sib_m, sibling)
        wires.start(19, expand_diag[0], diag.at[0], over_y)
        wires.start(1, expand_diag[1], diag.at[1], over_y)
        for b in range(2):
            for k in (1, 2, 3):
                wires.start(10 + 3 * b + k, far_source(b, k), zfar.at[1, b, k - 1], lines[k - 1])

    @pl.when(i == 1)
    def _():
        for copy in own():
            copy.wait()
        for b in range(2):
            along_z(0, x, b)
        wires.arrive(0, sib_m)

        def sweep(m, _):
            part = (m // 8, lax.rem(m // 2, 4), lax.rem(m, 2))
            add_into(here_m.at[part], sib_m.at[part])
            return 0

        lax.fori_loop(0, 16, sweep, 0)
        wires.start(2, here_m.at[1 - x, :, 1 - y], diag_m, over_y)
        wires.start(3, zown.at[x, :, 1 - y], last_y, over_y)
        wires.start(4, here_m.at[x, :, 1 - y], side_m.at[1], over_y)

    @pl.when(i == 2)
    def _():
        wires.arrive(19, diag.at[0])
        to_x(0, 5)

    @pl.when(i == 3)
    def _():
        wires.arrive(1, diag.at[1])
        to_x(1, 9)

    @pl.when(i == 4)
    def _():
        wires.arrive(2, diag_m)

        def sweep(m, _):
            add_into(here_m.at[1 - x, m, y], diag_m.at[m])
            return 0

        lax.fori_loop(0, 4, sweep, 0)
        wires.start(6, here_m.at[1 - x, :, y], side_m.at[0], over_x)
        spread(0, 7)

    @pl.when(i == 5)
    def _():
        spread(1, 17)

    attend_back_pair(*ins, *outs)

    @pl.when(i == pl.num_programs(0) - 1)
    def _():
        wires.arrive(5, side_x.at[0])
        wires.arrive(9, side_x.at[1])

        def sweep(m, _):
            part = (m // 4, lax.rem(m, 4))
            both = side_x[part].astype(F32) + side_y[part].astype(F32)
            total_e[part] = (here[part].astype(F32) + both).astype(BF)
            return 0

        lax.fori_loop(0, 8, sweep, 0)
        wires.arrive(4, side_m.at[1])
        wires.arrive(6, side_m.at[0])
        for n in range(4):
            both = side_m[0, n].astype(F32) + side_m[1, n].astype(F32)
            total_m[n] = (here_m[x, n, y].astype(F32) + both).astype(BF)
        wires.arrive(3, last_y)
        for b, slot in ((0, 7), (1, 17)):
            wires.arrive(slot, last_x.at[b])
            wires.arrive(slot + 1, last_d.at[b])
        for b in range(2):
            one = zown[x, b, y].astype(F32) + last_y[b].astype(F32)
            two = last_x[b].astype(F32) + last_d[b].astype(F32)
            total_s[:, b * width : (b + 1) * width] = one + two
        wires.sent(0, grad_m.at[:, :, :, 1 - c])
        wires.sent(19, expand_diag[0])
        wires.sent(1, expand_diag[1])
        wires.sent(2, here_m.at[1 - x, :, 1 - y])
        wires.sent(3, zown.at[x, :, 1 - y])
        wires.sent(4, here_m.at[x, :, 1 - y])
        wires.sent(5, away.at[0])
        wires.sent(9, away.at[1])
        wires.sent(6, here_m.at[1 - x, :, y])
        for b, slot in ((0, 7), (1, 17)):
            wires.sent(slot, zown.at[1 - x, b, y])
            wires.sent(slot + 1, zown.at[1 - x, b, 1 - y])
        for b in range(2):
            for k in (1, 2, 3):
                wires.sent(10 + 3 * b + k, far_source(b, k))


def attend_back(q, k, v, do, o, p, grads):
    _, rows, half = q.shape
    keys = k.shape[1]
    per = half // PAIR
    of_q = pl.BlockSpec((1, rows, PAIR), lambda i: (i // per, 0, lax.rem(i, per)))
    of_k = pl.BlockSpec((1, keys, PAIR), lambda i: (i // per, 0, lax.rem(i, per)))
    of_p = pl.BlockSpec((2, rows, keys), lambda i: (i, 0, 0))
    shapes = [
        jax.ShapeDtypeStruct(q.shape, BF),
        jax.ShapeDtypeStruct(k.shape, BF),
        jax.ShapeDtypeStruct(k.shape, BF),
    ]
    common = dict(grid=(2 * per,), name="attend_back")
    if not grads:
        return pl.pallas_call(
            attend_back_pair,
            in_specs=[of_q, of_k, of_k, of_q, of_q, of_p],
            out_specs=[of_q, of_k, of_k],
            out_shape=shapes,
            compiler_params=params(),
            **common,
        )(q, k, v, do, o, p)
    mine, grad_m = grads[0], grads[3]
    parts, unit = mine.shape[1], mine.shape[5:]
    lined = (parts, 4, *unit)
    own_rows, w = grad_m.shape[4:]
    lined_m = (4, own_rows, w)
    totals = [
        jax.ShapeDtypeStruct((own_rows, parts * unit[1]), F32),
        jax.ShapeDtypeStruct(lined, BF),
        jax.ShapeDtypeStruct(lined_m, BF),
    ]
    return pl.pallas_call(
        attend_back_kernel,
        in_specs=[of_q, of_k, of_k, of_q, of_q, of_p, *[anywhere()] * 4],
        out_specs=[of_q, of_k, of_k, *[pl.BlockSpec(t.shape, lambda i, t=t: (0,) * t.ndim) for t in totals]],
        out_shape=[*shapes, *totals],
        scratch_shapes=[
            *[pltpu.VMEM(lined, BF)] * 5,
            pltpu.VMEM((2, parts, 2, *unit), BF),
            pltpu.VMEM((2, parts, 3, 2, *unit), BF),
            *[pltpu.VMEM((parts, *unit), BF)] * 3,
            pltpu.VMEM((2, 4, 2, own_rows, w), BF),
            pltpu.VMEM((2, 4, 2, own_rows, w), BF),
            pltpu.VMEM(lined_m, BF),
            pltpu.VMEM((2, *lined_m), BF),
            pltpu.SemaphoreType.DMA((6,)),
            pltpu.SemaphoreType.DMA((20,)),
            pltpu.SemaphoreType.DMA((20,)),
        ],
        compiler_params=params(collective_id=3, has_side_effects=True),
        **common,
    )(q, k, v, do, o, p, *grads)


def normal_parts(h):
    z = jnp.abs(h) * 0.7071067811865476
    t = 1.0 / (1.0 + 0.3275911 * z)
    bell = jnp.exp(-z * z)
    poly = t * (
        0.254829592
        + t * (-0.284496736 + t * (1.421413741 + t * (-1.453152027 + t * 1.061405429)))
    )
    tail = 0.5 * poly * bell
    return jnp.where(h < 0, tail, 1.0 - tail), bell * 0.3989422804014327


def mean_rows(values):
    return jnp.mean(values, axis=-1, keepdims=True)


def tubes_of(patch_ref, mask_ref, token_ref):
    return jnp.where(mask_ref[...] > 0, token_ref[...][None], patch_ref[...].astype(F32))


class Middle:
    def __init__(self, ins, outs, scratch):
        self.patch, self.mask, self.token, self.o, self.inv, self.dy, self.vec, self.wm = ins
        self.out, self.dx1, self.do, self.gm, self.gv = outs
        self.x1, self.a2, self.acc, self.da2 = scratch

    def open(self):
        x1 = tubes_of(self.patch, self.mask, self.token) + self.vec[4:5]
        for h in range(2):
            x1 = x1 + dot(self.o[h], self.wm[h], NT)
        self.x1[...] = x1
        centred = x1 - mean_rows(x1)
        scale = lax.rsqrt(mean_rows(centred * centred) + 1e-6)
        self.a2[...] = (centred * scale * self.vec[5:6] + self.vec[6:7]).astype(BF)
        self.acc[...] = x1 + self.vec[11:12]
        self.da2[...] = jnp.zeros_like(self.da2)

    def block(self, n, we, ws, keep, hook):
        a2, dy = self.a2[...], self.dy[...]
        hidden = dot(a2, we) + self.vec[pl.ds(7 + n, 1)]
        cdf, density = normal_parts(hidden)
        u = (hidden * cdf).astype(BF)
        du = dot(dy, ws)
        dh = (du * (cdf + hidden * density)).astype(BF)
        self.gv[pl.ds(4 + n, 1)] = jnp.sum(dh.astype(F32), axis=0, keepdims=True)
        keep(0, dot(dy, u, TN).astype(BF))
        keep(1, dot(a2, dh, TN).astype(BF))
        hook()
        self.acc[...] += dot(u, ws, NT)
        self.da2[...] += dot(dh, we, NT)

    def close(self):
        self.out[...] = self.acc[...].astype(BF)
        x1, top, da2 = self.x1[...], self.dy[...].astype(F32), self.da2[...]
        centred = x1 - mean_rows(x1)
        scale = lax.rsqrt(mean_rows(centred * centred) + 1e-6)
        xh = centred * scale
        e = da2 * self.vec[5:6]
        dx1 = top + scale * (e - mean_rows(e) - xh * mean_rows(e * xh))
        self.dx1[...] = dx1
        dxb = dx1.astype(BF)
        for h in range(2):
            self.do[h] = (dot(dxb, self.wm[h]) * self.inv[h]).astype(BF)
            self.gm[h] = dot(dxb, self.o[h], TN).astype(BF)
        self.gv[0:1] = jnp.sum(dxb.astype(F32), axis=0, keepdims=True)
        self.gv[1:2] = jnp.sum(da2 * xh, axis=0, keepdims=True)
        self.gv[2:3] = jnp.sum(da2, axis=0, keepdims=True)
        self.gv[3:4] = jnp.sum(top, axis=0, keepdims=True)


def middle_plain_kernel(*refs):
    we_ref, ws_ref = refs[8:10]
    ge_ref, gs_ref = refs[15:17]
    body = Middle(refs[:8], refs[10:15], refs[17:])
    i = pl.program_id(0)
    pl.when(i == 0)(body.open)

    def keep(n, grad):
        (gs_ref, ge_ref)[n][0] = grad

    body.block(i, we_ref[0], ws_ref[0], keep, lambda: None)
    pl.when(i == pl.num_programs(0) - 1)(body.close)


def middle_kernel(*refs):
    we_ref, ws_in = refs[8:10]
    body = Middle(refs[:8], refs[10:15], refs[18:22])
    mine, early_side, early_far = refs[15:18]
    ws, raw, sib, load_sem, put_sem, send_sem, recv_sem = refs[22:]
    i = pl.program_id(0)
    x, z, y, c = place()
    lines, over_x, over_y, sibling = neighbours()
    wires = Wires(send_sem, recv_sem)
    width = raw.shape[-1]
    half = lax.rem(x + i // 2, 2)
    part = lax.rem(i, 2)

    def cols(n):
        return pl.ds(n * width, width)

    def load():
        return pltpu.make_async_copy(ws_in.at[x], ws.at[x], load_sem)

    def put(n):
        h = x if n < 2 else 1 - x
        return pltpu.make_async_copy(raw.at[n % 2, :, :, :, c], mine.at[h, n % 2], put_sem.at[n % 2])

    def to_sibling(n):
        return raw.at[n % 2, :, :, :, 1 - c]

    def offer(n):
        wires.copy(10 + n, to_sibling(n), sib.at[n % 2], sibling).start()

    def finish(n):
        slot = n % 2
        wires.arrive(10 + n, sib.at[slot])
        wires.sent(10 + n, to_sibling(n))

        def sweep(m, _):
            at = (m // 8, lax.rem(m // 2, 4), lax.rem(m, 2))
            add_into(raw.at[slot, at[0], at[1], at[2], c], sib.at[slot, at[0], at[1], at[2]])
            return 0

        lax.fori_loop(0, 16, sweep, 0)
        put(n).start()

    def far_source(n, k):
        return mine.at[x, n, 0, lax.rem(z + k, 4)]

    def send_far(n):
        for k in (1, 2, 3):
            wires.start(14 + 3 * n + k, far_source(n, k), early_far.at[n, k - 1], lines[k - 1])

    def across(n, core):
        return ws.at[1 - x, :, 1 - y, core, :, cols(n)]

    def side(n, core):
        return ws.at[1 - x, :, y, core, :, cols(n)]

    def own_part(n):
        return ws_in.at[x, :, y, c, :, cols(n)]

    @pl.when(i == 0)
    def _():
        load().start()
        greet()
        for n, slot in enumerate((0, 9)):
            wires.start(slot, own_part(n), ws.at[x, :, y, c, :, cols(n)], over_x)
        body.open()
        load().wait()

    @pl.when(i == 2)
    def _():
        wires.arrive(3, side(0, 1 - c))
        wires.arrive(4, across(0, 1 - c))

    @pl.when(i == 3)
    def _():
        wires.arrive(7, side(1, 1 - c))
        wires.arrive(5, across(1, 1 - c))

    def hook():
        @pl.when(i == 0)
        def _():
            wires.arrive(0, side(0, c))
            wires.start(1, side(0, c), side(0, c), over_y)
            wires.start(3, side(0, c), side(0, c), sibling)
            offer(0)

        @pl.when(i == 1)
        def _():
            finish(0)
            offer(1)
            wires.arrive(9, side(1, c))
            wires.start(2, side(1, c), side(1, c), over_y)
            wires.start(7, side(1, c), side(1, c), sibling)
            wires.arrive(1, across(0, c))
            wires.start(4, across(0, c), across(0, c), sibling)
            put(0).wait()
            send_far(0)

        @pl.when(i == 2)
        def _():
            finish(1)
            offer(2)
            wires.arrive(2, across(1, c))
            wires.start(5, across(1, c), across(1, c), sibling)
            put(1).wait()
            send_far(1)
            wires.start(6, mine.at[x, :, 1, :, 1 - y], early_side, over_y)

        @pl.when(i == 3)
        def _():
            finish(2)
            offer(3)

    def keep(n, grad):
        raw[part, n] = grad.reshape(raw.shape[2:])

    weight = ws[half, :, :, :, :, pl.ds(pl.multiple_of(part * width, width), width)].reshape(-1, width)
    body.block(half * 2 + part, we_ref[0], weight, keep, hook)

    @pl.when(i == pl.num_programs(0) - 1)
    def _():
        body.close()
        put(2).wait()
        finish(3)
        wires.arrive(6, early_side)
        for n in range(2):
            for k in (1, 2, 3):
                wires.arrive(14 + 3 * n + k, early_far.at[n, k - 1])
                wires.sent(14 + 3 * n + k, far_source(n, k))
        for n in range(2):
            wires.sent((0, 9)[n], own_part(n))
            wires.sent(1 + n, side(n, c))
            wires.sent((3, 7)[n], side(n, c))
            wires.sent(4 + n, across(n, c))
        wires.sent(6, mine.at[x, :, 1, :, 1 - y])
        put(3).wait()


def middle(patches, mask, token, o, inv, dy, vectors, wm, we, ws, direct):
    rows, width = patches.shape
    hidden = we.shape[2]
    per = hidden // width

    def whole(shape):
        return pl.BlockSpec(shape, lambda i: (0,) * len(shape))

    def of_w(i):
        turn = i // per
        if direct:
            turn = lax.rem(turn + lax.axis_index("mp"), 2)
        return (turn, 0, lax.rem(i, per))

    by_block = pl.BlockSpec((1, width, width), of_w)
    ins = [patches, mask, token, o, inv, dy, vectors, wm, we, ws]
    shapes = [
        jax.ShapeDtypeStruct((rows, width), BF),
        jax.ShapeDtypeStruct((rows, width), F32),
        jax.ShapeDtypeStruct(o.shape, BF),
        jax.ShapeDtypeStruct(wm.shape, BF),
        jax.ShapeDtypeStruct((8, width), F32),
    ]
    in_specs = [pl.BlockSpec(v.shape, lambda i, v=v: (0,) * v.ndim, pipeline_mode=pl.Buffered(1)) for v in ins[:8]]
    out_specs = [whole(v.shape) for v in shapes]
    scratch = [
        pltpu.VMEM((rows, width), F32),
        pltpu.VMEM((rows, width), BF),
        pltpu.VMEM((rows, width), F32),
        pltpu.VMEM((rows, width), F32),
    ]
    common = dict(grid=(2 * per,), name="middle")
    if not direct:
        return pl.pallas_call(
            middle_plain_kernel,
            in_specs=[*in_specs, by_block, by_block],
            out_specs=[*out_specs, by_block, by_block],
            out_shape=[*shapes, *[jax.ShapeDtypeStruct(we.shape, BF)] * 2],
            scratch_shapes=scratch,
            compiler_params=params(),
            **common,
        )(*ins)
    own_rows = ws.shape[4]
    unit = (own_rows, width)
    return pl.pallas_call(
        middle_kernel,
        in_specs=[*in_specs, by_block, anywhere()],
        out_specs=[*out_specs, *[anywhere()] * 3],
        out_shape=[
            *shapes,
            jax.ShapeDtypeStruct((2, per, 2, 4, 2, *unit), BF),
            jax.ShapeDtypeStruct((per, 4, *unit), BF),
            jax.ShapeDtypeStruct((per, 3, 2, *unit), BF),
        ],
        scratch_shapes=[
            *scratch,
            pltpu.VMEM(ws.shape, BF),
            pltpu.VMEM((2, 2, 4, 2, 2, *unit), BF),
            pltpu.VMEM((2, 2, 4, 2, *unit), BF),
            pltpu.SemaphoreType.DMA,
            pltpu.SemaphoreType.DMA((2,)),
            pltpu.SemaphoreType.DMA((21,)),
            pltpu.SemaphoreType.DMA((21,)),
        ],
        compiler_params=params(collective_id=4, has_side_effects=True),
        **common,
    )(*ins)


def unproject_kernel(
    mine_ref, other_ref, dq_ref, dk_ref, dv_ref, w_ref, da_ref, send_ref, gw_ref, gv_ref
):
    rows = mine_ref.shape[0]
    half = w_ref.shape[2] // 3
    da, send = None, None
    gv_ref[...] = jnp.zeros_like(gv_ref)
    for h in range(2):
        cols = slice(h * half, (h + 1) * half)
        dq, dk, dv = dq_ref[h], dk_ref[h], dv_ref[h]
        wq, wk, wv = (w_ref[h, :, n * half : (n + 1) * half] for n in range(3))
        mine = dot(dq, wq, NT) + dot(dk[:rows], wk, NT) + dot(dv[:rows], wv, NT)
        other = dot(dk[rows:], wk, NT) + dot(dv[rows:], wv, NT)
        da = mine if da is None else da + mine
        send = other if send is None else send + other
        a, b = mine_ref[...], other_ref[...]
        gw_ref[h, :, :half] = dot(a, dq, TN).astype(BF)
        gw_ref[h, :, half : 2 * half] = (dot(a, dk[:rows], TN) + dot(b, dk[rows:], TN)).astype(BF)
        gw_ref[h, :, 2 * half :] = (dot(a, dv[:rows], TN) + dot(b, dv[rows:], TN)).astype(BF)
        gv_ref[0:1, cols] = jnp.sum(dq.astype(F32), axis=0, keepdims=True)
        gv_ref[1:2, cols] = jnp.sum(dv.astype(F32), axis=0, keepdims=True)
    da_ref[...] = da
    send_ref[...] = send.astype(BF)


def unproject(mine, other, dq, dk, dv, weight):
    rows, width = mine.shape
    return pl.pallas_call(
        unproject_kernel,
        out_shape=[
            jax.ShapeDtypeStruct((rows, width), F32),
            jax.ShapeDtypeStruct((rows, width), BF),
            jax.ShapeDtypeStruct(weight.shape, BF),
            jax.ShapeDtypeStruct((8, width), F32),
        ],
        in_specs=[in_vmem()] * 6,
        out_specs=[in_vmem()] * 4,
        compiler_params=params(),
        name="unproject",
    )(mine, other, dq, dk, dv, weight)


def lamb_parts(weight, moment, square, grad):
    correct = 1.0 - 0.5**STEP
    moment_new = 0.5 * moment + 0.5 * grad
    square_new = 0.5 * square + 0.5 * grad * grad
    update = moment_new / correct / (jnp.sqrt(square_new / correct) + 1e-06) + 0.01 * weight
    return moment_new, square_new, update


def whole_sum(values):
    return jnp.sum(jnp.sum(values, axis=0, keepdims=True), axis=1, keepdims=True)


def last_kernel(*refs):
    sources, refs = refs[:8], refs[8:]
    (mask_ref, token_ref, vec_ref, tail_ref), refs = refs[:4], refs[4:]
    (total_s, lined, lined_m), refs = refs[:3], refs[3:]
    masters, firsts, seconds, refs = refs[:4], refs[4:8], refs[8:12], refs[12:]
    pg_ref, early_ref, late_ref, *totals = refs[:6]
    totals.append(total_s)
    refs = refs[6:]
    loaded, refs = refs[:8], refs[8:]
    dk_ref, dv_ref, w_ref, a_ref, b_ref, dq_ref, patch_ref, dx1_ref = loaded
    gw, sib, diag, side, da_ref, send_ref, landing = refs[:7]
    far, refs = refs[7:10], refs[10:]
    held, came, final, late, late_line, load_sem, send_sem, recv_sem = refs
    x, z, y, c = place()
    lines, over_x, over_y, sibling = neighbours()
    wires = Wires(send_sem, recv_sem)
    rows, depth = a_ref.shape
    half = w_ref.shape[2] // 3
    cut = rows // 64 * 16
    spans = (pl.ds(0, cut), pl.ds(cut, rows - cut))
    loads = [pltpu.make_async_copy(s, d, load_sem.at[n]) for n, (s, d) in enumerate(zip(sources, loaded))]
    for load in loads:
        load.start()

    def flipped(code):
        def flip(v, bit):
            return 1 - v if bit else v

        return device(flip(x, code // 4), z, flip(y, code // 2 % 2), flip(c, code % 2))

    barrier = pltpu.get_barrier_semaphore()
    for other in (*lines, *[flipped(code) for code in range(1, 8)]):
        pl.semaphore_signal(barrier, inc=1, device_id=other, device_id_type=MESH)
    pl.semaphore_wait(barrier, 10)

    def ahead(k):
        return lax.rem(z + k, 4)

    for k in (1, 2, 3):
        wires.start(3 + k - 1, lined_m.at[ahead(k)], far[1].at[k - 1], lines[k - 1])
        wires.start(6 + k - 1, lined.at[:, ahead(k)], far[2].at[k - 1], lines[k - 1])

    def settle(n, own):
        total = own.astype(F32)
        for k in range(3):
            wires.arrive(3 * n + k, far[n].at[k])
            total = total + far[n][k].astype(F32)
        if n == 0:
            for part in range(3):
                totals[n][part] = total[:, part * half : (part + 1) * half]
        elif n == 1:
            totals[n][...] = total
        else:
            for part in range(total.shape[0]):
                totals[2][:, part * depth : (part + 1) * depth] = total[part]

    lane = lax.broadcasted_iota(jnp.int32, (8, PAIR), 1)
    squares = jnp.zeros((8, PAIR), F32)

    def add_squares(squares, n, pick):
        weight = masters[n][pick]
        update = lamb_parts(weight, firsts[n][pick], seconds[n][pick], totals[n][pick])[2]
        squares = squares + jnp.where(lane == 2 * n, whole_sum(weight * weight), 0.0)
        return squares + jnp.where(lane == 2 * n + 1, whole_sum(update * update), 0.0)

    def columns(n):
        return slice(n * half, (n + 1) * half)

    for n in range(3):
        loads[n].wait()
    for n, (start, size) in enumerate(((rows, cut), (rows + cut, rows - cut))):
        span = pl.ds(start, size)
        send = None
        for h in range(2):
            part = dot(dk_ref[h, span], w_ref[h, :, columns(1)], NT) + dot(dv_ref[h, span], w_ref[h, :, columns(2)], NT)
            send = part if send is None else send + part
        send_ref[spans[n]] = send.astype(BF)
        wires.start(12 + n, send_ref.at[spans[n]], landing.at[spans[n]], over_x)
    for n in range(3, 6):
        loads[n].wait()
    held[0] = jnp.zeros(held.shape[1:], F32)
    for h in range(2):
        held[0, 2:3, columns(h)] = jnp.sum(dq_ref[h].astype(F32), axis=0, keepdims=True)
        held[0, 3:4, columns(h)] = jnp.sum(dv_ref[h].astype(F32), axis=0, keepdims=True)
    held[0, 4:7] = tail_ref[0:3]
    held[0, 7:11] = tail_ref[4:8]
    held[0, 11:12] = tail_ref[3:4]
    wires.start(25, held.at[0], came.at[0], sibling)
    a, b = a_ref[...], b_ref[...]
    own, other = pl.ds(0, rows), pl.ds(rows, rows)

    def weight_grad(h, n):
        if n == 0:
            grad = dot(a, dq_ref[h], TN)
        else:
            ref = dk_ref if n == 1 else dv_ref
            grad = dot(a, ref[h, own], TN) + dot(b, ref[h, other], TN)
        gw[h, :, :, :, :, columns(n)] = grad.astype(BF).reshape(4, 2, 2, -1, half)

    def with_sibling(h, slot):
        wires.arrive(slot, sib.at[h])

        def sweep(m, _):
            add_into(gw.at[h, m // 2, lax.rem(m, 2), c], sib.at[h, m // 2, lax.rem(m, 2)])
            return 0

        lax.fori_loop(0, 8, sweep, 0)

    for n in range(3):
        weight_grad(1 - x, n)
    wires.start(14, gw.at[1 - x, :, :, 1 - c], sib.at[1 - x], sibling)
    wires.arrive(25, came.at[0])
    held[1] = held[0] + came[0]
    wires.start(26, held.at[1], came.at[1], over_y)
    weight_grad(x, 0)
    with_sibling(1 - x, 14)
    order = (1, 2, 3, 0)
    for k in order:
        wires.start(16 + k, gw.at[1 - x, ahead(k), 1 - y, c], diag.at[ahead(k)], over_y)
    weight_grad(x, 1)
    weight_grad(x, 2)
    wires.start(15, gw.at[x, :, :, 1 - c], sib.at[x], sibling)
    da = None
    for h in range(2):
        part = (
            dot(dq_ref[h], w_ref[h, :, columns(0)], NT)
            + dot(dk_ref[h, own], w_ref[h, :, columns(1)], NT)
            + dot(dv_ref[h, own], w_ref[h, :, columns(2)], NT)
        )
        da = part if da is None else da + part
    da_ref[...] = da
    wires.arrive(26, came.at[1])
    held[2] = held[1] + came[1]
    wires.start(27, held.at[2], came.at[2], over_x)
    with_sibling(x, 15)
    for k in order:
        wires.start(41 + k, gw.at[x, ahead(k), 1 - y, c], side.at[1, ahead(k)], over_y)
    for k in order:
        wires.arrive(16 + k, diag.at[ahead(k)])
        part = gw.at[1 - x, ahead(k), y, c]
        add_into(part, diag.at[ahead(k)])
        wires.start(20 + k, part, side.at[0, ahead(k)], over_x)
    settle(1, lined_m[z])
    settle(2, lined[:, z])
    for n in (1, 2, 3):
        squares = add_squares(squares, n, ...)
    for n in range(6, 8):
        loads[n].wait()
    tubes = tubes_of(patch_ref, mask_ref, token_ref)
    centred = tubes - mean_rows(tubes)
    scale = lax.rsqrt(mean_rows(centred * centred) + 1e-6)
    xh = centred * scale
    for n in range(2):
        wires.arrive(12 + n, landing.at[spans[n]])
    da = da_ref[...] + landing[...].astype(F32)
    me = x * 4 + y * 2 + c
    deep = depth // PAIR

    def late_row(n, values):
        for j in range(deep):
            late[me, n * deep + j : n * deep + j + 1] = values[:, j * PAIR : (j + 1) * PAIR]

    late_row(0, jnp.sum(da * xh, axis=0, keepdims=True))
    late_row(1, jnp.sum(da, axis=0, keepdims=True))
    e = da * vec_ref[0:1]
    dx = dx1_ref[...] + scale * (e - mean_rows(e) - xh * mean_rows(e * xh))
    masked = mask_ref[...] > 0
    pg_ref[...] = jnp.where(masked, 0.0, dx).astype(BF)
    late_row(2, jnp.sum(jnp.where(masked, dx, 0.0), axis=0, keepdims=True))
    wires.arrive(27, came.at[2])
    final[z] = held[2] + came[2]
    for k in (1, 2, 3):
        wires.start(27 + k, final.at[z], final.at[z], lines[k - 1])

    def with_sides(k):
        wires.arrive(41 + k, side.at[1, ahead(k)])
        wires.arrive(20 + k, side.at[0, ahead(k)])
        both = side[0, ahead(k)].astype(F32) + side[1, ahead(k)].astype(F32)
        part = gw.at[x, ahead(k), y, c]
        part[...] = (part[...].astype(F32) + both).astype(BF)
        if k:
            wires.start(k - 1, part, far[0].at[k - 1], lines[k - 1])

    for k in order:
        with_sides(k)
    for k in (1, 2, 3):
        wires.arrive(27 + k, final.at[ahead(4 - k)])
    early_ref[...] = final[0] + final[1] + final[2] + final[3]
    settle(0, gw[x, z, y, c])
    for part in range(3):
        squares = add_squares(squares, 0, part)
    late[me, 3 * deep : 3 * deep + 1] = squares[0:1]
    late[me, 3 * deep + 1 :] = jnp.zeros((late.shape[1] - 3 * deep - 1, PAIR), F32)
    for code in range(1, 8):
        wires.start(30 + code, late.at[me], late.at[me], flipped(code))

    def flip_index(code):
        return sum((1 - v if bit else v) * w for v, bit, w in ((x, code // 4, 4), (y, code // 2 % 2, 2), (c, code % 2, 1)))

    for code in range(1, 8):
        wires.arrive(30 + code, late.at[flip_index(code)])
    total = late[0]
    for n in range(1, 8):
        total = total + late[n]
    late_line[z] = total
    for k in (1, 2, 3):
        wires.start(37 + k, late_line.at[z], late_line.at[z], lines[k - 1])
    for k in (1, 2, 3):
        wires.arrive(37 + k, late_line.at[ahead(4 - k)])
    late_ref[...] = late_line[0] + late_line[1] + late_line[2] + late_line[3]
    wires.drain()


def last(a, b, dq, dk, dv, wa, patches, mask, token, vectors, tail, dx1, sums, masters, firsts, seconds):
    rows, width = a.shape
    lined, lined_m = sums[1:]
    own_rows, w = lined_m.shape[1], wa.shape[2]
    far = [(own_rows, w), lined_m.shape[1:], (lined.shape[0], *lined.shape[2:])]
    late = (3 * (width // PAIR) + 8) // 8 * 8
    big = [dk, dv, wa, a, b, dq, patches, dx1]
    return pl.pallas_call(
        last_kernel,
        out_shape=[
            jax.ShapeDtypeStruct((rows, width), BF),
            jax.ShapeDtypeStruct((16, width), F32),
            jax.ShapeDtypeStruct((late, PAIR), F32),
            *[jax.ShapeDtypeStruct(m.shape, F32) for m in masters[:3]],
        ],
        in_specs=[anywhere()] * 8 + [in_vmem()] * 19,
        out_specs=[in_vmem()] * 6,
        scratch_shapes=[
            *[pltpu.VMEM(v.shape, v.dtype) for v in big],
            pltpu.VMEM((2, 4, 2, 2, own_rows, w), BF),
            pltpu.VMEM((2, 4, 2, own_rows, w), BF),
            pltpu.VMEM((4, own_rows, w), BF),
            pltpu.VMEM((2, 4, own_rows, w), BF),
            pltpu.VMEM((rows, width), F32),
            pltpu.VMEM((rows, width), BF),
            pltpu.VMEM((rows, width), BF),
            *[pltpu.VMEM((3, *f), BF) for f in far],
            pltpu.VMEM((3, 16, width), F32),
            pltpu.VMEM((3, 16, width), F32),
            pltpu.VMEM((4, 16, width), F32),
            pltpu.VMEM((8, late, PAIR), F32),
            pltpu.VMEM((4, late, PAIR), F32),
            pltpu.SemaphoreType.DMA((8,)),
            pltpu.SemaphoreType.DMA((45,)),
            pltpu.SemaphoreType.DMA((45,)),
        ],
        compiler_params=params(collective_id=1, has_side_effects=True),
        name="last",
    )(*big, mask, token, vectors, tail, *sums, *masters, *firsts, *seconds)


def lamb_kernel(*refs):
    masters, firsts, seconds, totals = (refs[4 * n : 4 * n + 4] for n in range(4))
    grad_ref, late_ref, vec_ref, vfirst_ref, vsecond_ref = refs[16:21]
    moments, squares, weights, copies = (refs[21 + 4 * n : 25 + 4 * n] for n in range(4))
    token_ref, bias_ref, vm_ref, vs_ref, vw_ref, norm_ref = refs[37:43]
    deep = vec_ref.shape[1] // PAIR

    def late_row(n):
        return jnp.concatenate([late_ref[n * deep + j : n * deep + j + 1] for j in range(deep)], axis=1)

    norms = jnp.sqrt(late_ref[3 * deep : 3 * deep + 1])
    for n in range(4):
        size, length = norms[:, 2 * n : 2 * n + 1], norms[:, 2 * n + 1 : 2 * n + 2]
        norm_ref[n : n + 1, 0:1] = size
        norm_ref[n : n + 1, 1:2] = length
        step = 0.5 * size / (length + 1e-06)
        for pick in range(3) if n == 0 else (...,):
            weight = masters[n][pick]
            moment, square, update = lamb_parts(weight, firsts[n][pick], seconds[n][pick], totals[n][pick])
            moments[n][pick] = moment
            squares[n][pick] = square
            renewed = weight - step * update
            weights[n][pick] = renewed
            copies[n][pick] = renewed.astype(BF)
    vectors = vec_ref[...]
    grad = jnp.concatenate([late_row(0), late_row(1), grad_ref[2:12]], axis=0)
    moment, square, update = lamb_parts(vectors, vfirst_ref[...], vsecond_ref[...], grad)
    vm_ref[...] = moment
    vs_ref[...] = square
    size = jnp.sqrt(jnp.sum(vectors * vectors, axis=-1, keepdims=True))
    length = jnp.sqrt(jnp.sum(update * update, axis=-1, keepdims=True))
    vw_ref[...] = vectors - 0.5 * size / (length + 1e-06) * update
    token_ref[...] = late_row(2).reshape(token_ref.shape)
    bias_ref[...] = grad_ref[11:12].reshape(bias_ref.shape)


def lamb(masters, firsts, seconds, totals, grad, squares, vectors, vfirst, vsecond):
    full = [jax.ShapeDtypeStruct(m.shape, F32) for m in masters]
    flat = jax.ShapeDtypeStruct((vectors.shape[1],), F32)
    like = jax.ShapeDtypeStruct(vectors.shape, F32)
    return pl.pallas_call(
        lamb_kernel,
        out_shape=[
            *full,
            *full,
            *full,
            *[jax.ShapeDtypeStruct(m.shape, BF) for m in masters],
            flat,
            flat,
            like,
            like,
            like,
            jax.ShapeDtypeStruct((4, 2), F32),
        ],
        in_specs=[in_vmem()] * 21,
        out_specs=[in_vmem()] * 22,
        compiler_params=params(),
        name="lamb",
    )(*masters, *firsts, *seconds, *totals, grad, squares, vectors, vfirst, vsecond)


def lamb_terms(weight, moment, square, gradient):
    moment_new = 0.5 * moment + 0.5 * gradient
    square_new = 0.5 * square + 0.5 * gradient * gradient
    correct = 1.0 - 0.5**STEP
    update = moment_new / correct / (jnp.sqrt(square_new / correct) + 1e-06) + 0.01 * weight
    return (
        moment_new,
        square_new,
        update,
        jnp.stack([jnp.sum(weight * weight), jnp.sum(update * update)]),
    )


def lamb_apply(weight, update, norms):
    renewed = weight - 0.5 * norms[0] / (norms[1] + 1e-06) * update
    return (renewed, renewed.astype(BF))


def per_device(
    patches,
    cube_mask,
    mask_token,
    cotangent,
    vectors,
    vector_first,
    vector_second,
    attend_master,
    attend_first,
    attend_second,
    mixing_master,
    mixing_first,
    mixing_second,
    expand_master,
    expand_first,
    expand_second,
    shrink_master,
    shrink_first,
    shrink_second,
):
    clips, rows, width = patches.shape
    axis = lax.axis_size("dp")
    own_rows = attend_master.shape[0]
    direct = axis == 16 and lax.axis_size("mp") == 2
    dy = cotangent[0]

    def lead(v):
        return v.transpose(1, 0, 2)

    if direct:
        masters = [lead(attend_master), mixing_master, expand_master, shrink_master]
        firsts = [lead(attend_first), mixing_first, expand_first, shrink_first]
        seconds = [lead(attend_second), mixing_second, expand_second, shrink_second]
        *wholes, q, k, v, a1, a1_other, mask = first(masters, patches[0], cube_mask, mask_token, vectors)
        wa = wholes[0].reshape(2, width, -1)
        o, o_low, inv, p, *rest = attend(q, k, v, wholes[1:])
        wm, we = (w.reshape(2, width, -1) for w in rest[:2])
        block_out, dx1, do, gm, tail, *grads = middle(
            patches[0], mask, mask_token, o_low, inv, dy, vectors, wm, we, rest[2], True
        )
        dq, dk, dv, *sums = attend_back(q, k, v, do, o, p, [*grads, gm.reshape(rest[0].shape)])
        patch_grad, early, late, *totals = last(
            a1,
            a1_other,
            dq,
            dk,
            dv,
            wa,
            patches[0],
            mask,
            mask_token,
            vectors,
            tail,
            dx1,
            sums,
            masters,
            firsts,
            seconds,
        )
        totals.append(sums[0])
        done = lamb(masters, firsts, seconds, totals, early, late, vectors, vector_first, vector_second)
        results = []
        for n in range(4):
            group = [done[n], done[4 + n], done[8 + n], done[12 + n]]
            results.extend([lead(g) for g in group] if n == 0 else group)
        return (block_out[None], patch_grad[None], done[16], done[17], *results, *done[18:])
    masters = [attend_master.reshape(own_rows, -1), mixing_master, expand_master, shrink_master]
    firsts = [attend_first.reshape(own_rows, -1), mixing_first, expand_first, shrink_first]
    seconds = [attend_second.reshape(own_rows, -1), mixing_second, expand_second, shrink_second]
    shards = [m.astype(BF) for m in masters]
    mask, token = cube_mask.reshape(rows, 1).astype(F32), mask_token[None]
    swap = [(0, 1), (1, 0)]
    chosen = mask > 0
    x = jnp.where(chosen, token, patches[0].astype(F32))
    centred = x - mean_rows(x)
    scale = lax.rsqrt(mean_rows(centred * centred) + 1e-6)
    wa, wm, we, ws = (
        lax.all_gather(lax.all_gather(s, "dp", axis=0, tiled=True), "mp", axis=0) for s in shards
    )
    a1 = (centred * scale * vectors[0] + vectors[1]).astype(BF)
    a1_other = lax.ppermute(a1, "mp", swap)
    q, k, v = project(a1, a1_other, wa, vectors[2:4])
    o, o_low, inv, p = attend(q, k, v, [])
    block_out, dx1, do, gm, gv, ge, gs = middle(
        patches[0], mask, mask_token, o_low, inv, dy, vectors, wm, we, ws, False
    )
    dq, dk, dv = attend_back(q, k, v, do, o, p, [])
    da1, da1_send, ga, gqv = unproject(a1, a1_other, dq, dk, dv, wa)
    da1 = da1 + lax.ppermute(da1_send, "mp", swap).astype(F32)
    totals = []
    for g in (ga, gm, ge, gs):
        g = lax.psum_scatter(g, "mp", scatter_dimension=0, tiled=True)
        totals.append(lax.psum_scatter(g[0].astype(F32), "dp", scatter_dimension=0, tiled=True))
    xh = centred * scale
    e = da1 * vectors[0]
    dx = dx1 + scale * (e - mean_rows(e) - xh * mean_rows(e * xh))
    patch_grad = jnp.where(chosen, 0.0, dx).astype(BF)
    token_part = jnp.sum(jnp.where(chosen, dx, 0.0), axis=0)
    vector_part = jnp.concatenate(
        [
            jnp.sum(da1 * xh, axis=0)[None],
            jnp.sum(da1, axis=0)[None],
            gqv[0:2],
            gv[0:3],
            gv[4:8],
            gv[3:4],
        ],
        axis=0,
    )
    terms = [lamb_terms(w, m, s, g) for w, m, s, g in zip(masters, firsts, seconds, totals)]
    squares = jnp.stack([t[3] for t in terms])
    vector_total, token_grad, square_total = lax.psum(
        (vector_part, token_part, squares), ("dp", "mp")
    )
    trust_norms = jnp.sqrt(square_total)
    results = []
    for n, (w, t) in enumerate(zip(masters, terms)):
        group = [t[0], t[1], *lamb_apply(w, t[2], trust_norms[n])]
        if n == 0:
            group = [g.reshape(attend_master.shape) for g in group]
        results.extend(group)
    vector_moment = 0.5 * vector_first + 0.5 * vector_total
    vector_square = 0.5 * vector_second + 0.5 * vector_total * vector_total
    correct = 1.0 - 0.5**STEP
    vector_update = (
        vector_moment / correct / (jnp.sqrt(vector_square / correct) + 1e-06) + 0.01 * vectors
    )
    row_weight = jnp.sqrt(jnp.sum(vectors * vectors, axis=-1, keepdims=True))
    row_update = jnp.sqrt(jnp.sum(vector_update * vector_update, axis=-1, keepdims=True))
    vector_weight = vectors - 0.5 * row_weight / (row_update + 1e-06) * vector_update
    return (
        block_out[None],
        patch_grad[None],
        token_grad,
        vector_total[11],
        *results,
        vector_moment,
        vector_square,
        vector_weight,
        trust_norms,
    )


def solution(mesh):
    rows = P("dp", "mp", None)
    flat = P("dp", "mp")
    deep = P("dp", None, "mp")
    copied = P()
    return jax.shard_map(
        per_device,
        mesh=mesh,
        in_specs=(rows, flat, copied, rows, copied, copied, copied, *[deep] * 3, *[flat] * 9),
        out_specs=(rows, rows, copied, copied, *[deep] * 4, *[flat] * 12, *[copied] * 4),
        check_vma=False,
    )
```

```python
import functools

import jax
import jax.numpy as jnp
from jax import lax
from jax.experimental import pallas as pl
from jax.experimental.pallas import tpu as pltpu
from jax.sharding import PartitionSpec as P

HD = 64
PAIR = 2 * HD
STEP = 5
BF = jnp.bfloat16
F32 = jnp.float32
NN = (((1,), (0,)), ((), ()))
NT = (((1,), (1,)), ((), ()))
TN = (((0,), (0,)), ((), ()))
LOG2E = 1.4426950408889634
MESH = pl.DeviceIdType.MESH
VMEM_LIMIT = 60 * 2**20


def dot(a, b, dims=NN):
    return lax.dot_general(a, b, dims, preferred_element_type=F32)


def params(**kw):
    return pltpu.CompilerParams(vmem_limit_bytes=VMEM_LIMIT, **kw)


def anywhere():
    return pl.BlockSpec(memory_space=pl.ANY)


def in_vmem():
    return pl.BlockSpec(memory_space=pltpu.VMEM)


def place():
    dp, x = lax.axis_index("dp"), lax.axis_index("mp")
    return x, dp // 4, lax.rem(dp // 2, 2), lax.rem(dp, 2)


def device(x, z, y, c):
    return ((z * 2 + y) * 2 + c, x)


def neighbours():
    x, z, y, c = place()
    lines = [device(x, lax.rem(z + k, 4), y, c) for k in (1, 2, 3)]
    return lines, device(1 - x, z, y, c), device(x, z, 1 - y, c), device(x, z, y, 1 - c)


def greet():
    lines, over_x, over_y, sibling = neighbours()
    barrier = pltpu.get_barrier_semaphore()
    for other in (*lines, over_x, over_y, sibling):
        pl.semaphore_signal(barrier, inc=1, device_id=other, device_id_type=MESH)
    pl.semaphore_wait(barrier, 6)


class Wires:
    def __init__(self, send_sem, recv_sem):
        self.send_sem, self.recv_sem = send_sem, recv_sem
        self.started = []

    def copy(self, slot, src, dst, other):
        return pltpu.make_async_remote_copy(
            src_ref=src,
            dst_ref=dst,
            send_sem=self.send_sem.at[slot],
            recv_sem=self.recv_sem.at[slot],
            device_id=other,
            device_id_type=MESH,
        )

    def start(self, slot, src, dst, other):
        self.copy(slot, src, dst, other).start()
        self.started.append((slot, src))

    def send(self, slot, whole, part, other):
        self.copy(slot, whole.at[part], whole.at[part], other).start()
        self.started.append((slot, whole, part))

    def arrive(self, slot, dst):
        x, z, y, c = place()
        self.copy(slot, dst, dst, device(x, z, y, 1 - c)).wait_recv()

    def sent(self, slot, src):
        x, z, y, c = place()
        self.copy(slot, src, src, device(x, z, y, 1 - c)).wait_send()

    def drain(self):
        for slot, src, *part in self.started:
            self.sent(slot, src.at[part[0]] if part else src)


ALL = slice(None)


def greet_near():
    _, *near = neighbours()
    barrier = pltpu.get_barrier_semaphore()
    for other in near:
        pl.semaphore_signal(barrier, inc=1, device_id=other, device_id_type=MESH)
    pl.semaphore_wait(barrier, 3)


def first_kernel(*refs):
    masters, (patch_ref, flag_ref, token_ref, vec_ref) = refs[:4], refs[4:8]
    wa_out, wm, we, ws, q_out, k_out, v_out, a1_out, other_out, mask_ref = refs[8:18]
    wa, landing, a1_ref, q_ref, k_ref, v_ref, sa, sm, se, ss, own_sem, put_sem, send_sem, recv_sem = refs[18:]
    x, z, y, c = place()
    lines, over_x, over_y, sibling = neighbours()
    wires = Wires(send_sem, recv_sem)
    rows = a1_ref.shape[0]
    cut = rows // 64 * 16
    halves = (pl.ds(0, cut), pl.ds(cut, rows - cut))
    width = wa.shape[-1] // 3
    for n in range(3):
        sa[:, n * width : (n + 1) * width] = masters[0][n].astype(BF)
    for shard, master in zip((sm, se, ss), masters[1:]):
        shard[...] = master[...].astype(BF)
    puts = []

    def put(src, dst):
        copy = pltpu.make_async_copy(src, dst, put_sem.at[len(puts)])
        copy.start()
        puts.append(copy)

    greet()

    def back(k):
        return lax.rem(z + 4 - k, 4)

    own = [pltpu.make_async_copy(sa, wa.at[x, z, y, c], own_sem.at[0])]
    for n, (shard, whole) in enumerate(((sm, wm), (se, we), (ss, ws))):
        own.append(pltpu.make_async_copy(shard, whole.at[x, z, y, c], own_sem.at[n + 1]))
    for copy in own:
        copy.start()
    for k in (1, 2, 3):
        wires.start(k - 1, sa, wa.at[x, z, y, c], lines[k - 1])
    wires.start(3, sa, wa.at[x, z, y, c], over_x)
    wires.start(7, sa, wa.at[x, z, y, c], over_y)
    others = ((sm, wm), (se, we), (ss, ws))
    for slot, (shard, whole) in zip((30, 34, 38), others):
        wires.start(slot, shard, whole.at[x, z, y, c], over_y)

    flags = jnp.broadcast_to(flag_ref[...].astype(F32), (PAIR, rows))
    mask_ref[...] = flags.T[:, :1]
    tubes = tubes_of(patch_ref, mask_ref, token_ref)
    centred = tubes - mean_rows(tubes)
    scale = lax.rsqrt(mean_rows(centred * centred) + 1e-6)
    a1_ref[...] = (centred * scale * vec_ref[0:1] + vec_ref[1:2]).astype(BF)
    wires.start(19, a1_ref.at[halves[0]], landing.at[halves[0]], over_x)
    put(a1_ref, a1_out)

    for k in (1, 2, 3):
        part = wa.at[x, back(k), y, c]
        wires.arrive(k - 1, part)
        wires.start(3 + k, part, part, over_x)
        wires.start(7 + k, part, part, over_y)
    for copy in own:
        copy.wait()
    line = wa.at[x, ALL, y, c]
    wires.start(15, line, line, sibling)
    wires.start(20, a1_ref.at[halves[1]], landing.at[halves[1]], over_x)
    for n, (shard, whole) in enumerate(others):
        for k in (1, 2, 3):
            wires.start(21 + 3 * n + k - 1, shard, whole.at[x, z, y, c], lines[k - 1])
    for k in range(4):
        part = wa.at[1 - x, back(k), y, c]
        wires.arrive(3 + k, part)
        wires.start(11 + k, part, part, over_y)
    line = wa.at[1 - x, ALL, y, c]
    wires.start(16, line, line, sibling)
    for k in range(4):
        wires.arrive(7 + k, wa.at[x, back(k), 1 - y, c])
    line = wa.at[x, ALL, 1 - y, c]
    wires.start(17, line, line, sibling)

    depth = a1_ref.shape[1]

    def columns(h):
        return pl.ds(pl.multiple_of(h * width, PAIR), width)

    def weight(h, n):
        return wa[h, :, :, :, :, n * width : (n + 1) * width].reshape(depth, width)

    def keys_values(h, source, span):
        k_ref[h, span] = dot(source, weight(h, 1)).astype(BF)
        values = dot(source, weight(h, 2)) + vec_ref[3:4, columns(h)]
        v_ref[h, span] = values.astype(BF)

    def project_own(h):
        queries = dot(a1_ref[...], weight(h, 0)) + vec_ref[2:3, columns(h)]
        q_ref[h] = (queries.astype(BF).astype(F32) * HD**-0.5).astype(BF)
        put(q_ref.at[h], q_out.at[h])
        keys_values(h, a1_ref[...], pl.ds(0, rows))
        for ref, out in ((k_ref, k_out), (v_ref, v_out)):
            put(ref.at[h, pl.ds(0, rows)], out.at[h, pl.ds(0, rows)])

    for slot, j in ((15, y), (17, 1 - y)):
        wires.arrive(slot, wa.at[x, ALL, j, 1 - c])
    project_own(x)

    def pass_on(n):
        whole = others[n][1]
        for k in (1, 2, 3):
            part = whole.at[x, back(k), y, c]
            wires.arrive(21 + 3 * n + k - 1, part)
            wires.start(30 + 4 * n + k, part, part, over_y)

    for k in range(4):
        wires.arrive(11 + k, wa.at[1 - x, back(k), 1 - y, c])
    line = wa.at[1 - x, ALL, 1 - y, c]
    wires.start(18, line, line, sibling)
    pass_on(0)
    for slot, j in ((16, y), (18, 1 - y)):
        wires.arrive(slot, wa.at[1 - x, ALL, j, 1 - c])
    out_copy = pltpu.make_async_copy(wa, wa_out, own_sem.at[0])
    out_copy.start()
    project_own(1 - x)
    pass_on(1)
    for n in range(2):
        wires.arrive(19 + n, landing.at[halves[n]])
        part = landing[halves[n]]
        put(landing.at[halves[n]], other_out.at[halves[n]])
        span = pl.ds(rows + (cut if n else 0), part.shape[0])
        for h in range(2):
            keys_values(h, part, span)
            for ref, out in ((k_ref, k_out), (v_ref, v_out)):
                put(ref.at[h, span], out.at[h, span])
    for n in range(2):
        for k in range(4):
            wires.arrive(30 + 4 * n + k, others[n][1].at[x, back(k), 1 - y, c])
    wires.arrive(38, ws.at[x, z, 1 - y, c])
    for k in (1, 2, 3):
        wires.arrive(27 + k - 1, ws.at[x, back(k), y, c])
    out_copy.wait()
    for copy in puts:
        copy.wait()
    wires.drain()


def first(masters, patches, flags, token, vectors):
    rows, width = patches.shape
    half = width // 2
    own_rows = masters[1].shape[0]
    shards = [(own_rows, 3 * half), *[m.shape for m in masters[1:]]]
    gathered = [(2, 4, 2, 2, *s) for s in shards]
    wholes = [jax.ShapeDtypeStruct(g, BF) for g in gathered]
    keys = jax.ShapeDtypeStruct((2, 2 * rows, half), BF)
    flat = jax.ShapeDtypeStruct((rows, width), BF)
    return pl.pallas_call(
        first_kernel,
        out_shape=[
            *wholes,
            jax.ShapeDtypeStruct((2, rows, half), BF),
            keys,
            keys,
            flat,
            flat,
            jax.ShapeDtypeStruct((rows, 1), F32),
        ],
        in_specs=[in_vmem()] * 8,
        out_specs=[anywhere()] * 9 + [in_vmem()],
        scratch_shapes=[
            pltpu.VMEM(gathered[0], BF),
            pltpu.VMEM((rows, width), BF),
            pltpu.VMEM((rows, width), BF),
            pltpu.VMEM((2, rows, half), BF),
            pltpu.VMEM((2, 2 * rows, half), BF),
            pltpu.VMEM((2, 2 * rows, half), BF),
            *[pltpu.VMEM(s, BF) for s in shards],
            pltpu.SemaphoreType.DMA((4,)),
            pltpu.SemaphoreType.DMA((17,)),
            pltpu.SemaphoreType.DMA((39,)),
            pltpu.SemaphoreType.DMA((39,)),
        ],
        compiler_params=params(collective_id=0, has_side_effects=True),
        name="first",
    )(*masters, patches, flags, token, vectors)


def add_into(dst, other):
    dst[...] = (dst[...].astype(F32) + other[...].astype(F32)).astype(BF)


def project_kernel(mine_ref, other_ref, w_ref, bias_ref, q_ref, k_ref, v_ref):
    rows = mine_ref.shape[0]
    half = w_ref.shape[2] // 3
    for h in range(2):
        cols = slice(h * half, (h + 1) * half)
        queries = dot(mine_ref[...], w_ref[h, :, :half]) + bias_ref[0:1, cols]
        q_ref[h] = (queries.astype(BF).astype(F32) * HD**-0.5).astype(BF)
        for part, ref in ((0, mine_ref), (1, other_ref)):
            span = slice(part * rows, (part + 1) * rows)
            k_ref[h, span] = dot(ref[...], w_ref[h, :, half : 2 * half]).astype(BF)
            v_ref[h, span] = (dot(ref[...], w_ref[h, :, 2 * half :]) + bias_ref[1:2, cols]).astype(BF)


def project(mine, other, weight, bias):
    rows, width = mine.shape
    keys = jax.ShapeDtypeStruct((2, 2 * rows, width // 2), BF)
    return pl.pallas_call(
        project_kernel,
        out_shape=[jax.ShapeDtypeStruct((2, rows, width // 2), BF), keys, keys],
        in_specs=[in_vmem()] * 4,
        out_specs=[in_vmem()] * 3,
        compiler_params=params(),
        name="project",
    )(mine, other, weight, bias)


def half_lanes():
    lane = lax.broadcasted_iota(jnp.int32, (1, PAIR), 1)
    return lane < HD, lane >= HD


def row_blocks(rows):
    cut = (rows // 2 + 15) // 16 * 16
    return ((0, cut), (cut, rows))


def key_parts(keys):
    cut = keys // 2 // 256 * 256
    return ((0, cut), (cut, keys))


def attend_pair(q_ref, k_ref, v_ref, o_ref, low_ref, inv_ref, p_ref):
    sides = half_lanes()
    k, v = k_ref[0], v_ref[0]
    parts = key_parts(k.shape[0])
    for a, b in row_blocks(q_ref.shape[1]):
        q = q_ref[0, a:b]
        outs, invs = [], []
        for h in range(2):
            q_h = jnp.where(sides[h], q, jnp.zeros_like(q))
            v_h = jnp.where(sides[h], v, jnp.ones_like(v))
            scores = [dot(q_h, k[c:d], NT) for c, d in parts]
            tops = [jnp.max(s, axis=-1, keepdims=True) for s in scores]
            top = functools.reduce(jnp.maximum, tops) * LOG2E
            out = None
            for s, (c, d) in zip(scores, parts):
                p = jnp.exp2(s * LOG2E - top).astype(BF)
                p_ref[h, a:b, c:d] = p
                more = dot(p, v_h[c:d])
                out = more if out is None else out + more
            spare = HD if h == 0 else 0
            inv = 1.0 / out[:, spare : spare + 1]
            outs.append(out * inv)
            invs.append(inv)
        o = jnp.where(sides[0], *outs)
        o_ref[0, a:b] = o
        low_ref[0, a:b] = o.astype(BF)
        inv_ref[0, a:b] = jnp.where(sides[0], *invs)


def attend_kernel(*refs):
    outs, (wm, we, ws, send_sem, recv_sem) = refs[6:10], refs[10:]
    i = pl.program_id(0)
    x, z, y, c = place()
    lines, over_x, over_y, sibling = neighbours()
    wires = Wires(send_sem, recv_sem)
    here, side, flank, across = (x, ALL, y, c), (1 - x, ALL, y, c), (x, ALL, 1 - y, c), (1 - x, ALL, 1 - y, c)
    ahead = [lax.rem(z + k, 4) for k in (1, 2, 3)]
    low, high = pl.ds(0, 2), pl.ds(2, 2)
    near_here, far_here = (x, low, y, c), (x, high, y, c)
    near_side, far_side = (1 - x, low, y, c), (1 - x, high, y, c)
    near_across, far_across = (1 - x, low, 1 - y, c), (1 - x, high, 1 - y, c)

    send = wires.send

    @pl.when(i == 0)
    def _():
        greet_near()
        send(0, we, near_here, over_x)
        send(15, we, far_here, over_x)
        for k in (1, 2, 3):
            send(16 + k, ws, (x, ahead[k - 1], y, c), over_y)
        send(2, wm, here, over_x)
        send(3, wm, flank, over_x)
        send(4, wm, here, sibling)
        send(5, wm, flank, sibling)
        send(6, we, here, sibling)
        send(7, we, flank, sibling)
        send(8, ws, here, sibling)

    @pl.when(i == 2)
    def _():
        wires.arrive(0, we.at[near_side])
        send(9, we, near_side, over_y)

    @pl.when(i == 4)
    def _():
        wires.arrive(15, we.at[far_side])
        send(16, we, far_side, over_y)
        send(10, we, side, sibling)
        for k in (1, 2, 3):
            wires.arrive(16 + k, ws.at[x, ahead[k - 1], 1 - y, c])
        send(11, ws, flank, sibling)

    @pl.when(i == 5)
    def _():
        wires.arrive(2, wm.at[side])
        send(12, wm, side, sibling)

    attend_pair(*refs[:3], *outs)

    @pl.when(i == pl.num_programs(0) - 1)
    def _():
        wires.arrive(3, wm.at[across])
        send(13, wm, across, sibling)
        wires.arrive(9, we.at[near_across])
        wires.arrive(16, we.at[far_across])
        send(14, we, across, sibling)
        for slot, whole, (a, b) in (
            (4, wm, (x, y)),
            (5, wm, (x, 1 - y)),
            (6, we, (x, y)),
            (7, we, (x, 1 - y)),
            (8, ws, (x, y)),
            (10, we, (1 - x, y)),
            (11, ws, (x, 1 - y)),
            (12, wm, (1 - x, y)),
            (13, wm, (1 - x, 1 - y)),
            (14, we, (1 - x, 1 - y)),
        ):
            wires.arrive(slot, whole.at[a, ALL, b, 1 - c])
        wires.drain()


def attend(q, k, v, wholes):
    _, rows, half = q.shape
    keys = k.shape[1]
    per = half // PAIR
    of_q = pl.BlockSpec((1, rows, PAIR), lambda i: (i // per, 0, lax.rem(i, per)))
    of_k = pl.BlockSpec((1, keys, PAIR), lambda i: (i // per, 0, lax.rem(i, per)))
    shapes = [
        jax.ShapeDtypeStruct(q.shape, F32),
        jax.ShapeDtypeStruct(q.shape, BF),
        jax.ShapeDtypeStruct(q.shape, F32),
        jax.ShapeDtypeStruct((4 * per, rows, keys), BF),
    ]
    of_p = pl.BlockSpec((2, rows, keys), lambda i: (i, 0, 0))
    common = dict(grid=(2 * per,), name="attend")
    if not wholes:
        return pl.pallas_call(
            attend_pair,
            in_specs=[of_q, of_k, of_k],
            out_specs=[of_q, of_q, of_q, of_p],
            out_shape=shapes,
            compiler_params=params(),
            **common,
        )(q, k, v)
    return pl.pallas_call(
        attend_kernel,
        in_specs=[of_q, of_k, of_k, *[anywhere()] * 3],
        out_specs=[of_q, of_q, of_q, of_p, *[anywhere()] * 3],
        out_shape=[*shapes, *[jax.ShapeDtypeStruct(w.shape, BF) for w in wholes]],
        input_output_aliases={3: 4, 4: 5, 5: 6},
        scratch_shapes=[pltpu.SemaphoreType.DMA((20,)), pltpu.SemaphoreType.DMA((20,))],
        compiler_params=params(collective_id=2, has_side_effects=True),
        **common,
    )(q, k, v, *wholes)


def attend_back_pair(q_ref, k_ref, v_ref, do_ref, o_ref, p_ref, dq_ref, dk_ref, dv_ref):
    sides = half_lanes()
    k, v = k_ref[0], v_ref[0]
    parts = key_parts(k.shape[0])
    grad_k = [[None] * 2 for _ in parts]
    grad_v = [[None] * 2 for _ in parts]

    def plus(total, more):
        return more if total is None else total + more

    for a, b in row_blocks(q_ref.shape[1]):
        q, do = q_ref[0, a:b], do_ref[0, a:b]
        prod = do.astype(F32) * o_ref[0, a:b]
        q_t, do_t = q.T, do.T
        outs = []
        for h in range(2):
            do_h = jnp.where(sides[h], do, jnp.zeros_like(do))
            row_dot = jnp.sum(jnp.where(sides[h], prod, 0.0), axis=-1, keepdims=True)
            out = None
            rows = slice(h * HD, (h + 1) * HD)
            for n, (c, d) in enumerate(parts):
                p = p_ref[h, a:b, c:d]
                grad_p = dot(do_h, v[c:d], NT)
                ds = (p.astype(F32) * (grad_p - row_dot)).astype(BF)
                out = plus(out, dot(ds, k[c:d]))
                grad_k[n][h] = plus(grad_k[n][h], dot(q_t[rows], ds))
                grad_v[n][h] = plus(grad_v[n][h], dot(do_t[rows], p))
            outs.append(out)
        dq_ref[0, a:b] = (jnp.where(sides[0], *outs) * HD**-0.5).astype(BF)
    for n, (c, d) in enumerate(parts):
        dk_ref[0, c:d] = jnp.concatenate(grad_k[n], axis=0).T.astype(BF)
        dv_ref[0, c:d] = jnp.concatenate(grad_v[n], axis=0).T.astype(BF)


def attend_back_kernel(*refs):
    ins, (mine, early_side, early_far, grad_m) = refs[:6], refs[6:10]
    outs, total_s, total_e, total_m = refs[10:13], refs[13], refs[14], refs[15]
    here, away, side_y, side_x, diag = refs[16:21]
    zown, zfar, last_x, last_y, last_d = refs[21:26]
    here_m, sib_m, diag_m, side_m = refs[26:30]
    own_sem, send_sem, recv_sem = refs[30:]
    i = pl.program_id(0)
    x, z, y, c = place()
    lines, over_x, over_y, sibling = neighbours()
    over_xy = device(1 - x, z, 1 - y, c)
    wires = Wires(send_sem, recv_sem)
    width = here.shape[-1]

    def own():
        pairs = (
            (early_far, zfar.at[0]),
            (mine.at[:, :, 0, z], zown),
            (early_side, side_y),
            (mine.at[x, :, 1, :, y], here),
            (mine.at[1 - x, :, 1, :, y], away),
            (grad_m.at[:, :, :, c], here_m),
        )
        return [pltpu.make_async_copy(a, b, own_sem.at[n]) for n, (a, b) in enumerate(pairs)]

    def along_z(h, n, b):
        def sweep(j, _):
            total = zown[n, b, j].astype(F32)
            for k in range(3):
                total = total + zfar[h, b, k, j].astype(F32)
            zown[n, b, j] = total.astype(BF)
            return 0

        lax.fori_loop(0, 2, sweep, 0)

    def spread(b, slot):
        for k in (1, 2, 3):
            wires.arrive(10 + 3 * b + k, zfar.at[1, b, k - 1])
        along_z(1, 1 - x, b)
        wires.start(slot, zown.at[1 - x, b, y], last_x.at[b], over_x)
        wires.start(slot + 1, zown.at[1 - x, b, 1 - y], last_d.at[b], over_xy)

    def to_x(b, slot):
        def sweep(m, _):
            add_into(away.at[b, m], diag.at[b, m])
            return 0

        lax.fori_loop(0, 4, sweep, 0)
        wires.start(slot, away.at[b], side_x.at[b], over_x)

    def far_source(b, k):
        return mine.at[1 - x, b, 0, lax.rem(z + k, 4)]

    expand_diag = [mine.at[1 - x, b, 1, :, 1 - y] for b in range(2)]

    @pl.when(i == 0)
    def _():
        copies = own()
        for copy in copies:
            copy.start()
        barrier = pltpu.get_barrier_semaphore()
        for other in (*lines, over_x, over_y, sibling, over_xy):
            pl.semaphore_signal(barrier, inc=1, device_id=other, device_id_type=MESH)
        pl.semaphore_wait(barrier, 7)
        wires.start(0, grad_m.at[:, :, :, 1 - c], sib_m, sibling)
        wires.start(19, expand_diag[0], diag.at[0], over_y)
        wires.start(1, expand_diag[1], diag.at[1], over_y)
        for b in range(2):
            for k in (1, 2, 3):
                wires.start(10 + 3 * b + k, far_source(b, k), zfar.at[1, b, k - 1], lines[k - 1])

    @pl.when(i == 1)
    def _():
        for copy in own():
            copy.wait()
        for b in range(2):
            along_z(0, x, b)
        wires.arrive(0, sib_m)

        def sweep(m, _):
            part = (m // 8, lax.rem(m // 2, 4), lax.rem(m, 2))
            add_into(here_m.at[part], sib_m.at[part])
            return 0

        lax.fori_loop(0, 16, sweep, 0)
        wires.start(2, here_m.at[1 - x, :, 1 - y], diag_m, over_y)
        wires.start(3, zown.at[x, :, 1 - y], last_y, over_y)
        wires.start(4, here_m.at[x, :, 1 - y], side_m.at[1], over_y)

    @pl.when(i == 2)
    def _():
        wires.arrive(19, diag.at[0])
        to_x(0, 5)

    @pl.when(i == 3)
    def _():
        wires.arrive(1, diag.at[1])
        to_x(1, 9)

    @pl.when(i == 4)
    def _():
        wires.arrive(2, diag_m)

        def sweep(m, _):
            add_into(here_m.at[1 - x, m, y], diag_m.at[m])
            return 0

        lax.fori_loop(0, 4, sweep, 0)
        wires.start(6, here_m.at[1 - x, :, y], side_m.at[0], over_x)
        spread(0, 7)

    @pl.when(i == 5)
    def _():
        spread(1, 17)

    attend_back_pair(*ins, *outs)

    @pl.when(i == pl.num_programs(0) - 1)
    def _():
        wires.arrive(5, side_x.at[0])
        wires.arrive(9, side_x.at[1])

        def sweep(m, _):
            part = (m // 4, lax.rem(m, 4))
            both = side_x[part].astype(F32) + side_y[part].astype(F32)
            total_e[part] = (here[part].astype(F32) + both).astype(BF)
            return 0

        lax.fori_loop(0, 8, sweep, 0)
        wires.arrive(4, side_m.at[1])
        wires.arrive(6, side_m.at[0])
        for n in range(4):
            both = side_m[0, n].astype(F32) + side_m[1, n].astype(F32)
            total_m[n] = (here_m[x, n, y].astype(F32) + both).astype(BF)
        wires.arrive(3, last_y)
        for b, slot in ((0, 7), (1, 17)):
            wires.arrive(slot, last_x.at[b])
            wires.arrive(slot + 1, last_d.at[b])
        for b in range(2):
            one = zown[x, b, y].astype(F32) + last_y[b].astype(F32)
            two = last_x[b].astype(F32) + last_d[b].astype(F32)
            total_s[:, b * width : (b + 1) * width] = one + two
        wires.sent(0, grad_m.at[:, :, :, 1 - c])
        wires.sent(19, expand_diag[0])
        wires.sent(1, expand_diag[1])
        wires.sent(2, here_m.at[1 - x, :, 1 - y])
        wires.sent(3, zown.at[x, :, 1 - y])
        wires.sent(4, here_m.at[x, :, 1 - y])
        wires.sent(5, away.at[0])
        wires.sent(9, away.at[1])
        wires.sent(6, here_m.at[1 - x, :, y])
        for b, slot in ((0, 7), (1, 17)):
            wires.sent(slot, zown.at[1 - x, b, y])
            wires.sent(slot + 1, zown.at[1 - x, b, 1 - y])
        for b in range(2):
            for k in (1, 2, 3):
                wires.sent(10 + 3 * b + k, far_source(b, k))


def attend_back(q, k, v, do, o, p, grads):
    _, rows, half = q.shape
    keys = k.shape[1]
    per = half // PAIR
    of_q = pl.BlockSpec((1, rows, PAIR), lambda i: (i // per, 0, lax.rem(i, per)))
    of_k = pl.BlockSpec((1, keys, PAIR), lambda i: (i // per, 0, lax.rem(i, per)))
    of_p = pl.BlockSpec((2, rows, keys), lambda i: (i, 0, 0))
    shapes = [
        jax.ShapeDtypeStruct(q.shape, BF),
        jax.ShapeDtypeStruct(k.shape, BF),
        jax.ShapeDtypeStruct(k.shape, BF),
    ]
    common = dict(grid=(2 * per,), name="attend_back")
    if not grads:
        return pl.pallas_call(
            attend_back_pair,
            in_specs=[of_q, of_k, of_k, of_q, of_q, of_p],
            out_specs=[of_q, of_k, of_k],
            out_shape=shapes,
            compiler_params=params(),
            **common,
        )(q, k, v, do, o, p)
    mine, grad_m = grads[0], grads[3]
    parts, unit = mine.shape[1], mine.shape[5:]
    lined = (parts, 4, *unit)
    own_rows, w = grad_m.shape[4:]
    lined_m = (4, own_rows, w)
    totals = [
        jax.ShapeDtypeStruct((own_rows, parts * unit[1]), F32),
        jax.ShapeDtypeStruct(lined, BF),
        jax.ShapeDtypeStruct(lined_m, BF),
    ]
    return pl.pallas_call(
        attend_back_kernel,
        in_specs=[of_q, of_k, of_k, of_q, of_q, of_p, *[anywhere()] * 4],
        out_specs=[of_q, of_k, of_k, *[pl.BlockSpec(t.shape, lambda i, t=t: (0,) * t.ndim) for t in totals]],
        out_shape=[*shapes, *totals],
        scratch_shapes=[
            *[pltpu.VMEM(lined, BF)] * 5,
            pltpu.VMEM((2, parts, 2, *unit), BF),
            pltpu.VMEM((2, parts, 3, 2, *unit), BF),
            *[pltpu.VMEM((parts, *unit), BF)] * 3,
            pltpu.VMEM((2, 4, 2, own_rows, w), BF),
            pltpu.VMEM((2, 4, 2, own_rows, w), BF),
            pltpu.VMEM(lined_m, BF),
            pltpu.VMEM((2, *lined_m), BF),
            pltpu.SemaphoreType.DMA((6,)),
            pltpu.SemaphoreType.DMA((20,)),
            pltpu.SemaphoreType.DMA((20,)),
        ],
        compiler_params=params(collective_id=3, has_side_effects=True),
        **common,
    )(q, k, v, do, o, p, *grads)


def normal_parts(h):
    z = jnp.abs(h) * 0.7071067811865476
    t = 1.0 / (1.0 + 0.3275911 * z)
    bell = jnp.exp(-z * z)
    poly = t * (
        0.254829592
        + t * (-0.284496736 + t * (1.421413741 + t * (-1.453152027 + t * 1.061405429)))
    )
    tail = 0.5 * poly * bell
    return jnp.where(h < 0, tail, 1.0 - tail), bell * 0.3989422804014327


def mean_rows(values):
    return jnp.mean(values, axis=-1, keepdims=True)


def tubes_of(patch_ref, mask_ref, token_ref):
    return jnp.where(mask_ref[...] > 0, token_ref[...][None], patch_ref[...].astype(F32))


class Middle:
    def __init__(self, ins, outs, scratch):
        self.patch, self.mask, self.token, self.o, self.inv, self.dy, self.vec, self.wm = ins
        self.out, self.dx1, self.do, self.gm, self.gv = outs
        self.x1, self.a2, self.acc, self.da2 = scratch

    def open(self):
        x1 = tubes_of(self.patch, self.mask, self.token) + self.vec[4:5]
        for h in range(2):
            x1 = x1 + dot(self.o[h], self.wm[h], NT)
        self.x1[...] = x1
        centred = x1 - mean_rows(x1)
        scale = lax.rsqrt(mean_rows(centred * centred) + 1e-6)
        self.a2[...] = (centred * scale * self.vec[5:6] + self.vec[6:7]).astype(BF)
        self.acc[...] = x1 + self.vec[11:12]
        self.da2[...] = jnp.zeros_like(self.da2)

    def block(self, n, we, ws, keep, hook):
        a2, dy = self.a2[...], self.dy[...]
        hidden = dot(a2, we) + self.vec[pl.ds(7 + n, 1)]
        cdf, density = normal_parts(hidden)
        u = (hidden * cdf).astype(BF)
        du = dot(dy, ws)
        dh = (du * (cdf + hidden * density)).astype(BF)
        self.gv[pl.ds(4 + n, 1)] = jnp.sum(dh.astype(F32), axis=0, keepdims=True)
        keep(0, dot(dy, u, TN).astype(BF))
        keep(1, dot(a2, dh, TN).astype(BF))
        hook()
        self.acc[...] += dot(u, ws, NT)
        self.da2[...] += dot(dh, we, NT)

    def close(self):
        self.out[...] = self.acc[...].astype(BF)
        x1, top, da2 = self.x1[...], self.dy[...].astype(F32), self.da2[...]
        centred = x1 - mean_rows(x1)
        scale = lax.rsqrt(mean_rows(centred * centred) + 1e-6)
        xh = centred * scale
        e = da2 * self.vec[5:6]
        dx1 = top + scale * (e - mean_rows(e) - xh * mean_rows(e * xh))
        self.dx1[...] = dx1
        dxb = dx1.astype(BF)
        for h in range(2):
            self.do[h] = (dot(dxb, self.wm[h]) * self.inv[h]).astype(BF)
            self.gm[h] = dot(dxb, self.o[h], TN).astype(BF)
        self.gv[0:1] = jnp.sum(dxb.astype(F32), axis=0, keepdims=True)
        self.gv[1:2] = jnp.sum(da2 * xh, axis=0, keepdims=True)
        self.gv[2:3] = jnp.sum(da2, axis=0, keepdims=True)
        self.gv[3:4] = jnp.sum(top, axis=0, keepdims=True)


def middle_plain_kernel(*refs):
    we_ref, ws_ref = refs[8:10]
    ge_ref, gs_ref = refs[15:17]
    body = Middle(refs[:8], refs[10:15], refs[17:])
    i = pl.program_id(0)
    pl.when(i == 0)(body.open)

    def keep(n, grad):
        (gs_ref, ge_ref)[n][0] = grad

    body.block(i, we_ref[0], ws_ref[0], keep, lambda: None)
    pl.when(i == pl.num_programs(0) - 1)(body.close)


def middle_kernel(*refs):
    we_ref, ws_in = refs[8:10]
    body = Middle(refs[:8], refs[10:15], refs[18:22])
    mine, early_side, early_far = refs[15:18]
    ws, raw, sib, load_sem, put_sem, send_sem, recv_sem = refs[22:]
    i = pl.program_id(0)
    x, z, y, c = place()
    lines, over_x, over_y, sibling = neighbours()
    wires = Wires(send_sem, recv_sem)
    width = raw.shape[-1]
    half = lax.rem(x + i // 2, 2)
    part = lax.rem(i, 2)

    def cols(n):
        return pl.ds(n * width, width)

    def load():
        return pltpu.make_async_copy(ws_in.at[x], ws.at[x], load_sem)

    def put(n):
        h = x if n < 2 else 1 - x
        return pltpu.make_async_copy(raw.at[n % 2, :, :, :, c], mine.at[h, n % 2], put_sem.at[n % 2])

    def to_sibling(n):
        return raw.at[n % 2, :, :, :, 1 - c]

    def offer(n):
        wires.copy(10 + n, to_sibling(n), sib.at[n % 2], sibling).start()

    def finish(n):
        slot = n % 2
        wires.arrive(10 + n, sib.at[slot])
        wires.sent(10 + n, to_sibling(n))

        def sweep(m, _):
            at = (m // 8, lax.rem(m // 2, 4), lax.rem(m, 2))
            add_into(raw.at[slot, at[0], at[1], at[2], c], sib.at[slot, at[0], at[1], at[2]])
            return 0

        lax.fori_loop(0, 16, sweep, 0)
        put(n).start()

    def far_source(n, k):
        return mine.at[x, n, 0, lax.rem(z + k, 4)]

    def send_far(n):
        for k in (1, 2, 3):
            wires.start(14 + 3 * n + k, far_source(n, k), early_far.at[n, k - 1], lines[k - 1])

    def across(n, core):
        return ws.at[1 - x, :, 1 - y, core, :, cols(n)]

    def side(n, core):
        return ws.at[1 - x, :, y, core, :, cols(n)]

    def own_part(n):
        return ws_in.at[x, :, y, c, :, cols(n)]

    @pl.when(i == 0)
    def _():
        load().start()
        greet()
        for n, slot in enumerate((0, 9)):
            wires.start(slot, own_part(n), ws.at[x, :, y, c, :, cols(n)], over_x)
        body.open()
        load().wait()

    @pl.when(i == 2)
    def _():
        wires.arrive(3, side(0, 1 - c))
        wires.arrive(4, across(0, 1 - c))

    @pl.when(i == 3)
    def _():
        wires.arrive(7, side(1, 1 - c))
        wires.arrive(5, across(1, 1 - c))

    def hook():
        @pl.when(i == 0)
        def _():
            wires.arrive(0, side(0, c))
            wires.start(1, side(0, c), side(0, c), over_y)
            wires.start(3, side(0, c), side(0, c), sibling)
            offer(0)

        @pl.when(i == 1)
        def _():
            finish(0)
            offer(1)
            wires.arrive(9, side(1, c))
            wires.start(2, side(1, c), side(1, c), over_y)
            wires.start(7, side(1, c), side(1, c), sibling)
            wires.arrive(1, across(0, c))
            wires.start(4, across(0, c), across(0, c), sibling)
            put(0).wait()
            send_far(0)

        @pl.when(i == 2)
        def _():
            finish(1)
            offer(2)
            wires.arrive(2, across(1, c))
            wires.start(5, across(1, c), across(1, c), sibling)
            put(1).wait()
            send_far(1)
            wires.start(6, mine.at[x, :, 1, :, 1 - y], early_side, over_y)

        @pl.when(i == 3)
        def _():
            finish(2)
            offer(3)

    def keep(n, grad):
        raw[part, n] = grad.reshape(raw.shape[2:])

    weight = ws[half, :, :, :, :, pl.ds(pl.multiple_of(part * width, width), width)].reshape(-1, width)
    body.block(half * 2 + part, we_ref[0], weight, keep, hook)

    @pl.when(i == pl.num_programs(0) - 1)
    def _():
        body.close()
        put(2).wait()
        finish(3)
        wires.arrive(6, early_side)
        for n in range(2):
            for k in (1, 2, 3):
                wires.arrive(14 + 3 * n + k, early_far.at[n, k - 1])
                wires.sent(14 + 3 * n + k, far_source(n, k))
        for n in range(2):
            wires.sent((0, 9)[n], own_part(n))
            wires.sent(1 + n, side(n, c))
            wires.sent((3, 7)[n], side(n, c))
            wires.sent(4 + n, across(n, c))
        wires.sent(6, mine.at[x, :, 1, :, 1 - y])
        put(3).wait()


def middle(patches, mask, token, o, inv, dy, vectors, wm, we, ws, direct):
    rows, width = patches.shape
    hidden = we.shape[2]
    per = hidden // width

    def whole(shape):
        return pl.BlockSpec(shape, lambda i: (0,) * len(shape))

    def of_w(i):
        turn = i // per
        if direct:
            turn = lax.rem(turn + lax.axis_index("mp"), 2)
        return (turn, 0, lax.rem(i, per))

    by_block = pl.BlockSpec((1, width, width), of_w)
    ins = [patches, mask, token, o, inv, dy, vectors, wm, we, ws]
    shapes = [
        jax.ShapeDtypeStruct((rows, width), BF),
        jax.ShapeDtypeStruct((rows, width), F32),
        jax.ShapeDtypeStruct(o.shape, BF),
        jax.ShapeDtypeStruct(wm.shape, BF),
        jax.ShapeDtypeStruct((8, width), F32),
    ]
    in_specs = [pl.BlockSpec(v.shape, lambda i, v=v: (0,) * v.ndim, pipeline_mode=pl.Buffered(1)) for v in ins[:8]]
    out_specs = [whole(v.shape) for v in shapes]
    scratch = [
        pltpu.VMEM((rows, width), F32),
        pltpu.VMEM((rows, width), BF),
        pltpu.VMEM((rows, width), F32),
        pltpu.VMEM((rows, width), F32),
    ]
    common = dict(grid=(2 * per,), name="middle")
    if not direct:
        return pl.pallas_call(
            middle_plain_kernel,
            in_specs=[*in_specs, by_block, by_block],
            out_specs=[*out_specs, by_block, by_block],
            out_shape=[*shapes, *[jax.ShapeDtypeStruct(we.shape, BF)] * 2],
            scratch_shapes=scratch,
            compiler_params=params(),
            **common,
        )(*ins)
    own_rows = ws.shape[4]
    unit = (own_rows, width)
    return pl.pallas_call(
        middle_kernel,
        in_specs=[*in_specs, by_block, anywhere()],
        out_specs=[*out_specs, *[anywhere()] * 3],
        out_shape=[
            *shapes,
            jax.ShapeDtypeStruct((2, per, 2, 4, 2, *unit), BF),
            jax.ShapeDtypeStruct((per, 4, *unit), BF),
            jax.ShapeDtypeStruct((per, 3, 2, *unit), BF),
        ],
        scratch_shapes=[
            *scratch,
            pltpu.VMEM(ws.shape, BF),
            pltpu.VMEM((2, 2, 4, 2, 2, *unit), BF),
            pltpu.VMEM((2, 2, 4, 2, *unit), BF),
            pltpu.SemaphoreType.DMA,
            pltpu.SemaphoreType.DMA((2,)),
            pltpu.SemaphoreType.DMA((21,)),
            pltpu.SemaphoreType.DMA((21,)),
        ],
        compiler_params=params(collective_id=4, has_side_effects=True),
        **common,
    )(*ins)


def unproject_kernel(
    mine_ref, other_ref, dq_ref, dk_ref, dv_ref, w_ref, da_ref, send_ref, gw_ref, gv_ref
):
    rows = mine_ref.shape[0]
    half = w_ref.shape[2] // 3
    da, send = None, None
    gv_ref[...] = jnp.zeros_like(gv_ref)
    for h in range(2):
        cols = slice(h * half, (h + 1) * half)
        dq, dk, dv = dq_ref[h], dk_ref[h], dv_ref[h]
        wq, wk, wv = (w_ref[h, :, n * half : (n + 1) * half] for n in range(3))
        mine = dot(dq, wq, NT) + dot(dk[:rows], wk, NT) + dot(dv[:rows], wv, NT)
        other = dot(dk[rows:], wk, NT) + dot(dv[rows:], wv, NT)
        da = mine if da is None else da + mine
        send = other if send is None else send + other
        a, b = mine_ref[...], other_ref[...]
        gw_ref[h, :, :half] = dot(a, dq, TN).astype(BF)
        gw_ref[h, :, half : 2 * half] = (dot(a, dk[:rows], TN) + dot(b, dk[rows:], TN)).astype(BF)
        gw_ref[h, :, 2 * half :] = (dot(a, dv[:rows], TN) + dot(b, dv[rows:], TN)).astype(BF)
        gv_ref[0:1, cols] = jnp.sum(dq.astype(F32), axis=0, keepdims=True)
        gv_ref[1:2, cols] = jnp.sum(dv.astype(F32), axis=0, keepdims=True)
    da_ref[...] = da
    send_ref[...] = send.astype(BF)


def unproject(mine, other, dq, dk, dv, weight):
    rows, width = mine.shape
    return pl.pallas_call(
        unproject_kernel,
        out_shape=[
            jax.ShapeDtypeStruct((rows, width), F32),
            jax.ShapeDtypeStruct((rows, width), BF),
            jax.ShapeDtypeStruct(weight.shape, BF),
            jax.ShapeDtypeStruct((8, width), F32),
        ],
        in_specs=[in_vmem()] * 6,
        out_specs=[in_vmem()] * 4,
        compiler_params=params(),
        name="unproject",
    )(mine, other, dq, dk, dv, weight)


def lamb_parts(weight, moment, square, grad):
    correct = 1.0 - 0.5**STEP
    moment_new = 0.5 * moment + 0.5 * grad
    square_new = 0.5 * square + 0.5 * grad * grad
    update = moment_new / correct / (jnp.sqrt(square_new / correct) + 1e-06) + 0.01 * weight
    return moment_new, square_new, update


def whole_sum(values):
    return jnp.sum(jnp.sum(values, axis=0, keepdims=True), axis=1, keepdims=True)


def last_kernel(*refs):
    sources, refs = refs[:8], refs[8:]
    (mask_ref, token_ref, vec_ref, tail_ref), refs = refs[:4], refs[4:]
    (total_s, lined, lined_m), refs = refs[:3], refs[3:]
    masters, firsts, seconds, refs = refs[:4], refs[4:8], refs[8:12], refs[12:]
    pg_ref, early_ref, late_ref, *totals = refs[:6]
    totals.append(total_s)
    refs = refs[6:]
    loaded, refs = refs[:8], refs[8:]
    dk_ref, dv_ref, w_ref, a_ref, b_ref, dq_ref, patch_ref, dx1_ref = loaded
    gw, sib, diag, side, da_ref, send_ref, landing = refs[:7]
    far, refs = refs[7:10], refs[10:]
    held, came, final, late, late_line, load_sem, send_sem, recv_sem = refs
    x, z, y, c = place()
    lines, over_x, over_y, sibling = neighbours()
    wires = Wires(send_sem, recv_sem)
    rows, depth = a_ref.shape
    half = w_ref.shape[2] // 3
    cut = rows // 64 * 16
    spans = (pl.ds(0, cut), pl.ds(cut, rows - cut))
    loads = [pltpu.make_async_copy(s, d, load_sem.at[n]) for n, (s, d) in enumerate(zip(sources, loaded))]
    for load in loads:
        load.start()

    def flipped(code):
        def flip(v, bit):
            return 1 - v if bit else v

        return device(flip(x, code // 4), z, flip(y, code // 2 % 2), flip(c, code % 2))

    barrier = pltpu.get_barrier_semaphore()
    for other in (*lines, *[flipped(code) for code in range(1, 8)]):
        pl.semaphore_signal(barrier, inc=1, device_id=other, device_id_type=MESH)
    pl.semaphore_wait(barrier, 10)

    def ahead(k):
        return lax.rem(z + k, 4)

    for k in (1, 2, 3):
        wires.start(3 + k - 1, lined_m.at[ahead(k)], far[1].at[k - 1], lines[k - 1])
        wires.start(6 + k - 1, lined.at[:, ahead(k)], far[2].at[k - 1], lines[k - 1])

    def settle(n, own):
        total = own.astype(F32)
        for k in range(3):
            wires.arrive(3 * n + k, far[n].at[k])
            total = total + far[n][k].astype(F32)
        if n == 0:
            for part in range(3):
                totals[n][part] = total[:, part * half : (part + 1) * half]
        elif n == 1:
            totals[n][...] = total
        else:
            for part in range(total.shape[0]):
                totals[2][:, part * depth : (part + 1) * depth] = total[part]

    lane = lax.broadcasted_iota(jnp.int32, (8, PAIR), 1)
    squares = jnp.zeros((8, PAIR), F32)

    def add_squares(squares, n, pick):
        weight = masters[n][pick]
        update = lamb_parts(weight, firsts[n][pick], seconds[n][pick], totals[n][pick])[2]
        squares = squares + jnp.where(lane == 2 * n, whole_sum(weight * weight), 0.0)
        return squares + jnp.where(lane == 2 * n + 1, whole_sum(update * update), 0.0)

    def columns(n):
        return slice(n * half, (n + 1) * half)

    for n in range(3):
        loads[n].wait()
    for n, (start, size) in enumerate(((rows, cut), (rows + cut, rows - cut))):
        span = pl.ds(start, size)
        send = None
        for h in range(2):
            part = dot(dk_ref[h, span], w_ref[h, :, columns(1)], NT) + dot(dv_ref[h, span], w_ref[h, :, columns(2)], NT)
            send = part if send is None else send + part
        send_ref[spans[n]] = send.astype(BF)
        wires.start(12 + n, send_ref.at[spans[n]], landing.at[spans[n]], over_x)
    for n in range(3, 6):
        loads[n].wait()
    held[0] = jnp.zeros(held.shape[1:], F32)
    for h in range(2):
        held[0, 2:3, columns(h)] = jnp.sum(dq_ref[h].astype(F32), axis=0, keepdims=True)
        held[0, 3:4, columns(h)] = jnp.sum(dv_ref[h].astype(F32), axis=0, keepdims=True)
    held[0, 4:7] = tail_ref[0:3]
    held[0, 7:11] = tail_ref[4:8]
    held[0, 11:12] = tail_ref[3:4]
    wires.start(25, held.at[0], came.at[0], sibling)
    a, b = a_ref[...], b_ref[...]
    own, other = pl.ds(0, rows), pl.ds(rows, rows)

    def weight_grad(h, n):
        if n == 0:
            grad = dot(a, dq_ref[h], TN)
        else:
            ref = dk_ref if n == 1 else dv_ref
            grad = dot(a, ref[h, own], TN) + dot(b, ref[h, other], TN)
        gw[h, :, :, :, :, columns(n)] = grad.astype(BF).reshape(4, 2, 2, -1, half)

    def with_sibling(h, slot):
        wires.arrive(slot, sib.at[h])

        def sweep(m, _):
            add_into(gw.at[h, m // 2, lax.rem(m, 2), c], sib.at[h, m // 2, lax.rem(m, 2)])
            return 0

        lax.fori_loop(0, 8, sweep, 0)

    for n in range(3):
        weight_grad(1 - x, n)
    wires.start(14, gw.at[1 - x, :, :, 1 - c], sib.at[1 - x], sibling)
    wires.arrive(25, came.at[0])
    held[1] = held[0] + came[0]
    wires.start(26, held.at[1], came.at[1], over_y)
    weight_grad(x, 0)
    with_sibling(1 - x, 14)
    order = (1, 2, 3, 0)
    for k in order:
        wires.start(16 + k, gw.at[1 - x, ahead(k), 1 - y, c], diag.at[ahead(k)], over_y)
    weight_grad(x, 1)
    weight_grad(x, 2)
    wires.start(15, gw.at[x, :, :, 1 - c], sib.at[x], sibling)
    da = None
    for h in range(2):
        part = (
            dot(dq_ref[h], w_ref[h, :, columns(0)], NT)
            + dot(dk_ref[h, own], w_ref[h, :, columns(1)], NT)
            + dot(dv_ref[h, own], w_ref[h, :, columns(2)], NT)
        )
        da = part if da is None else da + part
    da_ref[...] = da
    wires.arrive(26, came.at[1])
    held[2] = held[1] + came[1]
    wires.start(27, held.at[2], came.at[2], over_x)
    with_sibling(x, 15)
    for k in order:
        wires.start(41 + k, gw.at[x, ahead(k), 1 - y, c], side.at[1, ahead(k)], over_y)
    for k in order:
        wires.arrive(16 + k, diag.at[ahead(k)])
        part = gw.at[1 - x, ahead(k), y, c]
        add_into(part, diag.at[ahead(k)])
        wires.start(20 + k, part, side.at[0, ahead(k)], over_x)
    settle(1, lined_m[z])
    settle(2, lined[:, z])
    for n in (1, 2, 3):
        squares = add_squares(squares, n, ...)
    for n in range(6, 8):
        loads[n].wait()
    tubes = tubes_of(patch_ref, mask_ref, token_ref)
    centred = tubes - mean_rows(tubes)
    scale = lax.rsqrt(mean_rows(centred * centred) + 1e-6)
    xh = centred * scale
    for n in range(2):
        wires.arrive(12 + n, landing.at[spans[n]])
    da = da_ref[...] + landing[...].astype(F32)
    me = x * 4 + y * 2 + c
    deep = depth // PAIR

    def late_row(n, values):
        for j in range(deep):
            late[me, n * deep + j : n * deep + j + 1] = values[:, j * PAIR : (j + 1) * PAIR]

    late_row(0, jnp.sum(da * xh, axis=0, keepdims=True))
    late_row(1, jnp.sum(da, axis=0, keepdims=True))
    e = da * vec_ref[0:1]
    dx = dx1_ref[...] + scale * (e - mean_rows(e) - xh * mean_rows(e * xh))
    masked = mask_ref[...] > 0
    pg_ref[...] = jnp.where(masked, 0.0, dx).astype(BF)
    late_row(2, jnp.sum(jnp.where(masked, dx, 0.0), axis=0, keepdims=True))
    wires.arrive(27, came.at[2])
    final[z] = held[2] + came[2]
    for k in (1, 2, 3):
        wires.start(27 + k, final.at[z], final.at[z], lines[k - 1])

    def with_sides(k):
        wires.arrive(41 + k, side.at[1, ahead(k)])
        wires.arrive(20 + k, side.at[0, ahead(k)])
        both = side[0, ahead(k)].astype(F32) + side[1, ahead(k)].astype(F32)
        part = gw.at[x, ahead(k), y, c]
        part[...] = (part[...].astype(F32) + both).astype(BF)
        if k:
            wires.start(k - 1, part, far[0].at[k - 1], lines[k - 1])

    for k in order:
        with_sides(k)
    for k in (1, 2, 3):
        wires.arrive(27 + k, final.at[ahead(4 - k)])
    early_ref[...] = final[0] + final[1] + final[2] + final[3]
    settle(0, gw[x, z, y, c])
    for part in range(3):
        squares = add_squares(squares, 0, part)
    late[me, 3 * deep : 3 * deep + 1] = squares[0:1]
    late[me, 3 * deep + 1 :] = jnp.zeros((late.shape[1] - 3 * deep - 1, PAIR), F32)
    for code in range(1, 8):
        wires.start(30 + code, late.at[me], late.at[me], flipped(code))

    def flip_index(code):
        return sum((1 - v if bit else v) * w for v, bit, w in ((x, code // 4, 4), (y, code // 2 % 2, 2), (c, code % 2, 1)))

    for code in range(1, 8):
        wires.arrive(30 + code, late.at[flip_index(code)])
    total = late[0]
    for n in range(1, 8):
        total = total + late[n]
    late_line[z] = total
    for k in (1, 2, 3):
        wires.start(37 + k, late_line.at[z], late_line.at[z], lines[k - 1])
    for k in (1, 2, 3):
        wires.arrive(37 + k, late_line.at[ahead(4 - k)])
    late_ref[...] = late_line[0] + late_line[1] + late_line[2] + late_line[3]
    wires.drain()


def last(a, b, dq, dk, dv, wa, patches, mask, token, vectors, tail, dx1, sums, masters, firsts, seconds):
    rows, width = a.shape
    lined, lined_m = sums[1:]
    own_rows, w = lined_m.shape[1], wa.shape[2]
    far = [(own_rows, w), lined_m.shape[1:], (lined.shape[0], *lined.shape[2:])]
    late = (3 * (width // PAIR) + 8) // 8 * 8
    big = [dk, dv, wa, a, b, dq, patches, dx1]
    return pl.pallas_call(
        last_kernel,
        out_shape=[
            jax.ShapeDtypeStruct((rows, width), BF),
            jax.ShapeDtypeStruct((16, width), F32),
            jax.ShapeDtypeStruct((late, PAIR), F32),
            *[jax.ShapeDtypeStruct(m.shape, F32) for m in masters[:3]],
        ],
        in_specs=[anywhere()] * 8 + [in_vmem()] * 19,
        out_specs=[in_vmem()] * 6,
        scratch_shapes=[
            *[pltpu.VMEM(v.shape, v.dtype) for v in big],
            pltpu.VMEM((2, 4, 2, 2, own_rows, w), BF),
            pltpu.VMEM((2, 4, 2, own_rows, w), BF),
            pltpu.VMEM((4, own_rows, w), BF),
            pltpu.VMEM((2, 4, own_rows, w), BF),
            pltpu.VMEM((rows, width), F32),
            pltpu.VMEM((rows, width), BF),
            pltpu.VMEM((rows, width), BF),
            *[pltpu.VMEM((3, *f), BF) for f in far],
            pltpu.VMEM((3, 16, width), F32),
            pltpu.VMEM((3, 16, width), F32),
            pltpu.VMEM((4, 16, width), F32),
            pltpu.VMEM((8, late, PAIR), F32),
            pltpu.VMEM((4, late, PAIR), F32),
            pltpu.SemaphoreType.DMA((8,)),
            pltpu.SemaphoreType.DMA((45,)),
            pltpu.SemaphoreType.DMA((45,)),
        ],
        compiler_params=params(collective_id=1, has_side_effects=True),
        name="last",
    )(*big, mask, token, vectors, tail, *sums, *masters, *firsts, *seconds)


def lamb_kernel(*refs):
    masters, firsts, seconds, totals = (refs[4 * n : 4 * n + 4] for n in range(4))
    grad_ref, late_ref, vec_ref, vfirst_ref, vsecond_ref = refs[16:21]
    moments, squares, weights, copies = (refs[23 + 4 * n : 27 + 4 * n] for n in range(4))
    token_ref, bias_ref, vm_ref, vs_ref, vw_ref, norm_ref = refs[39:45]
    for n in range(2):
        refs[45 + n][...] = refs[21 + n][...]
    deep = vec_ref.shape[1] // PAIR

    def late_row(n):
        return jnp.concatenate([late_ref[n * deep + j : n * deep + j + 1] for j in range(deep)], axis=1)

    norms = jnp.sqrt(late_ref[3 * deep : 3 * deep + 1])
    for n in range(4):
        size, length = norms[:, 2 * n : 2 * n + 1], norms[:, 2 * n + 1 : 2 * n + 2]
        norm_ref[0:1, n : n + 1] = size
        norm_ref[1:2, n : n + 1] = length
        step = 0.5 * size / (length + 1e-06)
        for pick in range(3) if n == 0 else (...,):
            weight = masters[n][pick]
            moment, square, update = lamb_parts(weight, firsts[n][pick], seconds[n][pick], totals[n][pick])
            moments[n][pick] = moment
            squares[n][pick] = square
            renewed = weight - step * update
            weights[n][pick] = renewed
            copies[n][pick] = renewed.astype(BF)
    vectors = vec_ref[...]
    grad = jnp.concatenate([late_row(0), late_row(1), grad_ref[2:12]], axis=0)
    moment, square, update = lamb_parts(vectors, vfirst_ref[...], vsecond_ref[...], grad)
    vm_ref[...] = moment
    vs_ref[...] = square
    size = jnp.sqrt(jnp.sum(vectors * vectors, axis=-1, keepdims=True))
    length = jnp.sqrt(jnp.sum(update * update, axis=-1, keepdims=True))
    vw_ref[...] = vectors - 0.5 * size / (length + 1e-06) * update
    token_ref[...] = late_row(2).reshape(token_ref.shape)
    bias_ref[...] = grad_ref[11:12].reshape(bias_ref.shape)


def lamb(masters, firsts, seconds, totals, grad, squares, vectors, vfirst, vsecond, finished):
    full = [jax.ShapeDtypeStruct(m.shape, F32) for m in masters]
    flat = jax.ShapeDtypeStruct((vectors.shape[1],), F32)
    like = jax.ShapeDtypeStruct(vectors.shape, F32)
    return pl.pallas_call(
        lamb_kernel,
        out_shape=[
            *full,
            *full,
            *full,
            *[jax.ShapeDtypeStruct(m.shape, BF) for m in masters],
            flat,
            flat,
            like,
            like,
            like,
            jax.ShapeDtypeStruct((2, 4), F32),
            *[jax.ShapeDtypeStruct(v.shape, v.dtype) for v in finished],
        ],
        in_specs=[in_vmem()] * 23,
        out_specs=[in_vmem()] * 24,
        compiler_params=params(),
        name="lamb",
    )(*masters, *firsts, *seconds, *totals, grad, squares, vectors, vfirst, vsecond, *finished)


def lamb_terms(weight, moment, square, gradient):
    moment_new = 0.5 * moment + 0.5 * gradient
    square_new = 0.5 * square + 0.5 * gradient * gradient
    correct = 1.0 - 0.5**STEP
    update = moment_new / correct / (jnp.sqrt(square_new / correct) + 1e-06) + 0.01 * weight
    return (
        moment_new,
        square_new,
        update,
        jnp.stack([jnp.sum(weight * weight), jnp.sum(update * update)]),
    )


def lamb_apply(weight, update, norms):
    renewed = weight - 0.5 * norms[0] / (norms[1] + 1e-06) * update
    return (renewed, renewed.astype(BF))


def per_device(
    patches,
    cube_mask,
    mask_token,
    cotangent,
    vectors,
    vector_first,
    vector_second,
    attend_master,
    attend_first,
    attend_second,
    mixing_master,
    mixing_first,
    mixing_second,
    expand_master,
    expand_first,
    expand_second,
    shrink_master,
    shrink_first,
    shrink_second,
):
    clips, rows, width = patches.shape
    axis = lax.axis_size("dp")
    own_rows = attend_master.shape[0]
    direct = axis == 16 and lax.axis_size("mp") == 2
    dy = cotangent[0]

    def lead(v):
        return v.transpose(1, 0, 2)

    if direct:
        masters = [lead(attend_master), mixing_master, expand_master, shrink_master]
        firsts = [lead(attend_first), mixing_first, expand_first, shrink_first]
        seconds = [lead(attend_second), mixing_second, expand_second, shrink_second]
        *wholes, q, k, v, a1, a1_other, mask = first(masters, patches[0], cube_mask, mask_token, vectors)
        wa = wholes[0].reshape(2, width, -1)
        o, o_low, inv, p, *rest = attend(q, k, v, wholes[1:])
        wm, we = (w.reshape(2, width, -1) for w in rest[:2])
        block_out, dx1, do, gm, tail, *grads = middle(
            patches[0], mask, mask_token, o_low, inv, dy, vectors, wm, we, rest[2], True
        )
        dq, dk, dv, *sums = attend_back(q, k, v, do, o, p, [*grads, gm.reshape(rest[0].shape)])
        patch_grad, early, late, *totals = last(
            a1,
            a1_other,
            dq,
            dk,
            dv,
            wa,
            patches[0],
            mask,
            mask_token,
            vectors,
            tail,
            dx1,
            sums,
            masters,
            firsts,
            seconds,
        )
        totals.append(sums[0])
        done = lamb(
            masters,
            firsts,
            seconds,
            totals,
            early,
            late,
            vectors,
            vector_first,
            vector_second,
            [block_out, patch_grad],
        )
        block_out, patch_grad = done[22:]
        results = []
        for n in range(4):
            group = [done[n], done[4 + n], done[8 + n], done[12 + n]]
            results.extend([lead(g) for g in group] if n == 0 else group)
        return (block_out[None], patch_grad[None], done[16], done[17], *results, *done[18:21], done[21].T)
    masters = [attend_master.reshape(own_rows, -1), mixing_master, expand_master, shrink_master]
    firsts = [attend_first.reshape(own_rows, -1), mixing_first, expand_first, shrink_first]
    seconds = [attend_second.reshape(own_rows, -1), mixing_second, expand_second, shrink_second]
    shards = [m.astype(BF) for m in masters]
    mask, token = cube_mask.reshape(rows, 1).astype(F32), mask_token[None]
    swap = [(0, 1), (1, 0)]
    chosen = mask > 0
    x = jnp.where(chosen, token, patches[0].astype(F32))
    centred = x - mean_rows(x)
    scale = lax.rsqrt(mean_rows(centred * centred) + 1e-6)
    wa, wm, we, ws = (
        lax.all_gather(lax.all_gather(s, "dp", axis=0, tiled=True), "mp", axis=0) for s in shards
    )
    a1 = (centred * scale * vectors[0] + vectors[1]).astype(BF)
    a1_other = lax.ppermute(a1, "mp", swap)
    q, k, v = project(a1, a1_other, wa, vectors[2:4])
    o, o_low, inv, p = attend(q, k, v, [])
    block_out, dx1, do, gm, gv, ge, gs = middle(
        patches[0], mask, mask_token, o_low, inv, dy, vectors, wm, we, ws, False
    )
    dq, dk, dv = attend_back(q, k, v, do, o, p, [])
    da1, da1_send, ga, gqv = unproject(a1, a1_other, dq, dk, dv, wa)
    da1 = da1 + lax.ppermute(da1_send, "mp", swap).astype(F32)
    totals = []
    for g in (ga, gm, ge, gs):
        g = lax.psum_scatter(g, "mp", scatter_dimension=0, tiled=True)
        totals.append(lax.psum_scatter(g[0].astype(F32), "dp", scatter_dimension=0, tiled=True))
    xh = centred * scale
    e = da1 * vectors[0]
    dx = dx1 + scale * (e - mean_rows(e) - xh * mean_rows(e * xh))
    patch_grad = jnp.where(chosen, 0.0, dx).astype(BF)
    token_part = jnp.sum(jnp.where(chosen, dx, 0.0), axis=0)
    vector_part = jnp.concatenate(
        [
            jnp.sum(da1 * xh, axis=0)[None],
            jnp.sum(da1, axis=0)[None],
            gqv[0:2],
            gv[0:3],
            gv[4:8],
            gv[3:4],
        ],
        axis=0,
    )
    terms = [lamb_terms(w, m, s, g) for w, m, s, g in zip(masters, firsts, seconds, totals)]
    squares = jnp.stack([t[3] for t in terms])
    vector_total, token_grad, square_total = lax.psum(
        (vector_part, token_part, squares), ("dp", "mp")
    )
    trust_norms = jnp.sqrt(square_total)
    results = []
    for n, (w, t) in enumerate(zip(masters, terms)):
        group = [t[0], t[1], *lamb_apply(w, t[2], trust_norms[n])]
        if n == 0:
            group = [g.reshape(attend_master.shape) for g in group]
        results.extend(group)
    vector_moment = 0.5 * vector_first + 0.5 * vector_total
    vector_square = 0.5 * vector_second + 0.5 * vector_total * vector_total
    correct = 1.0 - 0.5**STEP
    vector_update = (
        vector_moment / correct / (jnp.sqrt(vector_square / correct) + 1e-06) + 0.01 * vectors
    )
    row_weight = jnp.sqrt(jnp.sum(vectors * vectors, axis=-1, keepdims=True))
    row_update = jnp.sqrt(jnp.sum(vector_update * vector_update, axis=-1, keepdims=True))
    vector_weight = vectors - 0.5 * row_weight / (row_update + 1e-06) * vector_update
    return (
        block_out[None],
        patch_grad[None],
        token_grad,
        vector_total[11],
        *results,
        vector_moment,
        vector_square,
        vector_weight,
        trust_norms,
    )


def solution(mesh):
    rows = P("dp", "mp", None)
    flat = P("dp", "mp")
    deep = P("dp", None, "mp")
    copied = P()
    return jax.shard_map(
        per_device,
        mesh=mesh,
        in_specs=(rows, flat, copied, rows, copied, copied, copied, *[deep] * 3, *[flat] * 9),
        out_specs=(rows, rows, copied, copied, *[deep] * 4, *[flat] * 12, *[copied] * 4),
        check_vma=False,
    )
```
